128 devices in a mesh: rows: 32 (over z, y, core), mem: 4 (over x).
Axes of the slice: x: 4, y: 4, z: 4, core: 2. Of those that a mesh axis runs over, the one named last changes fastest.
Arguments:
- fine_members: float32 [16, 8, 512, 512], P('mem', None, 'rows'), may hold values from -6 to 6
- coarse_members: float32 [32, 8, 256, 256], P('mem', None, 'rows'), may hold values from -6 to 6
- diffusion: float32 [8], replicated, may hold values from 0.02 to 0.08
- hyper: float32 [8], replicated, may hold values from 0.002 to 0.008
- drift: float32 [8], replicated, may hold values from -0.2 to 0.2
- obs_value: float32 [32768], P('rows'), may hold values from -6 to 6
- obs_var: float32 [32768], P('rows'), may hold values from 0.5 to 5
- obs_row: int32 [32768], P('rows'), may hold values from 0 to 511, as said below
- obs_col: int32 [32768], P('rows'), may hold values from 0 to 511
- obs_layer: int32 [32768], P('rows'), may hold values from 0 to 7
- obs_count: int32 [32], P('rows'), may hold values from 256 to 1024, as said below
Outputs:
- analysis_mean: float32 [8, 512, 512], P(None, 'rows')
- pair_update: float32 [16, 8, 512, 512], P('mem', None, 'rows')
The draws below stay inside these ranges and needn't reach their ends.
Inputs may be any that keep to these rules, and one draw needn't show every extreme that they name: `obs_row`: observation slot s belongs to row tile t = s // 1024, and its row lies in that tile: from t * 16 to t * 16 + 15. `obs_count`: some tile has all 1024 slots live in every draw.
All inputs are finite; a program needn't handle non-finite values.
Results may differ from the reference program's by a relative error of at most 0.00016.
Values sent between devices are 32-bit elements; how exact they have to be, the bound alone decides.
A program may use at most 128 MiB of HBM per device.

```python
import math
import jax
import jax.numpy as jnp
from jax import lax

K = 8
NC = 512
RF = 16
OBS_CAP = 1024
STEPS = 3
NCC = 256
TILES = 32
NRF = 512
NRC = 256
M0 = 32
M1 = 16
E = 48
OBS = 32768


def draw_obs_row(key, part):
    key = jax.random.fold_in(key, 11)
    owner = jnp.arange(OBS, dtype=jnp.int32) // OBS_CAP
    return owner * RF + jax.random.randint(key, (OBS,), 0, RF, dtype=jnp.int32)


def draw_obs_count(key, part):
    key = jax.random.fold_in(key, 23)
    first, second = jax.random.split(key)
    counts = jax.random.randint(first, (TILES,), OBS_CAP // 4, OBS_CAP + 1, dtype=jnp.int32)
    full = jax.random.randint(second, (), 0, TILES, dtype=jnp.int32)
    return jnp.where(jnp.arange(TILES, dtype=jnp.int32) == full, OBS_CAP, counts).astype(jnp.int32)


def with_ends(array, rng, low, high):
    longest = array.shape.index(max(array.shape))
    spots = []
    for shift in (0, 1):
        where = [jax.random.randint(jax.random.fold_in(rng, axis), (), 0, length) for axis, length in enumerate(array.shape)]
        where[longest] = (where[longest] + shift) % array.shape[longest]
        spots.append(tuple(where))
    return array.at[spots[0]].set(low).at[spots[1]].set(high)


def block_levels(own_key, shape, cuts, least, largest):
    level, own = 1.0, jax.random.fold_in(own_key, 6)
    for axis_at, parts in cuts:
        steps = jnp.exp(jax.random.uniform(jax.random.fold_in(own, axis_at), (parts,), jnp.float32, least / len(cuts), largest / len(cuts)))
        level = level * jnp.repeat(steps, shape[axis_at] // parts).reshape([-1 if axis == axis_at else 1 for axis in range(len(shape))])
    return level


def noise(rng, shape, deviation, bound, cuts=(), kind=jnp.bfloat16):
    drawn = jax.random.normal(rng, shape, jnp.float32) * deviation
    if len(cuts) > 0:
        drawn = block_levels(rng, shape, cuts, -0.22, 0.18) * drawn
    return jnp.clip(drawn, min=-bound, max=bound).astype(kind)


def setup_inputs(seed: int = 0) -> dict:
    splits = jax.random.split(jax.random.key(seed), 12)
    return {
        "fine_members": noise(splits[0], (M1, K, NRF, NC), 1.0, 6.0, ((0, 4), (2, 32)), jnp.float32),
        "coarse_members": noise(splits[1], (M0, K, NRC, NCC), 1.0, 6.0, ((0, 4), (2, 32)), jnp.float32),
        "diffusion": jnp.clip(jax.random.uniform(splits[2], (K,), jnp.float32, 0.02, 0.08), 0.02, 0.08),
        "hyper": jnp.clip(jax.random.uniform(splits[3], (K,), jnp.float32, 0.002, 0.008), 0.002, 0.008),
        "drift": jnp.clip(jax.random.uniform(splits[4], (K,), jnp.float32, -0.2, 0.2), -0.2, 0.2),
        "obs_value": noise(splits[5], (OBS,), 1.0, 6.0, ((0, 32),), jnp.float32),
        "obs_var": jnp.clip(jnp.exp(math.log(5.0) - 2.3025851 * jax.random.uniform(splits[6], (OBS,), jnp.float32) ** block_levels(splits[6], (OBS,), ((0, 32),), -0.2, 0.2)), 0.5, 5.0),
        "obs_row": draw_obs_row(jax.random.fold_in(splits[11], 71), 0),
        "obs_col": with_ends(jax.random.randint(splits[8], (OBS,), 0, NC), jax.random.fold_in(splits[8], 1), 0, NC - 1).astype(jnp.int32),
        "obs_layer": with_ends(jax.random.randint(splits[9], (OBS,), 0, K), jax.random.fold_in(splits[9], 1), 0, K - 1).astype(jnp.int32),
        "obs_count": draw_obs_count(jax.random.fold_in(splits[11], 71), 0),
    }


def restrict(fine):
    shape = fine.shape
    blocks = fine.reshape(shape[:-2] + (shape[-2] // 2, 2, shape[-1] // 2, 2))
    return blocks.mean(axis=(-3, -1))

def prolong(coarse):
    return jnp.repeat(jnp.repeat(coarse, 2, axis=-2), 2, axis=-1)

def advance(padded, first_row, grid_rows, diffusion, hyper, drift):
    count = padded.shape[2]
    rows_at = first_row + jnp.arange(count, dtype=jnp.int32)
    inside = ((rows_at >= 0) & (rows_at < grid_rows)).astype(padded.dtype)[:, None]

    def plane(field):
        core = field[:, :, 1:-1]
        return field[:, :, 2:] + field[:, :, :-2] + jnp.roll(core, 1, axis=3) + jnp.roll(core, -1, axis=3) - 4.0 * core
    first = plane(padded) * inside[1:-1]
    second = plane(first)
    centre = padded[:, :, 2:-2]
    side = jnp.roll(centre, -1, axis=3) - jnp.roll(centre, 1, axis=3)
    upper = jnp.pad(centre[:, 1:], ((0, 0), (0, 1), (0, 0), (0, 0)))
    lower = jnp.pad(centre[:, :-1], ((0, 0), (1, 0), (0, 0), (0, 0)))
    out = centre + diffusion[None, :, None, None] * first[:, :, 1:-1] - hyper[None, :, None, None] * second - 0.5 * drift[None, :, None, None] * side + 0.1 * (upper - 2.0 * centre + lower)
    return out * inside[2:-2]

def pad_rows(field, width):
    return jnp.pad(field, ((0, 0), (0, 0), (width, width), (0, 0)))

def reference(fine_members, coarse_members, diffusion, hyper, drift, obs_value, obs_var, obs_row, obs_col, obs_layer, obs_count):
    members_c = jnp.concatenate([coarse_members, restrict(fine_members)], 0)
    fine = fine_members
    for step in range(STEPS):
        fine = advance(pad_rows(fine, 2), -2, NRF, diffusion, hyper, drift)
        members_c = advance(pad_rows(members_c, 2), -2, NRC, diffusion * 0.25, hyper * 0.0625, drift * 0.5)
    level_c = members_c[:M0]
    pair_c = members_c[M0:]
    mean_f = lax.optimization_barrier(jnp.mean(fine, 0))
    mean_p = lax.optimization_barrier(jnp.mean(pair_c, 0))
    mean_l = lax.optimization_barrier(jnp.mean(level_c, 0))
    level_anom = (level_c - mean_l) / math.sqrt(M0 - 1)
    fine_anom = fine - mean_f
    pair_anom = pair_c - mean_p
    fine_index = (obs_layer * NRF + obs_row) * NC + obs_col
    coarse_index = (obs_layer * NRC + obs_row // 2) * NCC + obs_col // 2
    level_obs = jnp.take(level_anom.reshape(M0, -1), coarse_index, axis=1)
    pair_obs = (jnp.take(fine_anom.reshape(M1, -1), fine_index, axis=1) - jnp.take(pair_anom.reshape(M1, -1), coarse_index, axis=1)) / math.sqrt(M1 - 1)
    columns = jnp.concatenate([level_obs, pair_obs], 0)
    mean_obs = jnp.take(mean_l.reshape(-1), coarse_index) + jnp.take(mean_f.reshape(-1), fine_index) - jnp.take(mean_p.reshape(-1), coarse_index)
    innov = obs_value - mean_obs
    live = (jnp.arange(OBS_CAP, dtype=jnp.int32)[None, :] < obs_count[:, None]).reshape(-1)
    weight = jnp.where(live, 1.0 / obs_var, 0.0)
    gram = jnp.dot(columns * weight[None, :], columns.T, precision=lax.Precision.HIGHEST)
    rhs = jnp.dot(columns, weight * innov, precision=lax.Precision.HIGHEST)
    system = jnp.eye(E, dtype=jnp.float32) + gram
    factor = jnp.linalg.cholesky(system)
    solved = jax.scipy.linalg.cho_solve((factor, True), jnp.concatenate([rhs[:, None], gram], 1))
    coef = jnp.concatenate([solved[:, :1], -0.5 * solved[:, 1 + M0:]], 1)
    pair_cols = (fine_anom - prolong(pair_anom)) / math.sqrt(M1 - 1)
    coarse_part = jnp.einsum('em,ekrc->mkrc', coef[:M0], level_anom, precision=lax.Precision.HIGHEST)
    fine_part = jnp.einsum('em,ekrc->mkrc', coef[M0:], pair_cols, precision=lax.Precision.HIGHEST)
    incr = prolong(coarse_part) + fine_part
    mu = prolong(mean_l) + mean_f - prolong(mean_p)
    analysis_mean = mu + incr[0]
    pair_update = math.sqrt(M1 - 1) * (pair_cols + incr[1:])
    return (analysis_mean, pair_update)
```

```python
import functools
import math

import jax
import jax.numpy as jnp
from jax import lax
from jax.experimental import pallas as pl
from jax.experimental.pallas import tpu as pltpu
from jax.sharding import PartitionSpec as P

STEPS = 3
HALO = 2 * STEPS
LANES = 128
MESH = pl.DeviceIdType.MESH
HIGHEST = lax.Precision.HIGHEST
F32 = jnp.float32
BF16 = jnp.bfloat16


def iota(shape, axis):
    return lax.broadcasted_iota(jnp.int32, shape, axis)


def halves(value):
    high = value.astype(BF16)
    return high, (value - high.astype(F32)).astype(BF16)


def dot(left, right):
    return jnp.dot(left, right, preferred_element_type=F32)


def exact_dot(left, right):
    return jnp.dot(left, right, precision=HIGHEST, preferred_element_type=F32)


def shifted(row):
    width = row.shape[-1]
    return pltpu.roll(row, 1, axis=1), pltpu.roll(row, width - 1, axis=1)


def layer_vector(ref, scale, layers, width):
    at = iota((layers, width), 0)
    out = jnp.zeros((layers, width), F32)
    for k in range(layers):
        out = jnp.where(at == k, ref[k] * scale, out)
    return out


def advance(reads, writes, count, first_row, grid_rows, coef):
    lap_c, hyp_c, drift_c, up_c, low_c = coef
    layers = up_c.shape[0]

    def inside(j):
        at = first_row + j
        return jnp.where((at >= 0) & (at < grid_rows), 1.0, 0.0).astype(F32)

    def start(read):
        q0, q1, q2, q3 = read(0), read(1), read(2), read(3)
        left, right = shifted(q1)
        f1 = (q2 + q0 + left + right - 4.0 * q1) * inside(1)
        left, right = shifted(q2)
        f2 = (q3 + q1 + left + right - 4.0 * q2) * inside(2)
        return f1, f2, right - left

    def one(i, carry, read, write):
        f1, f2, side = carry
        q2, q3, q4 = read(i + 2), read(i + 3), read(i + 4)
        left, right = shifted(q3)
        f3 = (q4 + q2 + left + right - 4.0 * q3) * inside(i + 3)
        fl, fr = shifted(f2)
        out = (
            0.8 * q2
            + up_c * pltpu.roll(q2, layers - 1, axis=0)
            + low_c * pltpu.roll(q2, 1, axis=0)
            + lap_c * f2
            - hyp_c * (f1 + f3 + fl + fr)
            - drift_c * side
        )
        write(i, out * inside(i + 2))
        return f2, f3, right - left

    unroll = 4

    def body(step, carries):
        carries = list(carries)
        for sub in range(unroll):
            for m in range(len(reads)):
                carries[m] = one(step * unroll + sub, carries[m], reads[m], writes[m])
        return tuple(carries)

    lax.fori_loop(0, count // unroll, body, tuple(start(read) for read in reads))


def cycle_kernel(
    sizes,
    fine_in,
    coarse_in,
    diff_ref,
    hyper_ref,
    drift_ref,
    val_ref,
    var_ref,
    row_ref,
    col_ref,
    layer_ref,
    count_ref,
    pair_out,
    mean_out,
    xv,
    zv,
    fq,
    cq,
    ft1,
    ft2,
    ct1,
    ct2,
    cres,
    g,
    ga,
    za,
    oc,
    rm,
    occ,
    rmc,
    sown,
    sx,
    ar0,
    ar1,
    kron_ref,
    inc,
    dg,
    dh,
    dl,
    mu,
    ob,
    mb,
    load_sem,
    hs_sem,
    hr_sem,
    ss_sem,
    sr_sem,
    as_sem,
    ar_sem,
    ts_sem,
    tr_sem,
    os_sem,
    or_sem,
    own_sem,
):
    tiles, groups, pairs, levels, K, RF, RC, NC, NCC, stages = sizes
    tile = lax.axis_index("rows")
    me = lax.axis_index("mem")
    level_all, pair_all = levels * groups, pairs * groups
    E = level_all + pair_all
    nv, nvc = NC // LANES, NCC // LANES
    lch, pch = levels // 2, pairs // 2
    RQ, RQC = RF // groups, RC // groups
    s_f, s_c = math.sqrt(pair_all - 1), math.sqrt(level_all - 1)

    def at(row, mem):
        return (row, mem)

    def mem_peer(i):
        return lax.rem(me + i, groups)

    def stage_peer(stage, i):
        stride, size = stage
        mine = lax.rem(tile // stride, size)
        return tile + (lax.rem(mine + i, size) - mine) * stride

    up = lax.rem(tile + tiles - 1, tiles)
    down = lax.rem(tile + 1, tiles)

    loads = []
    for v in range(nvc):
        loads.append(pltpu.make_async_copy(coarse_in.at[:, pl.ds(v * LANES, LANES)], zv.at[v], load_sem.at[v]))
    for v in range(nv):
        loads.append(pltpu.make_async_copy(fine_in.at[:, pl.ds(v * LANES, LANES)], xv.at[v], load_sem.at[nvc + v]))
    for load in loads:
        load.start()

    targets = [(up, me), (down, me)]
    targets += [(tile, mem_peer(i)) for i in range(1, groups)]
    for stage in stages:
        targets += [(stage_peer(stage, i), me) for i in range(1, stage[1])]
    barrier = pltpu.get_barrier_semaphore()
    for target in targets:
        pl.semaphore_signal(barrier, inc=1, device_id=at(*target), device_id_type=MESH)

    for load in loads[:nvc]:
        load.wait()

    def place_level(i, _):
        m, r = i // RC, lax.rem(i, RC)
        row = jnp.concatenate([zv[v, pl.ds(m * K * RC + r, K, stride=RC), :] for v in range(nvc)], 1)
        cq[m // 2, lax.rem(m, 2), HALO + r] = row
        return 0

    lax.fori_loop(0, levels * RC, place_level, 0)
    pl.semaphore_wait(barrier, len(targets))

    def coarse_halo(ch, way):
        src = HALO if way == 0 else RC
        dst = HALO + RC if way == 0 else 0
        return pltpu.make_async_remote_copy(
            src_ref=cq.at[ch, :, pl.ds(src, HALO)],
            dst_ref=cq.at[ch, :, pl.ds(dst, HALO)],
            send_sem=hs_sem.at[ch, way],
            recv_sem=hr_sem.at[ch, way],
            device_id=at(up if way == 0 else down, me),
            device_id_type=MESH,
        )

    def fine_halo(j, way):
        src = HALO if way == 0 else RF
        dst = HALO + RF if way == 0 else 0
        return pltpu.make_async_remote_copy(
            src_ref=fq.at[j, pl.ds(src, HALO)],
            dst_ref=fq.at[j, pl.ds(dst, HALO)],
            send_sem=hs_sem.at[lch + pch + j, way],
            recv_sem=hr_sem.at[lch + pch + j, way],
            device_id=at(up if way == 0 else down, me),
            device_id_type=MESH,
        )

    for ch in range(lch):
        for way in range(2):
            coarse_halo(ch, way).start()

    for load in loads[nvc:]:
        load.wait()

    halve = jnp.where(iota((NC, NCC), 0) // 2 == iota((NC, NCC), 1), 0.25, 0.0).astype(F32)
    widen = jnp.where(iota((NCC, NC), 1) // 2 == iota((NCC, NC), 0), 1.0, 0.0).astype(F32)
    widen_h = widen.astype(BF16)

    def place_fine(i, _):
        m, r = i // RF, lax.rem(i, RF)
        row = jnp.concatenate([xv[v, pl.ds(m * K * RF + r, K, stride=RF), :] for v in range(nv)], 1)
        fq[m, HALO + r] = row
        return 0

    lax.fori_loop(0, pairs * RF, place_fine, 0)
    for m in range(pairs):
        own = fq[m, HALO : HALO + RF].reshape(RC, 2, K, NC)
        rows = (own[:, 0] + own[:, 1]).reshape(RC * K, NC)
        cq[lch + m // 2, m % 2, HALO : HALO + RC] = exact_dot(rows, halve).reshape(RC, K, NCC)
    for ch in range(lch, lch + pch):
        for way in range(2):
            coarse_halo(ch, way).start()
    for j in range(pairs):
        for way in range(2):
            fine_halo(j, way).start()

    nb = 4
    per = val_ref.shape[0] * LANES // nb
    sub = per // LANES

    def row_of(ref, first, number):
        return jnp.concatenate([ref[i : i + 1, :] for i in range(first, first + number)], 1)

    for b in range(nb):
        col = row_of(col_ref, b * sub, sub)
        lay = row_of(layer_ref, b * sub, sub)
        loc = row_of(row_ref, b * sub, sub) - tile * RF
        oc[b] = jnp.where(iota((NC, per), 0) == col, 1.0, 0.0).astype(BF16)
        occ[b] = jnp.where(iota((NCC, per), 0) == (col >> 1), 1.0, 0.0).astype(BF16)
        rm[b] = jnp.where(iota((RF * K, per), 0) == loc * K + lay, 1.0, 0.0).astype(F32)
        rmc[b] = jnp.where(iota((RC * K, per), 0) == (loc >> 1) * K + lay, 1.0, 0.0).astype(F32)

    def coefs(scale_a, scale_h, scale_u, width):
        a = layer_vector(diff_ref, scale_a, K, width)
        h = layer_vector(hyper_ref, scale_h, K, width)
        u = layer_vector(drift_ref, scale_u, K, width)
        k = iota((K, width), 0)
        up_c = jnp.where(k < K - 1, 0.1, 0.0).astype(F32)
        low_c = jnp.where(k > 0, 0.1, 0.0).astype(F32)
        return a + 4.0 * h, h, 0.5 * u, up_c, low_c

    def zero_edges(clear_low, clear_high):
        @pl.when(tile == 0)
        def _():
            clear_low()

        @pl.when(tile == tiles - 1)
        def _():
            clear_high()

    coarse_coef = coefs(0.25, 0.0625, 0.5, NCC)
    row_c = tile * RC - HALO
    grid_c = tiles * RC

    def coarse_chunk(ch, _):
        coarse_halo(ch, 0).wait_recv()
        coarse_halo(ch, 1).wait_recv()

        def clear(first):
            cq[ch, :, first : first + HALO] = jnp.zeros((2, HALO, K, NCC), F32)

        zero_edges(lambda: clear(0), lambda: clear(HALO + RC))

        def reader(ref, m, lead):
            return lambda j: ref[lead + (m, j)]

        def writer(ref, m, lead):
            def write(i, value):
                ref[lead + (m, i)] = value
            return write

        both = range(2)
        advance([reader(cq, m, (ch,)) for m in both], [writer(ct1, m, ()) for m in both], RC + 8, row_c, grid_c, coarse_coef)
        advance([reader(ct1, m, ()) for m in both], [writer(ct2, m, ()) for m in both], RC + 4, row_c + 2, grid_c, coarse_coef)
        advance([reader(ct2, m, ()) for m in both], [writer(cres, m, (ch,)) for m in both], RC, row_c + 4, grid_c, coarse_coef)
        return 0

    lax.fori_loop(0, lch + pch, coarse_chunk, 0)

    def level_send(i):
        peer = mem_peer(i)
        return pltpu.make_async_remote_copy(
            src_ref=cres.at[pl.ds(0, lch), :, pl.ds(peer * RQC, RQC)],
            dst_ref=za.at[me],
            send_sem=ts_sem.at[0, i - 1],
            recv_sem=tr_sem.at[0, i - 1],
            device_id=at(tile, peer),
            device_id_type=MESH,
        )

    def pair_send(i):
        peer = mem_peer(i)
        return pltpu.make_async_remote_copy(
            src_ref=g.at[:, pl.ds(peer * RQ, RQ)],
            dst_ref=ga.at[me],
            send_sem=ts_sem.at[1, i - 1],
            recv_sem=tr_sem.at[1, i - 1],
            device_id=at(tile, peer),
            device_id_type=MESH,
        )

    for i in range(1, groups):
        level_send(i).start()

    fine_coef = coefs(1.0, 1.0, 1.0, NC)
    row_f = tile * RF - HALO
    grid_f = tiles * RF

    def fine_member(j, _):
        fine_halo(j, 0).wait_recv()
        fine_halo(j, 1).wait_recv()

        def clear(first):
            fq[j, first : first + HALO] = jnp.zeros((HALO, K, NC), F32)

        zero_edges(lambda: clear(0), lambda: clear(HALO + RF))

        def put(ref):
            def write(i, value):
                ref[i] = value
            return write

        def put_g(i, value):
            g[j, i] = value

        advance([lambda i: fq[j, i]], [put(ft1)], RF + 8, row_f, grid_f, fine_coef)
        advance([lambda i: ft1[i]], [put(ft2)], RF + 4, row_f + 2, grid_f, fine_coef)
        advance([lambda i: ft2[i]], [put_g], RF, row_f + 4, grid_f, fine_coef)
        coarse = cres[lch + j // 2, lax.rem(j, 2)].reshape(RC * K, NCC)
        wide = exact_dot(coarse, widen).reshape(RC, 1, K, NC)
        g[j] = (g[j].reshape(RC, 2, K, NC) - wide).reshape(RF, K, NC)
        return 0

    lax.fori_loop(0, pairs, fine_member, 0)

    def gather_block(b, _):
        high, low = halves(cres[0:lch].reshape(levels * RC * K, NCC))
        got = (dot(high, occ[b]) + dot(low, occ[b])).reshape(levels, RC * K, per)
        z = jnp.sum(got * rmc[b][None], axis=1)
        high, low = halves(g[...].reshape(pairs * RF * K, NC))
        got = (dot(high, oc[b]) + dot(low, oc[b])).reshape(pairs, RF * K, per)
        f = jnp.sum(got * rm[b][None], axis=1)
        rest = sown.shape[1] - levels - pairs
        sown[b] = jnp.concatenate([z, f, jnp.zeros((rest, per), F32)], 0)
        return 0

    lax.fori_loop(0, nb, gather_block, 0)

    def obs_send(i):
        return pltpu.make_async_remote_copy(
            src_ref=sown,
            dst_ref=sx.at[me],
            send_sem=ss_sem.at[i - 1],
            recv_sem=sr_sem.at[i - 1],
            device_id=at(tile, mem_peer(i)),
            device_id_type=MESH,
        )

    for i in range(1, groups):
        obs_send(i).start()
    for i in range(1, groups):
        pair_send(i).start()
    sx[me] = sown[...]
    own_level = pltpu.make_async_copy(cres.at[pl.ds(0, lch), :, pl.ds(me * RQC, RQC)], za.at[me], own_sem.at[0])
    own_pair = pltpu.make_async_copy(g.at[:, pl.ds(me * RQ, RQ)], ga.at[me], own_sem.at[1])
    own_level.start()
    own_pair.start()
    for i in range(1, groups):
        obs_send(i).wait_recv()

    gram = jnp.zeros((E + 8, E), F32)
    for b in range(nb):
        z = jnp.concatenate([sx[x, b, 0:levels] for x in range(groups)], 0)
        f = jnp.concatenate([sx[x, b, levels : levels + pairs] for x in range(groups)], 0)
        z_mean = jnp.mean(z, axis=0, keepdims=True)
        f_mean = jnp.mean(f, axis=0, keepdims=True)
        s = jnp.concatenate([(z - z_mean) * (1.0 / s_c), (f - f_mean) * (1.0 / s_f)], 0)
        innov = row_of(val_ref, b * sub, sub) - (z_mean + f_mean)
        slot = iota((1, per), 1) + b * per
        weight = jnp.where(slot < count_ref[0], 1.0 / row_of(var_ref, b * sub, sub), 0.0)
        extra = jnp.where(iota((8, per), 0) == 0, weight * innov, 0.0)
        left = jnp.concatenate([s * weight, extra], 0)
        gram = gram + lax.dot_general(
            left, s, (((1,), (1,)), ((), ())), precision=HIGHEST, preferred_element_type=F32
        )
    gram = jnp.concatenate([gram, jnp.zeros((E + 8, LANES - E), F32)], 1)

    slot0 = 0
    for s, stage in enumerate(stages):
        ar0[s] = gram
        sends = []
        for i in range(1, stage[1]):
            n = slot0 + i - 1
            send = pltpu.make_async_remote_copy(
                src_ref=ar0.at[s],
                dst_ref=ar1.at[n],
                send_sem=as_sem.at[n],
                recv_sem=ar_sem.at[n],
                device_id=at(stage_peer(stage, i), me),
                device_id_type=MESH,
            )
            send.start()
            sends.append((send, n))
        for send, n in sends:
            send.wait_recv()
            gram = gram + ar1[n]
        for send, n in sends:
            send.wait_send()
        slot0 += stage[1] - 1

    rows_t = E + pair_all + 8
    lane = iota((rows_t, LANES), 1)
    eye = jnp.where(iota((E, LANES), 0) == iota((E, LANES), 1), 1.0, 0.0).astype(F32)
    table = jnp.concatenate([gram[0:E] + eye, gram[level_all:E], gram[E:]], 0)
    for k in range(E):
        column = table[:, k : k + 1] * (1.0 / table[k : k + 1, k : k + 1])
        table = jnp.where(lane == k, column, table - column * table[k : k + 1, :])
    solved = jnp.concatenate([-0.5 * table[E : E + pair_all], table[E + pair_all :]], 0)

    spread = jnp.where(iota((LANES, E * K), 1) // K == iota((LANES, E * K), 0), 1.0, 0.0).astype(BF16)
    same = jnp.where(lax.rem(iota((K, E * K), 1), K) == iota((K, E * K), 0), 1.0, 0.0).astype(F32)
    coef_h, coef_l = halves(solved)

    def kron(part):
        wide = dot(part, spread)
        blocks = [wide[m : m + 1, :] * same for m in range(pair_all + 2)]
        return jnp.concatenate(blocks, 0).astype(BF16)

    kron_rows = kron_ref.shape[0] // 2
    kron_ref[0:kron_rows] = kron(coef_h)
    kron_ref[kron_rows:] = kron(coef_l)
    zk = level_all * K

    own_level.wait()
    own_pair.wait()
    for i in range(1, groups):
        level_send(i).wait_recv()
        pair_send(i).wait_recv()

    def anomalies(r, _):
        rc = r // 2
        z = za[:, :, :, rc].reshape(level_all, K, NCC)
        z_mean = jnp.mean(z, axis=0)
        high, low = halves(((z - z_mean[None]) * (1.0 / s_c)).reshape(zk, NCC))
        dh[r, 0:zk] = dot(high, widen_h).astype(BF16)
        dl[r, 0:zk] = dot(low, widen_h).astype(BF16)
        f = ga[:, :, r].reshape(pair_all, K, NC)
        f_mean = jnp.mean(f, axis=0)
        mu[r] = exact_dot(z_mean, widen) + f_mean
        anom = ((f - f_mean[None]) * (1.0 / s_f)).reshape(pair_all * K, NC)
        dg[r] = anom
        high, low = halves(anom)
        dh[r, zk:] = high
        dl[r, zk:] = low
        return 0

    lax.fori_loop(0, RQ, anomalies, 0)

    def result_send(r, i):
        peer = mem_peer(i)
        pair_copy = pltpu.make_async_remote_copy(
            src_ref=ob.at[pl.ds(peer * pairs, pairs), r],
            dst_ref=pair_out.at[:, me * RQ + r],
            send_sem=os_sem.at[0, r, i - 1],
            recv_sem=or_sem.at[0, r, i - 1],
            device_id=at(tile, peer),
            device_id_type=MESH,
        )
        mean_copy = pltpu.make_async_remote_copy(
            src_ref=mb.at[r],
            dst_ref=mean_out.at[me * RQ + r],
            send_sem=os_sem.at[1, r, i - 1],
            recv_sem=or_sem.at[1, r, i - 1],
            device_id=at(tile, peer),
            device_id_type=MESH,
        )
        return pair_copy, mean_copy

    np8 = pair_all * K

    def update(r, _):
        inc[...] = dot(kron_ref[...], dh[r])
        more = dot(kron_ref[0:kron_rows], dl[r])
        total = inc[0:kron_rows] + inc[kron_rows:] + more
        ob[:, r] = (s_f * (dg[r] + total[:np8])).reshape(pair_all, K, NC)
        mb[r] = mu[r] + total[np8 : np8 + K]
        for i in range(1, groups):
            for copy in result_send(r, i):
                copy.start()
        return 0

    lax.fori_loop(0, RQ, update, 0)
    own_out = pltpu.make_async_copy(ob.at[pl.ds(me * pairs, pairs)], pair_out.at[:, pl.ds(me * RQ, RQ)], own_sem.at[2])
    own_mean = pltpu.make_async_copy(mb, mean_out.at[pl.ds(me * RQ, RQ)], own_sem.at[3])
    own_out.start()
    own_mean.start()

    for ch in range(lch + pch):
        for way in range(2):
            coarse_halo(ch, way).wait_send()
    for j in range(pairs):
        for way in range(2):
            fine_halo(j, way).wait_send()
    for i in range(1, groups):
        level_send(i).wait_send()
        pair_send(i).wait_send()
        obs_send(i).wait_send()
    own_out.wait()
    own_mean.wait()
    for r in range(RQ):
        for i in range(1, groups):
            for copy in result_send(r, i):
                copy.wait_recv()
                copy.wait_send()


def order_kernel(K, RF, pair_in, mean_in, pair_out, mean_out, pv, mv, sem):
    nv = pv.shape[0]
    pairs = pair_in.shape[0]

    def put(value, ref, first, r):
        for v in range(nv):
            ref[v, pl.ds(first + r, K, stride=RF), :] = value[:, v * LANES : (v + 1) * LANES]

    def body(i, _):
        m, r = i // RF, lax.rem(i, RF)
        put(pair_in[m, r], pv, m * K * RF, r)
        return 0

    lax.fori_loop(0, pairs * RF, body, 0)

    def mean_body(r, _):
        put(mean_in[r], mv, 0, r)
        return 0

    lax.fori_loop(0, RF, mean_body, 0)
    copies = []
    for v in range(nv):
        copies.append(pltpu.make_async_copy(pv.at[v], pair_out.at[:, pl.ds(v * LANES, LANES)], sem.at[0, v]))
        copies.append(pltpu.make_async_copy(mv.at[v], mean_out.at[:, pl.ds(v * LANES, LANES)], sem.at[1, v]))
    for copy in copies:
        copy.start()
    for copy in copies:
        copy.wait()


def axis_stages(tiles):
    stages, stride = [], 1
    for size in (2, 4, 4):
        if stride < tiles:
            stages.append((stride, size))
            stride *= size
    return tuple(stages)


def per_device(
    fine_members,
    coarse_members,
    diffusion,
    hyper,
    drift,
    obs_value,
    obs_var,
    obs_row,
    obs_col,
    obs_layer,
    obs_count,
):
    tiles = lax.axis_size("rows")
    groups = lax.axis_size("mem")
    pairs, K, RF, NC = fine_members.shape
    levels, _, RC, NCC = coarse_members.shape
    stages = axis_stages(tiles)
    sizes = (tiles, groups, pairs, levels, K, RF, RC, NC, NCC, stages)
    slots = obs_value.shape[0]
    E = (pairs + levels) * groups
    nb = 4
    per = slots // nb
    RQ, RQC = RF // groups, RC // groups
    lch, pch = levels // 2, pairs // 2
    chunks = lch + pch + pairs
    peers = sum(size - 1 for _, size in stages)
    nv, nvc = NC // LANES, NCC // LANES
    srows = -(-(levels + pairs) // 8) * 8
    anyspace = pl.BlockSpec(memory_space=pl.ANY)
    vmem = pl.BlockSpec(memory_space=pltpu.VMEM)
    smem = pl.BlockSpec(memory_space=pltpu.SMEM)
    dma = pltpu.SemaphoreType.DMA

    def flat(obs):
        return obs.reshape(slots // LANES, LANES)

    pair_rows, mean_rows = pl.pallas_call(
        functools.partial(cycle_kernel, sizes),
        out_shape=(
            jax.ShapeDtypeStruct((pairs, RF, K, NC), F32),
            jax.ShapeDtypeStruct((RF, K, NC), F32),
        ),
        in_specs=[anyspace] * 2 + [smem] * 3 + [vmem] * 5 + [smem],
        out_specs=(anyspace, anyspace),
        scratch_shapes=[
            pltpu.VMEM((nv, pairs * K * RF, LANES), F32),
            pltpu.VMEM((nvc, levels * K * RC, LANES), F32),
            pltpu.VMEM((pairs, RF + 2 * HALO, K, NC), F32),
            pltpu.VMEM((lch + pch, 2, RC + 2 * HALO, K, NCC), F32),
            pltpu.VMEM((RF + 8, K, NC), F32),
            pltpu.VMEM((RF + 4, K, NC), F32),
            pltpu.VMEM((2, RC + 8, K, NCC), F32),
            pltpu.VMEM((2, RC + 4, K, NCC), F32),
            pltpu.VMEM((lch + pch, 2, RC, K, NCC), F32),
            pltpu.VMEM((pairs, RF, K, NC), F32),
            pltpu.VMEM((groups, pairs, RQ, K, NC), F32),
            pltpu.VMEM((groups, lch, 2, RQC, K, NCC), F32),
            pltpu.VMEM((nb, NC, per), BF16),
            pltpu.VMEM((nb, RF * K, per), F32),
            pltpu.VMEM((nb, NCC, per), BF16),
            pltpu.VMEM((nb, RC * K, per), F32),
            pltpu.VMEM((nb, srows, per), F32),
            pltpu.VMEM((groups, nb, srows, per), F32),
            pltpu.VMEM((len(stages), E + 8, LANES), F32),
            pltpu.VMEM((peers, E + 8, LANES), F32),
            pltpu.VMEM((2 * (pairs * groups + 2) * K, E * K), BF16),
            pltpu.VMEM((2 * (pairs * groups + 2) * K, NC), F32),
            pltpu.VMEM((RQ, pairs * groups * K, NC), F32),
            pltpu.VMEM((RQ, E * K, NC), BF16),
            pltpu.VMEM((RQ, E * K, NC), BF16),
            pltpu.VMEM((RQ, K, NC), F32),
            pltpu.VMEM((pairs * groups, RQ, K, NC), F32),
            pltpu.VMEM((RQ, K, NC), F32),
            dma((nv + nvc,)),
            dma((chunks, 2)),
            dma((chunks, 2)),
            dma((groups - 1,)),
            dma((groups - 1,)),
            dma((peers,)),
            dma((peers,)),
            dma((2, groups - 1)),
            dma((2, groups - 1)),
            dma((2, RQ, groups - 1)),
            dma((2, RQ, groups - 1)),
            dma((4,)),
        ],
        compiler_params=pltpu.CompilerParams(
            collective_id=0, has_side_effects=True, vmem_limit_bytes=48 * 1024 * 1024
        ),
        name="cycle",
    )(
        fine_members.reshape(pairs * K * RF, NC),
        coarse_members.reshape(levels * K * RC, NCC),
        diffusion,
        hyper,
        drift,
        flat(obs_value),
        flat(obs_var),
        flat(obs_row),
        flat(obs_col),
        flat(obs_layer),
        obs_count,
    )
    pair, mean = pl.pallas_call(
        functools.partial(order_kernel, K, RF),
        out_shape=(
            jax.ShapeDtypeStruct((pairs * K * RF, NC), F32),
            jax.ShapeDtypeStruct((K * RF, NC), F32),
        ),
        in_specs=[vmem, vmem],
        out_specs=(anyspace, anyspace),
        scratch_shapes=[
            pltpu.VMEM((nv, pairs * K * RF, LANES), F32),
            pltpu.VMEM((nv, K * RF, LANES), F32),
            dma((2, nv)),
        ],
        compiler_params=pltpu.CompilerParams(vmem_limit_bytes=16 * 1024 * 1024),
        name="order",
    )(pair_rows, mean_rows)
    return mean.reshape(K, RF, NC), pair.reshape(pairs, K, RF, NC)


def solution(mesh):
    in_specs = (
        P("mem", None, "rows", None),
        P("mem", None, "rows", None),
        P(),
        P(),
        P(),
        P("rows"),
        P("rows"),
        P("rows"),
        P("rows"),
        P("rows"),
        P("rows"),
    )
    out_specs = (P(None, "rows", None), P("mem", None, "rows", None))
    return jax.shard_map(
        per_device, mesh=mesh, in_specs=in_specs, out_specs=out_specs, check_vma=False
    )
```

```python
import functools
import math

import jax
import jax.numpy as jnp
from jax import lax
from jax.experimental import pallas as pl
from jax.experimental.pallas import tpu as pltpu
from jax.sharding import PartitionSpec as P

STEPS = 3
HALO = 2 * STEPS
LANES = 128
MESH = pl.DeviceIdType.MESH
HIGHEST = lax.Precision.HIGHEST
F32 = jnp.float32
BF16 = jnp.bfloat16


def iota(shape, axis):
    return lax.broadcasted_iota(jnp.int32, shape, axis)


def halves(value):
    high = value.astype(BF16)
    return high, (value - high.astype(F32)).astype(BF16)


def dot(left, right):
    return jnp.dot(left, right, preferred_element_type=F32)


def select_dot(left, right):
    rows = left.shape[0]
    high = left.astype(BF16)
    rest = left - high.astype(F32)
    mid = rest.astype(BF16)
    low = (rest - mid.astype(F32)).astype(BF16)
    out = dot(jnp.concatenate([high, mid, low], 0), right)
    return out[:rows] + (out[rows : 2 * rows] + out[2 * rows :])


def shifted(row):
    width = row.shape[-1]
    return pltpu.roll(row, 1, axis=1), pltpu.roll(row, width - 1, axis=1)


def layer_vector(ref, scale, layers, width):
    at = iota((layers, width), 0)
    out = jnp.zeros((layers, width), F32)
    for k in range(layers):
        out = jnp.where(at == k, ref[k] * scale, out)
    return out


def advance(reads, writes, count, first_row, grid_rows, coef):
    lap_c, hyp_c, drift_c, up_c, low_c = coef
    layers = up_c.shape[0]

    def inside(j):
        at = first_row + j
        return jnp.where((at >= 0) & (at < grid_rows), 1.0, 0.0).astype(F32)

    def start(read):
        q0, q1, q2, q3 = read(0), read(1), read(2), read(3)
        left, right = shifted(q1)
        f1 = (q2 + q0 + left + right - 4.0 * q1) * inside(1)
        left, right = shifted(q2)
        f2 = (q3 + q1 + left + right - 4.0 * q2) * inside(2)
        return f1, f2, right - left

    def one(i, carry, read, write):
        f1, f2, side = carry
        q2, q3, q4 = read(i + 2), read(i + 3), read(i + 4)
        left, right = shifted(q3)
        f3 = (q4 + q2 + left + right - 4.0 * q3) * inside(i + 3)
        fl, fr = shifted(f2)
        out = (
            0.8 * q2
            + up_c * pltpu.roll(q2, layers - 1, axis=0)
            + low_c * pltpu.roll(q2, 1, axis=0)
            + lap_c * f2
            - hyp_c * (f1 + f3 + fl + fr)
            - drift_c * side
        )
        write(i, out * inside(i + 2))
        return f2, f3, right - left

    carries = [start(read) for read in reads]
    for i in range(count):
        for m in range(len(reads)):
            carries[m] = one(i, carries[m], reads[m], writes[m])


def cycle_kernel(
    sizes,
    fine_in,
    coarse_in,
    diff_in,
    hyper_in,
    drift_in,
    val_in,
    var_in,
    row_in,
    col_in,
    layer_in,
    count_in,
    pair_out,
    mean_out,
    diff_ref,
    hyper_ref,
    drift_ref,
    count_ref,
    val_ref,
    var_ref,
    row_ref,
    col_ref,
    layer_ref,
    xv,
    zv,
    fq,
    cq,
    ft1,
    ft2,
    ct1,
    ct2,
    cres,
    g,
    ga,
    za,
    oc,
    rm,
    occ,
    rmc,
    sown,
    sx,
    ar0,
    ar1,
    kron_ref,
    inc,
    dg,
    dh,
    dl,
    mu,
    ob,
    mb,
    load_sem,
    small_sem,
    hs_sem,
    hr_sem,
    ss_sem,
    sr_sem,
    as_sem,
    ar_sem,
    ts_sem,
    tr_sem,
    os_sem,
    or_sem,
    own_sem,
):
    tiles, groups, pairs, levels, K, RF, RC, NC, NCC, stages = sizes
    tile = lax.axis_index("rows")
    me = lax.axis_index("mem")
    level_all, pair_all = levels * groups, pairs * groups
    E = level_all + pair_all
    nv, nvc = NC // LANES, NCC // LANES
    lch, pch = levels // 2, pairs // 2
    RQ, RQC = RF // groups, RC // groups
    s_f, s_c = math.sqrt(pair_all - 1), math.sqrt(level_all - 1)

    def at(row, mem):
        return (row, mem)

    def mem_peer(i):
        return lax.rem(me + i, groups)

    def stage_peer(stage, i):
        stride, size = stage
        mine = lax.rem(tile // stride, size)
        return tile + (lax.rem(mine + i, size) - mine) * stride

    up = lax.rem(tile + tiles - 1, tiles)
    down = lax.rem(tile + 1, tiles)

    loads = []
    for v in range(nvc):
        loads.append(pltpu.make_async_copy(coarse_in.at[:, pl.ds(v * LANES, LANES)], zv.at[v], load_sem.at[v]))
    for v in range(nv):
        loads.append(pltpu.make_async_copy(fine_in.at[:, pl.ds(v * LANES, LANES)], xv.at[v], load_sem.at[nvc + v]))
    for load in loads:
        load.start()
    smalls = [
        (diff_in, diff_ref),
        (hyper_in, hyper_ref),
        (drift_in, drift_ref),
        (count_in, count_ref),
        (val_in, val_ref),
        (var_in, var_ref),
        (row_in, row_ref),
        (col_in, col_ref),
        (layer_in, layer_ref),
    ]
    smalls = [pltpu.make_async_copy(a, b, small_sem.at[n]) for n, (a, b) in enumerate(smalls)]
    for small in smalls:
        small.start()

    targets = [(up, me), (down, me)]
    targets += [(tile, mem_peer(i)) for i in range(1, groups)]
    for stage in stages:
        targets += [(stage_peer(stage, i), me) for i in range(1, stage[1])]
    barrier = pltpu.get_barrier_semaphore()
    for target in targets:
        pl.semaphore_signal(barrier, inc=1, device_id=at(*target), device_id_type=MESH)

    for load in loads[:nvc]:
        load.wait()

    def place_level(m, _):
        for r in range(RC):
            row = jnp.concatenate([zv[v, pl.ds(m * K * RC + r, K, stride=RC), :] for v in range(nvc)], 1)
            cq[m // 2, lax.rem(m, 2), HALO + r] = row
        return 0

    lax.fori_loop(0, levels, place_level, 0)
    pl.semaphore_wait(barrier, len(targets))

    def coarse_halo(ch, way):
        src = HALO if way == 0 else RC
        dst = HALO + RC if way == 0 else 0
        return pltpu.make_async_remote_copy(
            src_ref=cq.at[ch, :, pl.ds(src, HALO)],
            dst_ref=cq.at[ch, :, pl.ds(dst, HALO)],
            send_sem=hs_sem.at[ch, way],
            recv_sem=hr_sem.at[ch, way],
            device_id=at(up if way == 0 else down, me),
            device_id_type=MESH,
        )

    def fine_halo(j, way):
        src = HALO if way == 0 else RF
        dst = HALO + RF if way == 0 else 0
        return pltpu.make_async_remote_copy(
            src_ref=fq.at[j, pl.ds(src, HALO)],
            dst_ref=fq.at[j, pl.ds(dst, HALO)],
            send_sem=hs_sem.at[lch + pch + j, way],
            recv_sem=hr_sem.at[lch + pch + j, way],
            device_id=at(up if way == 0 else down, me),
            device_id_type=MESH,
        )

    for ch in range(lch):
        for way in range(2):
            coarse_halo(ch, way).start()

    for load in loads[nvc:]:
        load.wait()

    halve = jnp.where(iota((NC, NCC), 0) // 2 == iota((NC, NCC), 1), 0.25, 0.0).astype(BF16)
    widen = jnp.where(iota((NCC, NC), 1) // 2 == iota((NCC, NC), 0), 1.0, 0.0).astype(BF16)

    def place_fine(m, _):
        for r in range(RF):
            row = jnp.concatenate([xv[v, pl.ds(m * K * RF + r, K, stride=RF), :] for v in range(nv)], 1)
            fq[m, HALO + r] = row
        own = fq[m, HALO : HALO + RF].reshape(RC, 2, K, NC)
        rows = (own[:, 0] + own[:, 1]).reshape(RC * K, NC)
        cq[lch + m // 2, lax.rem(m, 2), HALO : HALO + RC] = select_dot(rows, halve).reshape(RC, K, NCC)
        return 0

    lax.fori_loop(0, pairs, place_fine, 0)
    for ch in range(lch, lch + pch):
        for way in range(2):
            coarse_halo(ch, way).start()
    for j in range(pairs):
        for way in range(2):
            fine_halo(j, way).start()

    for small in smalls:
        small.wait()
    nb = 4
    per = val_ref.shape[0] * LANES // nb
    sub = per // LANES

    def row_of(ref, first, number):
        return jnp.concatenate([ref[i : i + 1, :] for i in range(first, first + number)], 1)

    for b in range(nb):
        col = row_of(col_ref, b * sub, sub)
        lay = row_of(layer_ref, b * sub, sub)
        loc = row_of(row_ref, b * sub, sub) - tile * RF
        oc[b] = jnp.where(iota((NC, per), 0) == col, 1.0, 0.0).astype(BF16)
        occ[b] = jnp.where(iota((NCC, per), 0) == (col >> 1), 1.0, 0.0).astype(BF16)
        rm[b] = jnp.where(iota((RF * K, per), 0) == loc * K + lay, 1.0, 0.0).astype(F32)
        rmc[b] = jnp.where(iota((RC * K, per), 0) == (loc >> 1) * K + lay, 1.0, 0.0).astype(F32)

    def coefs(scale_a, scale_h, scale_u, width):
        a = layer_vector(diff_ref, scale_a, K, width)
        h = layer_vector(hyper_ref, scale_h, K, width)
        u = layer_vector(drift_ref, scale_u, K, width)
        k = iota((K, width), 0)
        up_c = jnp.where(k < K - 1, 0.1, 0.0).astype(F32)
        low_c = jnp.where(k > 0, 0.1, 0.0).astype(F32)
        return a + 4.0 * h, h, 0.5 * u, up_c, low_c

    def zero_edges(clear_low, clear_high):
        @pl.when(tile == 0)
        def _():
            clear_low()

        @pl.when(tile == tiles - 1)
        def _():
            clear_high()

    coarse_coef = coefs(0.25, 0.0625, 0.5, NCC)
    row_c = tile * RC - HALO
    grid_c = tiles * RC

    def coarse_chunk(ch, _):
        coarse_halo(ch, 0).wait_recv()
        coarse_halo(ch, 1).wait_recv()

        def clear(first):
            cq[ch, :, first : first + HALO] = jnp.zeros((2, HALO, K, NCC), F32)

        zero_edges(lambda: clear(0), lambda: clear(HALO + RC))

        def reader(ref, m, lead):
            return lambda j: ref[lead + (m, j)]

        def writer(ref, m, lead):
            def write(i, value):
                ref[lead + (m, i)] = value
            return write

        both = range(2)
        advance([reader(cq, m, (ch,)) for m in both], [writer(ct1, m, ()) for m in both], RC + 8, row_c, grid_c, coarse_coef)
        advance([reader(ct1, m, ()) for m in both], [writer(ct2, m, ()) for m in both], RC + 4, row_c + 2, grid_c, coarse_coef)
        advance([reader(ct2, m, ()) for m in both], [writer(cres, m, (ch,)) for m in both], RC, row_c + 4, grid_c, coarse_coef)
        return 0

    lax.fori_loop(0, lch + pch, coarse_chunk, 0)

    def level_send(i):
        peer = mem_peer(i)
        return pltpu.make_async_remote_copy(
            src_ref=cres.at[pl.ds(0, lch), :, pl.ds(peer * RQC, RQC)],
            dst_ref=za.at[me],
            send_sem=ts_sem.at[0, i - 1],
            recv_sem=tr_sem.at[0, i - 1],
            device_id=at(tile, peer),
            device_id_type=MESH,
        )

    def pair_send(i):
        peer = mem_peer(i)
        return pltpu.make_async_remote_copy(
            src_ref=g.at[:, pl.ds(peer * RQ, RQ)],
            dst_ref=ga.at[me],
            send_sem=ts_sem.at[1, i - 1],
            recv_sem=tr_sem.at[1, i - 1],
            device_id=at(tile, peer),
            device_id_type=MESH,
        )

    for i in range(1, groups):
        level_send(i).start()

    fine_coef = coefs(1.0, 1.0, 1.0, NC)
    row_f = tile * RF - HALO
    grid_f = tiles * RF

    def fine_member(j, _):
        fine_halo(j, 0).wait_recv()
        fine_halo(j, 1).wait_recv()

        def clear(first):
            fq[j, first : first + HALO] = jnp.zeros((HALO, K, NC), F32)

        zero_edges(lambda: clear(0), lambda: clear(HALO + RF))

        def put(ref):
            def write(i, value):
                ref[i] = value
            return write

        def put_g(i, value):
            g[j, i] = value

        advance([lambda i: fq[j, i]], [put(ft1)], RF + 8, row_f, grid_f, fine_coef)
        advance([lambda i: ft1[i]], [put(ft2)], RF + 4, row_f + 2, grid_f, fine_coef)
        advance([lambda i: ft2[i]], [put_g], RF, row_f + 4, grid_f, fine_coef)
        coarse = cres[lch + j // 2, lax.rem(j, 2)].reshape(RC * K, NCC)
        wide = select_dot(coarse, widen).reshape(RC, 1, K, NC)
        g[j] = (g[j].reshape(RC, 2, K, NC) - wide).reshape(RF, K, NC)
        return 0

    lax.fori_loop(0, pairs, fine_member, 0)

    def gather_block(b, _):
        high, low = halves(cres[0:lch].reshape(levels * RC * K, NCC))
        got = (dot(high, occ[b]) + dot(low, occ[b])).reshape(levels, RC * K, per)
        z = jnp.sum(got * rmc[b][None], axis=1)
        high, low = halves(g[...].reshape(pairs * RF * K, NC))
        got = (dot(high, oc[b]) + dot(low, oc[b])).reshape(pairs, RF * K, per)
        f = jnp.sum(got * rm[b][None], axis=1)
        rest = sown.shape[1] - levels - pairs
        sown[b] = jnp.concatenate([z, f, jnp.zeros((rest, per), F32)], 0)
        return 0

    lax.fori_loop(0, nb, gather_block, 0)

    def obs_send(i):
        return pltpu.make_async_remote_copy(
            src_ref=sown,
            dst_ref=sx.at[me],
            send_sem=ss_sem.at[i - 1],
            recv_sem=sr_sem.at[i - 1],
            device_id=at(tile, mem_peer(i)),
            device_id_type=MESH,
        )

    for i in range(1, groups):
        obs_send(i).start()
    for i in range(1, groups):
        pair_send(i).start()
    sx[me] = sown[...]
    own_level = pltpu.make_async_copy(cres.at[pl.ds(0, lch), :, pl.ds(me * RQC, RQC)], za.at[me], own_sem.at[0])
    own_pair = pltpu.make_async_copy(g.at[:, pl.ds(me * RQ, RQ)], ga.at[me], own_sem.at[1])
    own_level.start()
    own_pair.start()
    for i in range(1, groups):
        obs_send(i).wait_recv()

    gram = jnp.zeros((E + 8, E), F32)
    for b in range(nb):
        z = jnp.concatenate([sx[x, b, 0:levels] for x in range(groups)], 0)
        f = jnp.concatenate([sx[x, b, levels : levels + pairs] for x in range(groups)], 0)
        z_mean = jnp.mean(z, axis=0, keepdims=True)
        f_mean = jnp.mean(f, axis=0, keepdims=True)
        s = jnp.concatenate([(z - z_mean) * (1.0 / s_c), (f - f_mean) * (1.0 / s_f)], 0)
        innov = row_of(val_ref, b * sub, sub) - (z_mean + f_mean)
        slot = iota((1, per), 1) + b * per
        weight = jnp.where(slot < count_ref[0], 1.0 / row_of(var_ref, b * sub, sub), 0.0)
        extra = jnp.where(iota((8, per), 0) == 0, weight * innov, 0.0)
        left = jnp.concatenate([s * weight, extra], 0)
        gram = gram + lax.dot_general(
            left, s, (((1,), (1,)), ((), ())), precision=HIGHEST, preferred_element_type=F32
        )
    gram = jnp.concatenate([gram, jnp.zeros((E + 8, LANES - E), F32)], 1)

    zk = level_all * K

    def level_anomalies():
        own_level.wait()
        for i in range(1, groups):
            level_send(i).wait_recv()

        def one(rc, _):
            z = za[:, :, :, rc].reshape(level_all, K, NCC)
            z_mean = jnp.mean(z, axis=0)
            high, low = halves(((z - z_mean[None]) * (1.0 / s_c)).reshape(zk, NCC))
            high, low = dot(high, widen).astype(BF16), dot(low, widen).astype(BF16)
            wide_mean = select_dot(z_mean, widen)
            for half in range(2):
                dh[2 * rc + half, 0:zk] = high
                dl[2 * rc + half, 0:zk] = low
                mu[2 * rc + half] = wide_mean
            return 0

        lax.fori_loop(0, RQC, one, 0)

    slot0 = 0
    for s, stage in enumerate(stages):
        ar0[s] = gram
        sends = []
        for i in range(1, stage[1]):
            n = slot0 + i - 1
            send = pltpu.make_async_remote_copy(
                src_ref=ar0.at[s],
                dst_ref=ar1.at[n],
                send_sem=as_sem.at[n],
                recv_sem=ar_sem.at[n],
                device_id=at(stage_peer(stage, i), me),
                device_id_type=MESH,
            )
            send.start()
            sends.append((send, n))
        if s == 0:
            level_anomalies()
        for send, n in sends:
            send.wait_recv()
            gram = gram + ar1[n]
        for send, n in sends:
            send.wait_send()
        slot0 += stage[1] - 1

    rows_t = E + pair_all + 8
    lane = iota((rows_t, LANES), 1)
    eye = jnp.where(iota((E, LANES), 0) == iota((E, LANES), 1), 1.0, 0.0).astype(F32)
    table = jnp.concatenate([gram[0:E] + eye, gram[level_all:E], gram[E:]], 0)
    width = 4
    for k in range(0, E, width):
        block = range(width)
        columns = [jnp.broadcast_to(table[:, k + i : k + i + 1], (rows_t, LANES)) for i in block]
        heads = [table[k + i : k + i + 1, :] for i in block]
        inv = [[columns[j][k + i : k + i + 1, :] for j in block] for i in block]
        for p in block:
            pivot = 1.0 / inv[p][p]
            scaled = [pivot if j == p else inv[p][j] * pivot for j in block]
            inv = [
                scaled
                if i == p
                else [
                    -inv[i][p] * pivot if j == p else inv[i][j] - inv[i][p] * scaled[j] for j in block
                ]
                for i in block
            ]
        ends = []
        for i in block:
            end = columns[0] * inv[0][i]
            for j in range(1, width):
                end = end + columns[j] * inv[j][i]
            ends.append(end)
        change = ends[0] * heads[0]
        for i in range(1, width):
            change = change + ends[i] * heads[i]
        table = table - change
        for i in block:
            table = jnp.where(lane == k + i, ends[i], table)
    solved = jnp.concatenate([-0.5 * table[E : E + pair_all], table[E + pair_all :]], 0)

    spread = jnp.where(iota((LANES, E * K), 1) // K == iota((LANES, E * K), 0), 1.0, 0.0).astype(BF16)
    same = jnp.where(lax.rem(iota((K, E * K), 1), K) == iota((K, E * K), 0), 1.0, 0.0).astype(F32)
    coef_h, coef_l = halves(solved)

    def kron(part):
        wide = dot(part, spread)
        blocks = [wide[m : m + 1, :] * same for m in range(pair_all + 2)]
        return jnp.concatenate(blocks, 0).astype(BF16)

    kron_rows = kron_ref.shape[0] // 2
    kron_ref[0:kron_rows] = kron(coef_h)
    kron_ref[kron_rows:] = kron(coef_l)

    own_pair.wait()
    for i in range(1, groups):
        pair_send(i).wait_recv()

    def pair_anomalies(r, _):
        f = ga[:, :, r].reshape(pair_all, K, NC)
        f_mean = jnp.mean(f, axis=0)
        mu[r] = mu[r] + f_mean
        anom = ((f - f_mean[None]) * (1.0 / s_f)).reshape(pair_all * K, NC)
        dg[r] = anom
        high, low = halves(anom)
        dh[r, zk:] = high
        dl[r, zk:] = low
        return 0

    lax.fori_loop(0, RQ, pair_anomalies, 0)

    def result_send(r, i):
        peer = mem_peer(i)
        pair_copy = pltpu.make_async_remote_copy(
            src_ref=ob.at[pl.ds(peer * pairs, pairs), r],
            dst_ref=pair_out.at[:, me * RQ + r],
            send_sem=os_sem.at[0, r, i - 1],
            recv_sem=or_sem.at[0, r, i - 1],
            device_id=at(tile, peer),
            device_id_type=MESH,
        )
        mean_copy = pltpu.make_async_remote_copy(
            src_ref=mb.at[r],
            dst_ref=mean_out.at[me * RQ + r],
            send_sem=os_sem.at[1, r, i - 1],
            recv_sem=or_sem.at[1, r, i - 1],
            device_id=at(tile, peer),
            device_id_type=MESH,
        )
        return pair_copy, mean_copy

    np8 = pair_all * K

    def update(r, _):
        inc[...] = dot(kron_ref[...], dh[r])
        more = dot(kron_ref[0:kron_rows], dl[r])
        total = inc[0:kron_rows] + inc[kron_rows:] + more
        ob[:, r] = (s_f * (dg[r] + total[:np8])).reshape(pair_all, K, NC)
        mb[r] = mu[r] + total[np8 : np8 + K]
        for i in range(1, groups):
            for copy in result_send(r, i):
                copy.start()
        return 0

    lax.fori_loop(0, RQ, update, 0)
    own_out = pltpu.make_async_copy(ob.at[pl.ds(me * pairs, pairs)], pair_out.at[:, pl.ds(me * RQ, RQ)], own_sem.at[2])
    own_mean = pltpu.make_async_copy(mb, mean_out.at[pl.ds(me * RQ, RQ)], own_sem.at[3])
    own_out.start()
    own_mean.start()

    for ch in range(lch + pch):
        for way in range(2):
            coarse_halo(ch, way).wait_send()
    for j in range(pairs):
        for way in range(2):
            fine_halo(j, way).wait_send()
    for i in range(1, groups):
        level_send(i).wait_send()
        pair_send(i).wait_send()
        obs_send(i).wait_send()
    own_out.wait()
    own_mean.wait()
    for r in range(RQ):
        for i in range(1, groups):
            for copy in result_send(r, i):
                copy.wait_recv()
                copy.wait_send()


def order_kernel(K, RF, pair_in, mean_in, pair_out, mean_out, pv, mv, sem):
    nv = pv.shape[0]
    pairs = pair_in.shape[0]

    def put(value, ref, first, r):
        for v in range(nv):
            ref[v, pl.ds(first + r, K, stride=RF), :] = value[:, v * LANES : (v + 1) * LANES]

    copies = []

    def send(ref, first, out, row):
        for v in range(nv):
            copy = pltpu.make_async_copy(
                ref.at[v, pl.ds(first, K * RF)],
                out.at[pl.ds(first, K * RF), pl.ds(v * LANES, LANES)],
                sem.at[row, v],
            )
            copy.start()
            copies.append(copy)

    for m in range(pairs):
        for r in range(RF):
            put(pair_in[m, r], pv, m * K * RF, r)
        send(pv, m * K * RF, pair_out, m)
    for r in range(RF):
        put(mean_in[r], mv, 0, r)
    send(mv, 0, mean_out, pairs)
    for copy in copies:
        copy.wait()


def axis_stages(tiles):
    stages, stride = [], 1
    for size in (2, 4, 4):
        if stride < tiles:
            stages.append((stride, size))
            stride *= size
    return tuple(stages)


def per_device(
    fine_members,
    coarse_members,
    diffusion,
    hyper,
    drift,
    obs_value,
    obs_var,
    obs_row,
    obs_col,
    obs_layer,
    obs_count,
):
    tiles = lax.axis_size("rows")
    groups = lax.axis_size("mem")
    pairs, K, RF, NC = fine_members.shape
    levels, _, RC, NCC = coarse_members.shape
    stages = axis_stages(tiles)
    sizes = (tiles, groups, pairs, levels, K, RF, RC, NC, NCC, stages)
    slots = obs_value.shape[0]
    E = (pairs + levels) * groups
    nb = 4
    per = slots // nb
    RQ, RQC = RF // groups, RC // groups
    lch, pch = levels // 2, pairs // 2
    chunks = lch + pch + pairs
    peers = sum(size - 1 for _, size in stages)
    nv, nvc = NC // LANES, NCC // LANES
    srows = -(-(levels + pairs) // 8) * 8
    anyspace = pl.BlockSpec(memory_space=pl.ANY)
    hbm = pl.BlockSpec(memory_space=pltpu.HBM)
    vmem = pl.BlockSpec(memory_space=pltpu.VMEM)
    dma = pltpu.SemaphoreType.DMA

    def flat(obs):
        return obs.reshape(slots // LANES, LANES)

    def keep(array):
        return pltpu.with_memory_space_constraint(array, pltpu.HBM)

    pair_rows, mean_rows = pl.pallas_call(
        functools.partial(cycle_kernel, sizes),
        out_shape=(
            jax.ShapeDtypeStruct((pairs, RF, K, NC), F32),
            jax.ShapeDtypeStruct((RF, K, NC), F32),
        ),
        in_specs=[hbm] * 11,
        out_specs=(anyspace, anyspace),
        scratch_shapes=[
            pltpu.SMEM((K,), F32),
            pltpu.SMEM((K,), F32),
            pltpu.SMEM((K,), F32),
            pltpu.SMEM((1,), jnp.int32),
            pltpu.VMEM((slots // LANES, LANES), F32),
            pltpu.VMEM((slots // LANES, LANES), F32),
            pltpu.VMEM((slots // LANES, LANES), jnp.int32),
            pltpu.VMEM((slots // LANES, LANES), jnp.int32),
            pltpu.VMEM((slots // LANES, LANES), jnp.int32),
            pltpu.VMEM((nv, pairs * K * RF, LANES), F32),
            pltpu.VMEM((nvc, levels * K * RC, LANES), F32),
            pltpu.VMEM((pairs, RF + 2 * HALO, K, NC), F32),
            pltpu.VMEM((lch + pch, 2, RC + 2 * HALO, K, NCC), F32),
            pltpu.VMEM((RF + 8, K, NC), F32),
            pltpu.VMEM((RF + 4, K, NC), F32),
            pltpu.VMEM((2, RC + 8, K, NCC), F32),
            pltpu.VMEM((2, RC + 4, K, NCC), F32),
            pltpu.VMEM((lch + pch, 2, RC, K, NCC), F32),
            pltpu.VMEM((pairs, RF, K, NC), F32),
            pltpu.VMEM((groups, pairs, RQ, K, NC), F32),
            pltpu.VMEM((groups, lch, 2, RQC, K, NCC), F32),
            pltpu.VMEM((nb, NC, per), BF16),
            pltpu.VMEM((nb, RF * K, per), F32),
            pltpu.VMEM((nb, NCC, per), BF16),
            pltpu.VMEM((nb, RC * K, per), F32),
            pltpu.VMEM((nb, srows, per), F32),
            pltpu.VMEM((groups, nb, srows, per), F32),
            pltpu.VMEM((len(stages), E + 8, LANES), F32),
            pltpu.VMEM((peers, E + 8, LANES), F32),
            pltpu.VMEM((2 * (pairs * groups + 2) * K, E * K), BF16),
            pltpu.VMEM((2 * (pairs * groups + 2) * K, NC), F32),
            pltpu.VMEM((RQ, pairs * groups * K, NC), F32),
            pltpu.VMEM((RQ, E * K, NC), BF16),
            pltpu.VMEM((RQ, E * K, NC), BF16),
            pltpu.VMEM((RQ, K, NC), F32),
            pltpu.VMEM((pairs * groups, RQ, K, NC), F32),
            pltpu.VMEM((RQ, K, NC), F32),
            dma((nv + nvc,)),
            dma((9,)),
            dma((chunks, 2)),
            dma((chunks, 2)),
            dma((groups - 1,)),
            dma((groups - 1,)),
            dma((peers,)),
            dma((peers,)),
            dma((2, groups - 1)),
            dma((2, groups - 1)),
            dma((2, RQ, groups - 1)),
            dma((2, RQ, groups - 1)),
            dma((4,)),
        ],
        compiler_params=pltpu.CompilerParams(
            collective_id=0, has_side_effects=True, vmem_limit_bytes=48 * 1024 * 1024
        ),
        name="cycle",
    )(
        keep(fine_members.reshape(pairs * K * RF, NC)),
        keep(coarse_members.reshape(levels * K * RC, NCC)),
        keep(diffusion),
        keep(hyper),
        keep(drift),
        keep(flat(obs_value)),
        keep(flat(obs_var)),
        keep(flat(obs_row)),
        keep(flat(obs_col)),
        keep(flat(obs_layer)),
        obs_count,
    )
    pair, mean = pl.pallas_call(
        functools.partial(order_kernel, K, RF),
        out_shape=(
            jax.ShapeDtypeStruct((pairs * K * RF, NC), F32),
            jax.ShapeDtypeStruct((K * RF, NC), F32),
        ),
        in_specs=[vmem, vmem],
        out_specs=(anyspace, anyspace),
        scratch_shapes=[
            pltpu.VMEM((nv, pairs * K * RF, LANES), F32),
            pltpu.VMEM((nv, K * RF, LANES), F32),
            dma((pairs + 1, nv)),
        ],
        compiler_params=pltpu.CompilerParams(vmem_limit_bytes=16 * 1024 * 1024),
        name="order",
    )(pair_rows, mean_rows)
    return mean.reshape(K, RF, NC), pair.reshape(pairs, K, RF, NC)


def solution(mesh):
    in_specs = (
        P("mem", None, "rows", None),
        P("mem", None, "rows", None),
        P(),
        P(),
        P(),
        P("rows"),
        P("rows"),
        P("rows"),
        P("rows"),
        P("rows"),
        P("rows"),
    )
    out_specs = (P(None, "rows", None), P("mem", None, "rows", None))
    return jax.shard_map(
        per_device, mesh=mesh, in_specs=in_specs, out_specs=out_specs, check_vma=False
    )
```

```python
import functools
import math

import jax
import jax.numpy as jnp
from jax import lax
from jax.experimental import pallas as pl
from jax.experimental.pallas import tpu as pltpu
from jax.sharding import PartitionSpec as P

STEPS = 3
HALO = 2 * STEPS
LANES = 128
MESH = pl.DeviceIdType.MESH
HIGHEST = lax.Precision.HIGHEST
F32 = jnp.float32
BF16 = jnp.bfloat16


def iota(shape, axis):
    return lax.broadcasted_iota(jnp.int32, shape, axis)


def halves(value):
    high = value.astype(BF16)
    return high, (value - high.astype(F32)).astype(BF16)


def dot(left, right):
    return jnp.dot(left, right, preferred_element_type=F32)


def select_dot(left, right):
    rows = left.shape[0]
    high = left.astype(BF16)
    rest = left - high.astype(F32)
    mid = rest.astype(BF16)
    low = (rest - mid.astype(F32)).astype(BF16)
    out = dot(jnp.concatenate([high, mid, low], 0), right)
    return out[:rows] + (out[rows : 2 * rows] + out[2 * rows :])


def column_at(place, parts):
    return (place % LANES) * parts + place // LANES


def place_of(column, parts):
    shift = parts.bit_length() - 1
    return (column & (parts - 1)) * LANES + (column >> shift)


def shifted(row):
    width = row.shape[-1]
    first, last = row[:, :LANES], row[:, width - LANES :]
    left = jnp.concatenate([pltpu.roll(last, 1, axis=1), row[:, : width - LANES]], 1)
    right = jnp.concatenate([row[:, LANES:], pltpu.roll(first, LANES - 1, axis=1)], 1)
    return left, right


def halved(row):
    tiles = [row[:, i * LANES : (i + 1) * LANES] for i in range(row.shape[1] // LANES)]
    return jnp.concatenate([a + b for a, b in zip(tiles[::2], tiles[1::2])], 1)


def doubled(row):
    tiles = [row[:, i * LANES : (i + 1) * LANES] for i in range(row.shape[1] // LANES)]
    return jnp.concatenate([tile for tile in tiles for _ in range(2)], 1)


def layer_vector(ref, scale, layers, width):
    at = iota((layers, width), 0)
    out = jnp.zeros((layers, width), F32)
    for k in range(layers):
        out = jnp.where(at == k, ref[k] * scale, out)
    return out


def advance(reads, writes, count, first_row, grid_rows, coef):
    lap_c, hyp_c, drift_c, up_c, low_c = coef
    layers = up_c.shape[0]

    def inside(j):
        at = first_row + j
        return jnp.where((at >= 0) & (at < grid_rows), 1.0, 0.0).astype(F32)

    def start(read):
        q0, q1, q2, q3 = read(0), read(1), read(2), read(3)
        left, right = shifted(q1)
        f1 = (q2 + q0 + left + right - 4.0 * q1) * inside(1)
        left, right = shifted(q2)
        f2 = (q3 + q1 + left + right - 4.0 * q2) * inside(2)
        return f1, f2, right - left

    def one(i, carry, read, write):
        f1, f2, side = carry
        q2, q3, q4 = read(i + 2), read(i + 3), read(i + 4)
        left, right = shifted(q3)
        f3 = (q4 + q2 + left + right - 4.0 * q3) * inside(i + 3)
        fl, fr = shifted(f2)
        out = (
            0.8 * q2
            + up_c * pltpu.roll(q2, layers - 1, axis=0)
            + low_c * pltpu.roll(q2, 1, axis=0)
            + lap_c * f2
            - hyp_c * (f1 + f3 + fl + fr)
            - drift_c * side
        )
        write(i, out * inside(i + 2))
        return f2, f3, right - left

    carries = [start(read) for read in reads]
    for i in range(count):
        for m in range(len(reads)):
            carries[m] = one(i, carries[m], reads[m], writes[m])


def cycle_kernel(
    sizes,
    fine_in,
    coarse_in,
    diff_in,
    hyper_in,
    drift_in,
    val_in,
    var_in,
    row_in,
    col_in,
    layer_in,
    count_in,
    pair_out,
    mean_out,
    diff_ref,
    hyper_ref,
    drift_ref,
    count_ref,
    val_ref,
    var_ref,
    row_ref,
    col_ref,
    layer_ref,
    xv,
    zv,
    fq,
    cq,
    ft1,
    ft2,
    ct1,
    ct2,
    cres,
    g,
    gn,
    ga,
    za,
    oc,
    rm,
    occ,
    rmc,
    sown,
    sx,
    ar0,
    ar1,
    kron_ref,
    inc,
    dg,
    dh,
    dl,
    mu,
    ob,
    mb,
    load_sem,
    small_sem,
    hs_sem,
    hr_sem,
    ss_sem,
    sr_sem,
    as_sem,
    ar_sem,
    ts_sem,
    tr_sem,
    os_sem,
    or_sem,
    own_sem,
):
    tiles, groups, pairs, levels, K, RF, RC, NC, NCC, stages = sizes
    tile = lax.axis_index("rows")
    me = lax.axis_index("mem")
    level_all, pair_all = levels * groups, pairs * groups
    E = level_all + pair_all
    nv, nvc = NC // LANES, NCC // LANES
    lch = levels // 2
    RQ, RQC = RF // groups, RC // groups
    s_f, s_c = math.sqrt(pair_all - 1), math.sqrt(level_all - 1)

    def at(row, mem):
        return (row, mem)

    def mem_peer(i):
        return lax.rem(me + i, groups)

    def stage_peer(stage, i):
        stride, size = stage
        mine = lax.rem(tile // stride, size)
        return tile + (lax.rem(mine + i, size) - mine) * stride

    up = lax.rem(tile + tiles - 1, tiles)
    down = lax.rem(tile + 1, tiles)

    loads = []
    for v in range(nvc):
        loads.append(pltpu.make_async_copy(coarse_in.at[:, pl.ds(v * LANES, LANES)], zv.at[v], load_sem.at[v]))
    for v in range(nv):
        loads.append(pltpu.make_async_copy(fine_in.at[:, pl.ds(v * LANES, LANES)], xv.at[v], load_sem.at[nvc + v]))
    for load in loads:
        load.start()
    smalls = [
        (diff_in, diff_ref),
        (hyper_in, hyper_ref),
        (drift_in, drift_ref),
        (count_in, count_ref),
        (val_in, val_ref),
        (var_in, var_ref),
        (row_in, row_ref),
        (col_in, col_ref),
        (layer_in, layer_ref),
    ]
    smalls = [pltpu.make_async_copy(a, b, small_sem.at[n]) for n, (a, b) in enumerate(smalls)]
    for small in smalls:
        small.start()

    targets = [(up, me), (down, me)]
    targets += [(tile, mem_peer(i)) for i in range(1, groups)]
    for stage in stages:
        targets += [(stage_peer(stage, i), me) for i in range(1, stage[1])]
    barrier = pltpu.get_barrier_semaphore()
    for target in targets:
        pl.semaphore_signal(barrier, inc=1, device_id=at(*target), device_id_type=MESH)

    for load in loads[:nvc]:
        load.wait()

    def columns_in(width):
        shape = (width, width)
        held = column_at(iota(shape, 1), width // LANES)
        return jnp.where(iota(shape, 0) == held, 1.0, 0.0).astype(BF16)

    order_c = columns_in(NCC)

    def place_level(ch, _):
        rows = []
        for m in range(2):
            for r in range(RC):
                first = (2 * ch + m) * K * RC + r
                rows.append(jnp.concatenate([zv[v, pl.ds(first, K, stride=RC), :] for v in range(nvc)], 1))
        placed = select_dot(jnp.concatenate(rows, 0), order_c).reshape(2, RC, K, NCC)
        for m in range(2):
            cq[2 * ch + m, HALO : HALO + RC] = placed[m]
        return 0

    lax.fori_loop(0, lch, place_level, 0)
    pl.semaphore_wait(barrier, len(targets))

    def halo_copy(ref, lead, src, dst, rows, number, way):
        return pltpu.make_async_remote_copy(
            src_ref=ref.at[lead, pl.ds(src, rows)],
            dst_ref=ref.at[lead, pl.ds(dst, rows)],
            send_sem=hs_sem.at[number, way],
            recv_sem=hr_sem.at[number, way],
            device_id=at(up if way == 0 else down, me),
            device_id_type=MESH,
        )

    def level_halo(ch, way):
        src, dst = ((HALO, HALO + RC), (RC, 0))[way]
        return halo_copy(cq, pl.ds(2 * ch, 2), src, dst, HALO, ch, way)

    def fine_halo(j, way):
        src, dst = ((HALO, HALO + RF), (RF, 0))[way]
        return halo_copy(fq, j, src, dst, HALO, lch + j, way)

    near = HALO // 2

    def pair_halo(j, way):
        src, dst = ((HALO + near, HALO + RC + near), (RC, 0))[way]
        return halo_copy(cq, levels + j, src, dst, HALO - near, lch + pairs + j, way)

    for ch in range(lch):
        for way in range(2):
            level_halo(ch, way).start()

    for load in loads[nvc:]:
        load.wait()

    order_f = columns_in(NC)

    def place_fine(m, _):
        rows = []
        for r in range(RF):
            first = m * K * RF + r
            rows.append(jnp.concatenate([xv[v, pl.ds(first, K, stride=RF), :] for v in range(nv)], 1))
        fq[m, HALO : HALO + RF] = select_dot(jnp.concatenate(rows, 0), order_f).reshape(RF, K, NC)
        restrict(m, HALO, HALO, RC)
        for way in range(2):
            fine_halo(m, way).start()
            pair_halo(m, way).start()
        return 0

    def restrict(m, fine_row, coarse_row, count):
        for r in range(count):
            both = fq[m, fine_row + 2 * r] + fq[m, fine_row + 2 * r + 1]
            cq[levels + m, coarse_row + r] = 0.25 * halved(both)

    lax.fori_loop(0, pairs, place_fine, 0)

    for small in smalls:
        small.wait()
    nb = 4
    per = val_ref.shape[0] * LANES // nb
    sub = per // LANES

    def row_of(ref, first, number):
        return jnp.concatenate([ref[i : i + 1, :] for i in range(first, first + number)], 1)

    for b in range(nb):
        col = row_of(col_ref, b * sub, sub)
        lay = row_of(layer_ref, b * sub, sub)
        loc = row_of(row_ref, b * sub, sub) - tile * RF
        oc[b] = jnp.where(iota((NC, per), 0) == place_of(col, nv), 1.0, 0.0).astype(BF16)
        occ[b] = jnp.where(iota((NCC, per), 0) == place_of(col >> 1, nvc), 1.0, 0.0).astype(BF16)
        rm[b] = jnp.where(iota((RF * K, per), 0) == loc * K + lay, 1.0, 0.0).astype(F32)
        rmc[b] = jnp.where(iota((RC * K, per), 0) == (loc >> 1) * K + lay, 1.0, 0.0).astype(F32)

    def coefs(scale_a, scale_h, scale_u, width):
        a = layer_vector(diff_ref, scale_a, K, width)
        h = layer_vector(hyper_ref, scale_h, K, width)
        u = layer_vector(drift_ref, scale_u, K, width)
        k = iota((K, width), 0)
        up_c = jnp.where(k < K - 1, 0.1, 0.0).astype(F32)
        low_c = jnp.where(k > 0, 0.1, 0.0).astype(F32)
        return a + 4.0 * h, h, 0.5 * u, up_c, low_c

    def zero_edges(clear_low, clear_high):
        @pl.when(tile == 0)
        def _():
            clear_low()

        @pl.when(tile == tiles - 1)
        def _():
            clear_high()

    coarse_coef = coefs(0.25, 0.0625, 0.5, NCC)
    row_c = tile * RC - HALO
    grid_c = tiles * RC

    def reader(ref, lead):
        return lambda j: ref[lead + (j,)]

    def writer(ref, lead):
        def write(i, value):
            ref[lead + (i,)] = value
        return write

    def coarse_steps(members):
        count = len(members)
        reads = [reader(cq, (m,)) for m in members]
        ones = [(ct1, (m,)) for m in range(count)]
        twos = [(ct2, (m,)) for m in range(count)]
        ends = [writer(cres, (m,)) for m in members]
        advance(reads, [writer(*x) for x in ones], RC + 8, row_c, grid_c, coarse_coef)
        advance([reader(*x) for x in ones], [writer(*x) for x in twos], RC + 4, row_c + 2, grid_c, coarse_coef)
        advance([reader(*x) for x in twos], ends, RC, row_c + 4, grid_c, coarse_coef)

    def level_chunk(ch, _):
        level_halo(ch, 0).wait_recv()
        level_halo(ch, 1).wait_recv()

        def clear(first):
            cq[pl.ds(2 * ch, 2), first : first + HALO] = jnp.zeros((2, HALO, K, NCC), F32)

        zero_edges(lambda: clear(0), lambda: clear(HALO + RC))
        coarse_steps([2 * ch, 2 * ch + 1])
        return 0

    lax.fori_loop(0, lch, level_chunk, 0)

    def level_send(i):
        peer = mem_peer(i)
        return pltpu.make_async_remote_copy(
            src_ref=cres.at[pl.ds(0, levels), pl.ds(peer * RQC, RQC)],
            dst_ref=za.at[me],
            send_sem=ts_sem.at[0, i - 1],
            recv_sem=tr_sem.at[0, i - 1],
            device_id=at(tile, peer),
            device_id_type=MESH,
        )

    def pair_send(i):
        peer = mem_peer(i)
        return pltpu.make_async_remote_copy(
            src_ref=gn.at[:, pl.ds(peer * RQ, RQ)],
            dst_ref=ga.at[me],
            send_sem=ts_sem.at[1, i - 1],
            recv_sem=tr_sem.at[1, i - 1],
            device_id=at(tile, peer),
            device_id_type=MESH,
        )

    for i in range(1, groups):
        level_send(i).start()

    fine_coef = coefs(1.0, 1.0, 1.0, NC)
    row_f = tile * RF - HALO
    grid_f = tiles * RF

    def fine_member(j, _):
        for way in range(2):
            fine_halo(j, way).wait_recv()
            pair_halo(j, way).wait_recv()

        def clear(first, first_c):
            fq[j, first : first + HALO] = jnp.zeros((HALO, K, NC), F32)
            cq[levels + j, first_c : first_c + HALO] = jnp.zeros((HALO, K, NCC), F32)

        restrict(j, 0, near, near)
        restrict(j, HALO + RF, HALO + RC, near)
        zero_edges(lambda: clear(0, 0), lambda: clear(HALO + RF, HALO + RC))
        coarse_steps([levels + j])

        def put_g(i, value):
            g[j, i] = value - doubled(cres[levels + j, i // 2])

        advance([reader(fq, (j,))], [writer(ft1, ())], RF + 8, row_f, grid_f, fine_coef)
        advance([reader(ft1, ())], [writer(ft2, ())], RF + 4, row_f + 2, grid_f, fine_coef)
        advance([reader(ft2, ())], [put_g], RF, row_f + 4, grid_f, fine_coef)
        return 0

    lax.fori_loop(0, pairs, fine_member, 0)

    def gather_block(pair, _):
        fs = []
        for part in range(2):
            b = 2 * pair + part
            high, low = halves(cres[0:levels].reshape(levels * RC * K, NCC))
            got = (dot(high, occ[b]) + dot(low, occ[b])).reshape(levels, RC * K, per)
            sown[b] = jnp.sum(got * rmc[b][None], axis=1)
            high, low = halves(g[...].reshape(pairs * RF * K, NC))
            got = (dot(high, oc[b]) + dot(low, oc[b])).reshape(pairs, RF * K, per)
            fs.append(jnp.sum(got * rm[b][None], axis=1))
        sown[nb + pair] = jnp.concatenate(fs, 0)
        return 0

    lax.fori_loop(0, nb // 2, gather_block, 0)

    def obs_send(i):
        return pltpu.make_async_remote_copy(
            src_ref=sown,
            dst_ref=sx.at[me],
            send_sem=ss_sem.at[i - 1],
            recv_sem=sr_sem.at[i - 1],
            device_id=at(tile, mem_peer(i)),
            device_id_type=MESH,
        )

    for i in range(1, groups):
        obs_send(i).start()
    sx[me] = sown[...]

    def order_pair(j, _):
        gn[j] = select_dot(g[j].reshape(RF * K, NC), columns_out(NC, 1)).reshape(RF, K, NC)
        return 0

    def columns_out(width, repeat):
        shape = (width, width * repeat)
        held = column_at(iota(shape, 0), width // LANES)
        return jnp.where(held == iota(shape, 1) // repeat, 1.0, 0.0).astype(BF16)

    lax.fori_loop(0, pairs, order_pair, 0)
    for i in range(1, groups):
        obs_send(i).wait_recv()
    for i in range(1, groups):
        pair_send(i).start()
    own_level = pltpu.make_async_copy(cres.at[pl.ds(0, levels), pl.ds(me * RQC, RQC)], za.at[me], own_sem.at[0])
    own_pair = pltpu.make_async_copy(gn.at[:, pl.ds(me * RQ, RQ)], ga.at[me], own_sem.at[1])
    own_level.start()
    own_pair.start()

    gram = jnp.zeros((E, E + 8), F32)
    for b in range(nb):
        z = jnp.concatenate([sx[x, b] for x in range(groups)], 0)
        first = (b % 2) * pairs
        f = jnp.concatenate([sx[x, nb + b // 2, first : first + pairs] for x in range(groups)], 0)
        z_mean = jnp.mean(z, axis=0, keepdims=True)
        f_mean = jnp.mean(f, axis=0, keepdims=True)
        s = jnp.concatenate([(z - z_mean) * (1.0 / s_c), (f - f_mean) * (1.0 / s_f)], 0)
        innov = row_of(val_ref, b * sub, sub) - (z_mean + f_mean)
        slot = iota((1, per), 1) + b * per
        weight = jnp.where(slot < count_ref[0], 1.0 / row_of(var_ref, b * sub, sub), 0.0)
        extra = jnp.where(iota((8, per), 0) == 0, weight * innov, 0.0)
        right = jnp.concatenate([s * weight, extra], 0)
        gram = gram + lax.dot_general(
            s, right, (((1,), (1,)), ((), ())), precision=HIGHEST, preferred_element_type=F32
        )
    half_e, half_l = E // 2, LANES // 2
    gram = jnp.concatenate([gram, jnp.zeros((E, LANES - E - 8), F32)], 1)
    gram = gram[:half_e] + pltpu.roll(gram[half_e:], half_l, axis=1)

    zk = level_all * K

    def level_anomalies():
        own_level.wait()
        for i in range(1, groups):
            level_send(i).wait_recv()

        widen = columns_out(NCC, 2)

        def one(rc, _):
            z = za[:, :, rc].reshape(level_all, K, NCC)
            z_mean = jnp.mean(z, axis=0)
            high, low = halves(((z - z_mean[None]) * (1.0 / s_c)).reshape(zk, NCC))
            high, low = dot(high, widen).astype(BF16), dot(low, widen).astype(BF16)
            wide_mean = select_dot(z_mean, widen)
            for half in range(2):
                dh[2 * rc + half, 0:zk] = high
                dl[2 * rc + half, 0:zk] = low
                mu[2 * rc + half] = wide_mean
            return 0

        lax.fori_loop(0, RQC, one, 0)

    slot0 = 0
    for s, stage in enumerate(stages):
        ar0[s] = gram
        sends = []
        for i in range(1, stage[1]):
            n = slot0 + i - 1
            send = pltpu.make_async_remote_copy(
                src_ref=ar0.at[s],
                dst_ref=ar1.at[n],
                send_sem=as_sem.at[n],
                recv_sem=ar_sem.at[n],
                device_id=at(stage_peer(stage, i), me),
                device_id_type=MESH,
            )
            send.start()
            sends.append((send, n))
        if s == 0:
            level_anomalies()
        for send, n in sends:
            send.wait_recv()
            gram = gram + ar1[n]
        for send, n in sends:
            send.wait_send()
        slot0 += stage[1] - 1

    rows_t = E + pair_all + 8
    lane = iota((rows_t, LANES), 1)
    eye = jnp.where(iota((E, LANES), 0) == iota((E, LANES), 1), 1.0, 0.0).astype(F32)
    full = jnp.concatenate([gram, pltpu.roll(gram, half_l, axis=1)], 0)
    rhs = jnp.sum(full[:, E : E + 1] * eye, axis=0, keepdims=True)
    full = jnp.where(iota((E, LANES), 1) < E, full, 0.0)
    rhs = jnp.where(iota((8, LANES), 0) == 0, rhs, 0.0)
    table = jnp.concatenate([full + eye, full[level_all:E], rhs], 0)
    width = 4
    for k in range(0, E, width):
        block = range(width)
        columns = [jnp.broadcast_to(table[:, k + i : k + i + 1], (rows_t, LANES)) for i in block]
        heads = [table[k + i : k + i + 1, :] for i in block]
        inv = [[columns[j][k + i : k + i + 1, :] for j in block] for i in block]
        for p in block:
            pivot = 1.0 / inv[p][p]
            scaled = [pivot if j == p else inv[p][j] * pivot for j in block]
            inv = [
                scaled
                if i == p
                else [
                    -inv[i][p] * pivot if j == p else inv[i][j] - inv[i][p] * scaled[j] for j in block
                ]
                for i in block
            ]
        ends = []
        for i in block:
            end = columns[0] * inv[0][i]
            for j in range(1, width):
                end = end + columns[j] * inv[j][i]
            ends.append(end)
        change = ends[0] * heads[0]
        for i in range(1, width):
            change = change + ends[i] * heads[i]
        table = table - change
        for i in block:
            table = jnp.where(lane == k + i, ends[i], table)
    solved = jnp.concatenate([-0.5 * table[E : E + pair_all], table[E + pair_all :]], 0)

    spread = jnp.where(iota((LANES, E * K), 1) // K == iota((LANES, E * K), 0), 1.0, 0.0).astype(BF16)
    same = jnp.where(lax.rem(iota((K, E * K), 1), K) == iota((K, E * K), 0), 1.0, 0.0).astype(F32)
    coef_h, coef_l = halves(solved)

    def kron(part):
        wide = dot(part, spread)
        blocks = [wide[m : m + 1, :] * same for m in range(pair_all + 2)]
        return jnp.concatenate(blocks, 0).astype(BF16)

    kron_rows = kron_ref.shape[0] // 2
    kron_ref[0:kron_rows] = kron(coef_h)
    kron_ref[kron_rows:] = kron(coef_l)

    own_pair.wait()
    for i in range(1, groups):
        pair_send(i).wait_recv()

    def pair_anomalies(r, _):
        f = ga[:, :, r].reshape(pair_all, K, NC)
        f_mean = jnp.mean(f, axis=0)
        mu[r] = mu[r] + f_mean
        anom = ((f - f_mean[None]) * (1.0 / s_f)).reshape(pair_all * K, NC)
        dg[r] = anom
        high, low = halves(anom)
        dh[r, zk:] = high
        dl[r, zk:] = low
        return 0

    lax.fori_loop(0, RQ, pair_anomalies, 0)

    def result_send(r, i):
        peer = mem_peer(i)
        pair_copy = pltpu.make_async_remote_copy(
            src_ref=ob.at[pl.ds(peer * pairs, pairs), r],
            dst_ref=pair_out.at[:, me * RQ + r],
            send_sem=os_sem.at[0, r, i - 1],
            recv_sem=or_sem.at[0, r, i - 1],
            device_id=at(tile, peer),
            device_id_type=MESH,
        )
        mean_copy = pltpu.make_async_remote_copy(
            src_ref=mb.at[r],
            dst_ref=mean_out.at[me * RQ + r],
            send_sem=os_sem.at[1, r, i - 1],
            recv_sem=or_sem.at[1, r, i - 1],
            device_id=at(tile, peer),
            device_id_type=MESH,
        )
        return pair_copy, mean_copy

    np8 = pair_all * K

    def update(r, _):
        inc[...] = dot(kron_ref[...], dh[r])
        more = dot(kron_ref[0:kron_rows], dl[r])
        total = inc[0:kron_rows] + inc[kron_rows:] + more
        ob[:, r] = (s_f * (dg[r] + total[:np8])).reshape(pair_all, K, NC)
        mb[r] = mu[r] + total[np8 : np8 + K]
        for i in range(1, groups):
            for copy in result_send(r, i):
                copy.start()
        return 0

    lax.fori_loop(0, RQ, update, 0)
    own_out = pltpu.make_async_copy(ob.at[pl.ds(me * pairs, pairs)], pair_out.at[:, pl.ds(me * RQ, RQ)], own_sem.at[2])
    own_mean = pltpu.make_async_copy(mb, mean_out.at[pl.ds(me * RQ, RQ)], own_sem.at[3])
    own_out.start()
    own_mean.start()

    for way in range(2):
        for ch in range(lch):
            level_halo(ch, way).wait_send()
        for j in range(pairs):
            fine_halo(j, way).wait_send()
            pair_halo(j, way).wait_send()
    for i in range(1, groups):
        level_send(i).wait_send()
        pair_send(i).wait_send()
        obs_send(i).wait_send()
    own_out.wait()
    own_mean.wait()
    for r in range(RQ):
        for i in range(1, groups):
            for copy in result_send(r, i):
                copy.wait_recv()
                copy.wait_send()


def order_kernel(K, RF, pair_in, mean_in, pair_out, mean_out, pv, mv, sem):
    nv = pv.shape[0]
    pairs = pair_in.shape[0]

    def put(value, ref, first, r):
        for v in range(nv):
            ref[v, pl.ds(first + r, K, stride=RF), :] = value[:, v * LANES : (v + 1) * LANES]

    copies = []

    def send(ref, first, out, row):
        for v in range(nv):
            copy = pltpu.make_async_copy(
                ref.at[v, pl.ds(first, K * RF)],
                out.at[pl.ds(first, K * RF), pl.ds(v * LANES, LANES)],
                sem.at[row, v],
            )
            copy.start()
            copies.append(copy)

    for m in range(pairs):
        for r in range(RF):
            put(pair_in[m, r], pv, m * K * RF, r)
        send(pv, m * K * RF, pair_out, m)
    for r in range(RF):
        put(mean_in[r], mv, 0, r)
    send(mv, 0, mean_out, pairs)
    for copy in copies:
        copy.wait()


def axis_stages(tiles):
    stages, stride = [], 1
    for size in (2, 4, 4):
        if stride < tiles:
            stages.append((stride, size))
            stride *= size
    return tuple(stages)


def per_device(
    fine_members,
    coarse_members,
    diffusion,
    hyper,
    drift,
    obs_value,
    obs_var,
    obs_row,
    obs_col,
    obs_layer,
    obs_count,
):
    tiles = lax.axis_size("rows")
    groups = lax.axis_size("mem")
    pairs, K, RF, NC = fine_members.shape
    levels, _, RC, NCC = coarse_members.shape
    stages = axis_stages(tiles)
    sizes = (tiles, groups, pairs, levels, K, RF, RC, NC, NCC, stages)
    slots = obs_value.shape[0]
    E = (pairs + levels) * groups
    nb = 4
    per = slots // nb
    RQ, RQC = RF // groups, RC // groups
    chunks = levels // 2 + 2 * pairs
    peers = sum(size - 1 for _, size in stages)
    nv, nvc = NC // LANES, NCC // LANES
    anyspace = pl.BlockSpec(memory_space=pl.ANY)
    hbm = pl.BlockSpec(memory_space=pltpu.HBM)
    vmem = pl.BlockSpec(memory_space=pltpu.VMEM)
    dma = pltpu.SemaphoreType.DMA

    def flat(obs):
        return obs.reshape(slots // LANES, LANES)

    def keep(array):
        return pltpu.with_memory_space_constraint(array, pltpu.HBM)

    pair_rows, mean_rows = pl.pallas_call(
        functools.partial(cycle_kernel, sizes),
        out_shape=(
            jax.ShapeDtypeStruct((pairs, RF, K, NC), F32),
            jax.ShapeDtypeStruct((RF, K, NC), F32),
        ),
        in_specs=[hbm] * 11,
        out_specs=(anyspace, anyspace),
        scratch_shapes=[
            pltpu.SMEM((K,), F32),
            pltpu.SMEM((K,), F32),
            pltpu.SMEM((K,), F32),
            pltpu.SMEM((1,), jnp.int32),
            pltpu.VMEM((slots // LANES, LANES), F32),
            pltpu.VMEM((slots // LANES, LANES), F32),
            pltpu.VMEM((slots // LANES, LANES), jnp.int32),
            pltpu.VMEM((slots // LANES, LANES), jnp.int32),
            pltpu.VMEM((slots // LANES, LANES), jnp.int32),
            pltpu.VMEM((nv, pairs * K * RF, LANES), F32),
            pltpu.VMEM((nvc, levels * K * RC, LANES), F32),
            pltpu.VMEM((pairs, RF + 2 * HALO, K, NC), F32),
            pltpu.VMEM((levels + pairs, RC + 2 * HALO, K, NCC), F32),
            pltpu.VMEM((RF + 8, K, NC), F32),
            pltpu.VMEM((RF + 4, K, NC), F32),
            pltpu.VMEM((2, RC + 8, K, NCC), F32),
            pltpu.VMEM((2, RC + 4, K, NCC), F32),
            pltpu.VMEM((levels + pairs, RC, K, NCC), F32),
            pltpu.VMEM((pairs, RF, K, NC), F32),
            pltpu.VMEM((pairs, RF, K, NC), F32),
            pltpu.VMEM((groups, pairs, RQ, K, NC), F32),
            pltpu.VMEM((groups, levels, RQC, K, NCC), F32),
            pltpu.VMEM((nb, NC, per), BF16),
            pltpu.VMEM((nb, RF * K, per), F32),
            pltpu.VMEM((nb, NCC, per), BF16),
            pltpu.VMEM((nb, RC * K, per), F32),
            pltpu.VMEM((nb + nb // 2, levels, per), F32),
            pltpu.VMEM((groups, nb + nb // 2, levels, per), F32),
            pltpu.VMEM((len(stages), E // 2, LANES), F32),
            pltpu.VMEM((peers, E // 2, LANES), F32),
            pltpu.VMEM((2 * (pairs * groups + 2) * K, E * K), BF16),
            pltpu.VMEM((2 * (pairs * groups + 2) * K, NC), F32),
            pltpu.VMEM((RQ, pairs * groups * K, NC), F32),
            pltpu.VMEM((RQ, E * K, NC), BF16),
            pltpu.VMEM((RQ, E * K, NC), BF16),
            pltpu.VMEM((RQ, K, NC), F32),
            pltpu.VMEM((pairs * groups, RQ, K, NC), F32),
            pltpu.VMEM((RQ, K, NC), F32),
            dma((nv + nvc,)),
            dma((9,)),
            dma((chunks, 2)),
            dma((chunks, 2)),
            dma((groups - 1,)),
            dma((groups - 1,)),
            dma((peers,)),
            dma((peers,)),
            dma((2, groups - 1)),
            dma((2, groups - 1)),
            dma((2, RQ, groups - 1)),
            dma((2, RQ, groups - 1)),
            dma((4,)),
        ],
        compiler_params=pltpu.CompilerParams(
            collective_id=0, has_side_effects=True, vmem_limit_bytes=48 * 1024 * 1024
        ),
        name="cycle",
    )(
        keep(fine_members.reshape(pairs * K * RF, NC)),
        keep(coarse_members.reshape(levels * K * RC, NCC)),
        keep(diffusion),
        keep(hyper),
        keep(drift),
        keep(flat(obs_value)),
        keep(flat(obs_var)),
        keep(flat(obs_row)),
        keep(flat(obs_col)),
        keep(flat(obs_layer)),
        obs_count,
    )
    pair, mean = pl.pallas_call(
        functools.partial(order_kernel, K, RF),
        out_shape=(
            jax.ShapeDtypeStruct((pairs * K * RF, NC), F32),
            jax.ShapeDtypeStruct((K * RF, NC), F32),
        ),
        in_specs=[vmem, vmem],
        out_specs=(anyspace, anyspace),
        scratch_shapes=[
            pltpu.VMEM((nv, pairs * K * RF, LANES), F32),
            pltpu.VMEM((nv, K * RF, LANES), F32),
            dma((pairs + 1, nv)),
        ],
        compiler_params=pltpu.CompilerParams(vmem_limit_bytes=16 * 1024 * 1024),
        name="order",
    )(pair_rows, mean_rows)
    return mean.reshape(K, RF, NC), pair.reshape(pairs, K, RF, NC)


def solution(mesh):
    in_specs = (
        P("mem", None, "rows", None),
        P("mem", None, "rows", None),
        P(),
        P(),
        P(),
        P("rows"),
        P("rows"),
        P("rows"),
        P("rows"),
        P("rows"),
        P("rows"),
    )
    out_specs = (P(None, "rows", None), P("mem", None, "rows", None))
    return jax.shard_map(
        per_device, mesh=mesh, in_specs=in_specs, out_specs=out_specs, check_vma=False
    )
```

```python
import functools
import itertools
import math

import jax
import jax.numpy as jnp
from jax import lax
from jax.experimental import pallas as pl
from jax.experimental.pallas import tpu as pltpu
from jax.sharding import PartitionSpec as P

STEPS = 3
EARLY = 4
HALO = 2 * STEPS
LANES = 128
MESH = pl.DeviceIdType.MESH
HIGHEST = lax.Precision.HIGHEST
F32 = jnp.float32
BF16 = jnp.bfloat16


def iota(shape, axis):
    return lax.broadcasted_iota(jnp.int32, shape, axis)


def halves(value):
    high = value.astype(BF16)
    return high, (value - high.astype(F32)).astype(BF16)


def dot(left, right):
    return jnp.dot(left, right, preferred_element_type=F32)


def select_dot(left, right):
    rows = left.shape[0]
    high = left.astype(BF16)
    rest = left - high.astype(F32)
    mid = rest.astype(BF16)
    low = (rest - mid.astype(F32)).astype(BF16)
    out = dot(jnp.concatenate([high, mid, low], 0), right)
    return out[:rows] + (out[rows : 2 * rows] + out[2 * rows :])


def column_at(place, parts):
    return (place % LANES) * parts + place // LANES


def place_of(column, parts):
    shift = parts.bit_length() - 1
    return (column & (parts - 1)) * LANES + (column >> shift)


def shifted(row):
    width = row.shape[-1]
    first, last = row[:, :LANES], row[:, width - LANES :]
    left = jnp.concatenate([pltpu.roll(last, 1, axis=1), row[:, : width - LANES]], 1)
    right = jnp.concatenate([row[:, LANES:], pltpu.roll(first, LANES - 1, axis=1)], 1)
    return left, right


def halved(row):
    tiles = [row[:, i * LANES : (i + 1) * LANES] for i in range(row.shape[1] // LANES)]
    return jnp.concatenate([a + b for a, b in zip(tiles[::2], tiles[1::2])], 1)


def doubled(row):
    tiles = [row[:, i * LANES : (i + 1) * LANES] for i in range(row.shape[1] // LANES)]
    return jnp.concatenate([tile for tile in tiles for _ in range(2)], 1)


def layer_vector(ref, scale, layers, width):
    at = iota((layers, width), 0)
    out = jnp.zeros((layers, width), F32)
    for k in range(layers):
        out = jnp.where(at == k, ref[k] * scale, out)
    return out


def advance(reads, writes, count, first_row, grid_rows, own, coef):
    lap_c, hyp_c, drift_c, up_c, low_c = coef
    layers = up_c.shape[0]
    beside = (count + 4 - own) // 2

    def inside(j, value):
        if beside <= j < beside + own:
            return value
        at = first_row + j
        return value * jnp.where((at >= 0) & (at < grid_rows), 1.0, 0.0).astype(F32)

    def start(read):
        q0, q1, q2, q3 = read(0), read(1), read(2), read(3)
        left, right = shifted(q1)
        f1 = inside(1, q2 + q0 + left + right - 4.0 * q1)
        left, right = shifted(q2)
        f2 = inside(2, q3 + q1 + left + right - 4.0 * q2)
        return f1, f2, right - left

    def one(i, carry, read, write):
        f1, f2, side = carry
        q2, q3, q4 = read(i + 2), read(i + 3), read(i + 4)
        left, right = shifted(q3)
        f3 = inside(i + 3, q4 + q2 + left + right - 4.0 * q3)
        fl, fr = shifted(f2)
        out = (
            0.8 * q2
            + up_c * pltpu.roll(q2, layers - 1, axis=0)
            + low_c * pltpu.roll(q2, 1, axis=0)
            + lap_c * f2
            - hyp_c * (f1 + f3 + fl + fr)
            - drift_c * side
        )
        write(i, inside(i + 2, out))
        return f2, f3, right - left

    carries = [start(read) for read in reads]
    for i in range(count):
        for m in range(len(reads)):
            carries[m] = one(i, carries[m], reads[m], writes[m])


def cycle_kernel(
    sizes,
    fine_in,
    coarse_in,
    diff_in,
    hyper_in,
    drift_in,
    val_in,
    var_in,
    row_in,
    col_in,
    layer_in,
    count_in,
    pair_out,
    mean_out,
    diff_ref,
    hyper_ref,
    drift_ref,
    count_ref,
    val_ref,
    var_ref,
    row_ref,
    col_ref,
    layer_ref,
    xv,
    zv,
    fq,
    cq,
    ft1,
    ft2,
    ct1,
    ct2,
    cres,
    g,
    ga,
    za,
    oc,
    rm,
    occ,
    rmc,
    sown,
    sx,
    ar0,
    ar1,
    kron_ref,
    inc,
    dg,
    dh,
    dl,
    mu,
    ob,
    mb,
    load_sem,
    small_sem,
    hs_sem,
    hr_sem,
    ss_sem,
    sr_sem,
    as_sem,
    ar_sem,
    ts_sem,
    tr_sem,
    os_sem,
    or_sem,
    own_sem,
):
    tiles, groups, pairs, levels, K, RF, RC, NC, NCC, stages = sizes
    tile = lax.axis_index("rows")
    me = lax.axis_index("mem")
    level_all, pair_all = levels * groups, pairs * groups
    E = level_all + pair_all
    nv, nvc = NC // LANES, NCC // LANES
    lch = levels // 2
    RQ, RQC = RF // groups, RC // groups
    s_f, s_c = math.sqrt(pair_all - 1), math.sqrt(level_all - 1)

    def at(row, mem):
        return (row, mem)

    def mem_peer(i):
        return lax.rem(me + i, groups)

    def stage_peers(stage):
        peers = []
        for offsets in itertools.product(*[range(size) for _, size in stage]):
            if any(offsets):
                peer = tile
                for offset, (stride, size) in zip(offsets, stage):
                    mine = lax.rem(tile // stride, size)
                    peer = peer + (lax.rem(mine + offset, size) - mine) * stride
                peers.append(peer)
        return peers

    up = lax.rem(tile + tiles - 1, tiles)
    down = lax.rem(tile + 1, tiles)

    loads = []
    for v in range(nv):
        loads.append(pltpu.make_async_copy(fine_in.at[:, pl.ds(v * LANES, LANES)], xv.at[v], load_sem.at[v]))
    for v in range(nvc):
        loads.append(pltpu.make_async_copy(coarse_in.at[:, pl.ds(v * LANES, LANES)], zv.at[v], load_sem.at[nv + v]))
    for load in loads:
        load.start()
    smalls = [
        (diff_in, diff_ref),
        (hyper_in, hyper_ref),
        (drift_in, drift_ref),
        (count_in, count_ref),
        (val_in, val_ref),
        (var_in, var_ref),
        (row_in, row_ref),
        (col_in, col_ref),
        (layer_in, layer_ref),
    ]
    smalls = [pltpu.make_async_copy(a, b, small_sem.at[n]) for n, (a, b) in enumerate(smalls)]
    for small in smalls:
        small.start()

    targets = [(up, me), (down, me)]
    targets += [(tile, mem_peer(i)) for i in range(1, groups)]
    for stage in stages:
        targets += [(peer, me) for peer in stage_peers(stage)]
    barrier = pltpu.get_barrier_semaphore()
    for target in targets:
        pl.semaphore_signal(barrier, inc=1, device_id=at(*target), device_id_type=MESH)

    def columns_in(width):
        shape = (width, width)
        held = column_at(iota(shape, 1), width // LANES)
        return jnp.where(iota(shape, 0) == held, 1.0, 0.0).astype(BF16)

    def halo_copy(ref, lead, src, dst, rows, number, way):
        return pltpu.make_async_remote_copy(
            src_ref=ref.at[lead, pl.ds(src, rows)],
            dst_ref=ref.at[lead, pl.ds(dst, rows)],
            send_sem=hs_sem.at[number, way],
            recv_sem=hr_sem.at[number, way],
            device_id=at(up if way == 0 else down, me),
            device_id_type=MESH,
        )

    def level_halo(ch, way):
        src, dst = ((HALO, HALO + RC), (RC, 0))[way]
        return halo_copy(cq, pl.ds(2 * ch, 2), src, dst, HALO, ch, way)

    def fine_halo(j, way):
        src, dst = ((HALO, HALO + RF), (RF, 0))[way]
        return halo_copy(fq, j, src, dst, HALO, lch + j, way)

    near = HALO // 2

    def pair_halo(j, way):
        src, dst = ((HALO + near, HALO + RC + near), (RC, 0))[way]
        return halo_copy(cq, levels + j, src, dst, HALO - near, lch + pairs + j, way)

    order_f = columns_in(NC)

    def place_fine(m):
        rows = []
        for r in range(RF):
            first = m * K * RF + r
            rows.append(jnp.concatenate([xv[v, pl.ds(first, K, stride=RF), :] for v in range(nv)], 1))
        fq[m, HALO : HALO + RF] = select_dot(jnp.concatenate(rows, 0), order_f).reshape(RF, K, NC)
        restrict(m, HALO, HALO, RC)

    def send_fine(m):
        for way in range(2):
            fine_halo(m, way).start()
            pair_halo(m, way).start()

    def restrict(m, fine_row, coarse_row, count):
        for r in range(count):
            both = fq[m, fine_row + 2 * r] + fq[m, fine_row + 2 * r + 1]
            cq[levels + m, coarse_row + r] = 0.25 * halved(both)

    def place_and_send(m, _):
        place_fine(m)
        send_fine(m)
        return 0

    for load in loads[:nv]:
        load.wait()
    place_fine(0)
    pl.semaphore_wait(barrier, len(targets))
    send_fine(0)
    lax.fori_loop(1, pairs, place_and_send, 0)

    for load in loads[nv:]:
        load.wait()
    order_c = columns_in(NCC)

    def place_level(ch, _):
        rows = []
        for m in range(2):
            for r in range(RC):
                first = (2 * ch + m) * K * RC + r
                rows.append(jnp.concatenate([zv[v, pl.ds(first, K, stride=RC), :] for v in range(nvc)], 1))
        placed = select_dot(jnp.concatenate(rows, 0), order_c).reshape(2, RC, K, NCC)
        for m in range(2):
            cq[2 * ch + m, HALO : HALO + RC] = placed[m]
        for way in range(2):
            level_halo(ch, way).start()
        return 0

    lax.fori_loop(0, lch, place_level, 0)

    for small in smalls:
        small.wait()
    nb = 4
    per = val_ref.shape[0] * LANES // nb
    sub = per // LANES

    def row_of(ref, first, number):
        return jnp.concatenate([ref[i : i + 1, :] for i in range(first, first + number)], 1)

    for b in range(nb):
        col = row_of(col_ref, b * sub, sub)
        lay = row_of(layer_ref, b * sub, sub)
        loc = row_of(row_ref, b * sub, sub) - tile * RF
        oc[b] = jnp.where(iota((NC, per), 0) == place_of(col, nv), 1.0, 0.0).astype(BF16)
        occ[b] = jnp.where(iota((NCC, per), 0) == place_of(col >> 1, nvc), 1.0, 0.0).astype(BF16)
        rm[b] = jnp.where(iota((RF * K, per), 0) == loc * K + lay, 1.0, 0.0).astype(F32)
        rmc[b] = jnp.where(iota((RC * K, per), 0) == (loc >> 1) * K + lay, 1.0, 0.0).astype(F32)

    def coefs(scale_a, scale_h, scale_u, width):
        a = layer_vector(diff_ref, scale_a, K, width)
        h = layer_vector(hyper_ref, scale_h, K, width)
        u = layer_vector(drift_ref, scale_u, K, width)
        k = iota((K, width), 0)
        up_c = jnp.where(k < K - 1, 0.1, 0.0).astype(F32)
        low_c = jnp.where(k > 0, 0.1, 0.0).astype(F32)
        return a + 4.0 * h, h, 0.5 * u, up_c, low_c

    def zero_edges(clear_low, clear_high):
        @pl.when(tile == 0)
        def _():
            clear_low()

        @pl.when(tile == tiles - 1)
        def _():
            clear_high()

    coarse_coef = coefs(0.25, 0.0625, 0.5, NCC)
    row_c = tile * RC - HALO
    grid_c = tiles * RC

    def reader(ref, lead):
        return lambda j: ref[lead + (j,)]

    def writer(ref, lead):
        def write(i, value):
            ref[lead + (i,)] = value
        return write

    def coarse_steps(members):
        count = len(members)
        reads = [reader(cq, (m,)) for m in members]
        ones = [(ct1, (m,)) for m in range(count)]
        twos = [(ct2, (m,)) for m in range(count)]
        ends = [writer(cres, (m,)) for m in members]
        advance(reads, [writer(*x) for x in ones], RC + 8, row_c, grid_c, RC, coarse_coef)
        advance([reader(*x) for x in ones], [writer(*x) for x in twos], RC + 4, row_c + 2, grid_c, RC, coarse_coef)
        advance([reader(*x) for x in twos], ends, RC, row_c + 4, grid_c, RC, coarse_coef)

    def level_send(ch, i):
        peer = mem_peer(i)
        return pltpu.make_async_remote_copy(
            src_ref=cres.at[pl.ds(2 * ch, 2), pl.ds(peer * RQC, RQC)],
            dst_ref=za.at[me, pl.ds(2 * ch, 2)],
            send_sem=ts_sem.at[ch, i - 1],
            recv_sem=tr_sem.at[ch, i - 1],
            device_id=at(tile, peer),
            device_id_type=MESH,
        )

    def pair_send(j, i):
        peer = mem_peer(i)
        return pltpu.make_async_remote_copy(
            src_ref=g.at[j, pl.ds(peer * RQ, RQ)],
            dst_ref=ga.at[me, j],
            send_sem=ts_sem.at[lch + j, i - 1],
            recv_sem=tr_sem.at[lch + j, i - 1],
            device_id=at(tile, peer),
            device_id_type=MESH,
        )

    def level_chunk(ch, _):
        level_halo(ch, 0).wait_recv()
        level_halo(ch, 1).wait_recv()

        def clear(first):
            cq[pl.ds(2 * ch, 2), first : first + HALO] = jnp.zeros((2, HALO, K, NCC), F32)

        zero_edges(lambda: clear(0), lambda: clear(HALO + RC))
        coarse_steps([2 * ch, 2 * ch + 1])
        return 0

    def gather(values, columns, rows, number):
        high, low = halves(values)
        got = dot(high, columns) + dot(low, columns)
        return jnp.sum(got.reshape((number,) + rows.shape) * rows[None], axis=1)

    def level_gather(b, _):
        sown[b] = gather(cres[0:levels].reshape(levels * RC * K, NCC), occ[b], rmc[b], levels)
        return 0

    def pair_gather(half, _):
        fs = [gather(g[...].reshape(pairs * RF * K, NC), oc[2 * half + b], rm[2 * half + b], pairs) for b in range(2)]
        sown[nb + half] = jnp.concatenate(fs, 0)
        return 0

    def obs_send(part, i):
        span = (pl.ds(nb, nb // 2), pl.ds(0, nb))[part]
        return pltpu.make_async_remote_copy(
            src_ref=sown.at[span],
            dst_ref=sx.at[me, span],
            send_sem=ss_sem.at[part, i - 1],
            recv_sem=sr_sem.at[part, i - 1],
            device_id=at(tile, mem_peer(i)),
            device_id_type=MESH,
        )

    fine_coef = coefs(1.0, 1.0, 1.0, NC)
    row_f = tile * RF - HALO
    grid_f = tiles * RF

    def fine_member(j, _):
        for way in range(2):
            fine_halo(j, way).wait_recv()
            pair_halo(j, way).wait_recv()

        def clear(first, first_c):
            fq[j, first : first + HALO] = jnp.zeros((HALO, K, NC), F32)
            cq[levels + j, first_c : first_c + HALO] = jnp.zeros((HALO, K, NCC), F32)

        restrict(j, 0, near, near)
        restrict(j, HALO + RF, HALO + RC, near)
        zero_edges(lambda: clear(0, 0), lambda: clear(HALO + RF, HALO + RC))
        coarse_steps([levels + j])

        def put_g(i, value):
            g[j, i] = value - doubled(cres[levels + j, i // 2])

        advance([reader(fq, (j,))], [writer(ft1, ())], RF + 8, row_f, grid_f, RF, fine_coef)
        advance([reader(ft1, ())], [writer(ft2, ())], RF + 4, row_f + 2, grid_f, RF, fine_coef)
        advance([reader(ft2, ())], [put_g], RF, row_f + 4, grid_f, RF, fine_coef)

        @pl.when(j < EARLY)
        def _():
            for i in range(1, groups):
                pair_send(j, i).start()

        return 0

    lax.fori_loop(0, pairs, fine_member, 0)

    lax.fori_loop(0, nb // 2, pair_gather, 0)
    for i in range(1, groups):
        obs_send(0, i).start()

    lax.fori_loop(0, lch, level_chunk, 0)
    lax.fori_loop(0, nb, level_gather, 0)
    for i in range(1, groups):
        obs_send(1, i).start()
    sx[me] = sown[...]
    for i in range(1, groups):
        obs_send(0, i).wait_recv()
        obs_send(1, i).wait_recv()
    for j in range(EARLY, pairs):
        for i in range(1, groups):
            pair_send(j, i).start()
    for ch in range(lch):
        for i in range(1, groups):
            level_send(ch, i).start()
    own_level = pltpu.make_async_copy(cres.at[pl.ds(0, levels), pl.ds(me * RQC, RQC)], za.at[me], own_sem.at[0])
    own_pair = pltpu.make_async_copy(g.at[:, pl.ds(me * RQ, RQ)], ga.at[me], own_sem.at[1])
    own_level.start()
    own_pair.start()

    gram = jnp.zeros((E, E + 8), F32)
    for b in range(nb):
        z = jnp.concatenate([sx[x, b] for x in range(groups)], 0)
        first = (b % 2) * pairs
        f = jnp.concatenate([sx[x, nb + b // 2, first : first + pairs] for x in range(groups)], 0)
        z_mean = jnp.mean(z, axis=0, keepdims=True)
        f_mean = jnp.mean(f, axis=0, keepdims=True)
        s = jnp.concatenate([(z - z_mean) * (1.0 / s_c), (f - f_mean) * (1.0 / s_f)], 0)
        innov = row_of(val_ref, b * sub, sub) - (z_mean + f_mean)
        slot = iota((1, per), 1) + b * per
        weight = jnp.where(slot < count_ref[0], 1.0 / row_of(var_ref, b * sub, sub), 0.0)
        extra = jnp.where(iota((8, per), 0) == 0, weight * innov, 0.0)
        right = jnp.concatenate([s * weight, extra], 0)
        gram = gram + lax.dot_general(
            s, right, (((1,), (1,)), ((), ())), precision=HIGHEST, preferred_element_type=F32
        )
    half_e, half_l = E // 2, LANES // 2
    gram = jnp.concatenate([gram, jnp.zeros((E, LANES - E - 8), F32)], 1)
    gram = gram[:half_e] + pltpu.roll(gram[half_e:], half_l, axis=1)

    zk = level_all * K

    def level_anomalies():
        own_level.wait()
        for ch in range(lch):
            for i in range(1, groups):
                level_send(ch, i).wait_recv()

        widen = columns_out(NCC, 2)

        def one(rc, _):
            z = za[:, :, rc].reshape(level_all, K, NCC)
            z_mean = jnp.mean(z, axis=0)
            high, low = halves(((z - z_mean[None]) * (1.0 / s_c)).reshape(zk, NCC))
            high, low = dot(high, widen).astype(BF16), dot(low, widen).astype(BF16)
            wide_mean = select_dot(z_mean, widen)
            for half in range(2):
                dh[2 * rc + half, 0:zk] = high
                dl[2 * rc + half, 0:zk] = low
                mu[2 * rc + half] = mu[2 * rc + half] + wide_mean
            return 0

        lax.fori_loop(0, RQC, one, 0)

    def columns_out(width, repeat):
        shape = (width, width * repeat)
        held = column_at(iota(shape, 0), width // LANES)
        return jnp.where(held == iota(shape, 1) // repeat, 1.0, 0.0).astype(BF16)

    def pair_anomalies():
        own_pair.wait()
        for j in range(pairs):
            for i in range(1, groups):
                pair_send(j, i).wait_recv()
        natural = columns_out(NC, 1)

        def one(r, _):
            f = ga[:, :, r].reshape(pair_all, K, NC)
            f_mean = jnp.mean(f, axis=0)
            mu[r] = select_dot(f_mean, natural)
            anom = ((f - f_mean[None]) * (1.0 / s_f)).reshape(pair_all * K, NC)
            high = anom.astype(BF16)
            rest = anom - high.astype(F32)
            mid = rest.astype(BF16)
            low = (rest - mid.astype(F32)).astype(BF16)
            high, mid, low = dot(high, natural), dot(mid, natural), dot(low, natural)
            dg[r] = high + (mid + low)
            dh[r, zk:] = high.astype(BF16)
            dl[r, zk:] = mid.astype(BF16)
            return 0

        lax.fori_loop(0, RQ, one, 0)

    slot0 = 0
    for s, stage in enumerate(stages):
        ar0[s] = gram
        sends = []
        for n, peer in enumerate(stage_peers(stage), slot0):
            send = pltpu.make_async_remote_copy(
                src_ref=ar0.at[s],
                dst_ref=ar1.at[n],
                send_sem=as_sem.at[n],
                recv_sem=ar_sem.at[n],
                device_id=at(peer, me),
                device_id_type=MESH,
            )
            send.start()
            sends.append((send, n))
        if s == 0:
            pair_anomalies()
        if s == len(stages) - 1:
            level_anomalies()
        for send, n in sends:
            send.wait_recv()
            gram = gram + ar1[n]
        for send, n in sends:
            send.wait_send()
        slot0 += len(sends)

    rows_t = E + pair_all + 8
    lane = iota((rows_t, LANES), 1)
    eye = jnp.where(iota((E, LANES), 0) == iota((E, LANES), 1), 1.0, 0.0).astype(F32)
    full = jnp.concatenate([gram, pltpu.roll(gram, half_l, axis=1)], 0)
    rhs = jnp.sum(full[:, E : E + 1] * eye, axis=0, keepdims=True)
    full = jnp.where(iota((E, LANES), 1) < E, full, 0.0)
    rhs = jnp.where(iota((8, LANES), 0) == 0, rhs, 0.0)
    table = jnp.concatenate([full + eye, full[level_all:E], rhs], 0)
    width = 4
    for k in range(0, E, width):
        block = range(width)
        columns = [jnp.broadcast_to(table[:, k + i : k + i + 1], (rows_t, LANES)) for i in block]
        heads = [table[k + i : k + i + 1, :] for i in block]
        inv = [[columns[j][k + i : k + i + 1, :] for j in block] for i in block]
        for p in block:
            pivot = 1.0 / inv[p][p]
            scaled = [pivot if j == p else inv[p][j] * pivot for j in block]
            inv = [
                scaled
                if i == p
                else [
                    -inv[i][p] * pivot if j == p else inv[i][j] - inv[i][p] * scaled[j] for j in block
                ]
                for i in block
            ]
        ends = []
        for i in block:
            end = columns[0] * inv[0][i]
            for j in range(1, width):
                end = end + columns[j] * inv[j][i]
            ends.append(end)
        change = ends[0] * heads[0]
        for i in range(1, width):
            change = change + ends[i] * heads[i]
        table = table - change
        for i in block:
            table = jnp.where(lane == k + i, ends[i], table)
    solved = jnp.concatenate([-0.5 * table[E : E + pair_all], table[E + pair_all :]], 0)

    spread = jnp.where(iota((LANES, E * K), 1) // K == iota((LANES, E * K), 0), 1.0, 0.0).astype(BF16)
    same = jnp.where(lax.rem(iota((K, E * K), 1), K) == iota((K, E * K), 0), 1.0, 0.0).astype(F32)
    coef_h, coef_l = halves(solved)

    def kron(part):
        wide = dot(part, spread)
        blocks = [wide[m : m + 1, :] * same for m in range(pair_all + 2)]
        return jnp.concatenate(blocks, 0).astype(BF16)

    kron_rows = kron_ref.shape[0] // 2
    kron_ref[0:kron_rows] = kron(coef_h)
    kron_ref[kron_rows:] = kron(coef_l)

    def result_send(r, i):
        peer = mem_peer(i)
        pair_copy = pltpu.make_async_remote_copy(
            src_ref=ob.at[pl.ds(peer * pairs, pairs), r],
            dst_ref=pair_out.at[:, me * RQ + r],
            send_sem=os_sem.at[0, r, i - 1],
            recv_sem=or_sem.at[0, r, i - 1],
            device_id=at(tile, peer),
            device_id_type=MESH,
        )
        mean_copy = pltpu.make_async_remote_copy(
            src_ref=mb.at[r],
            dst_ref=mean_out.at[me * RQ + r],
            send_sem=os_sem.at[1, r, i - 1],
            recv_sem=or_sem.at[1, r, i - 1],
            device_id=at(tile, peer),
            device_id_type=MESH,
        )
        return pair_copy, mean_copy

    np8 = pair_all * K

    def update(r, _):
        inc[...] = dot(kron_ref[...], dh[r])
        more = dot(kron_ref[0:kron_rows], dl[r])
        total = inc[0:kron_rows] + inc[kron_rows:] + more
        ob[:, r] = (s_f * (dg[r] + total[:np8])).reshape(pair_all, K, NC)
        mb[r] = mu[r] + total[np8 : np8 + K]
        for i in sorted(range(1, groups), key=lambda i: -min(i, groups - i)):
            for copy in result_send(r, i):
                copy.start()
        return 0

    lax.fori_loop(0, RQ, update, 0)
    own_out = pltpu.make_async_copy(ob.at[pl.ds(me * pairs, pairs)], pair_out.at[:, pl.ds(me * RQ, RQ)], own_sem.at[2])
    own_mean = pltpu.make_async_copy(mb, mean_out.at[pl.ds(me * RQ, RQ)], own_sem.at[3])
    own_out.start()
    own_mean.start()

    for way in range(2):
        for ch in range(lch):
            level_halo(ch, way).wait_send()
        for j in range(pairs):
            fine_halo(j, way).wait_send()
            pair_halo(j, way).wait_send()
    for i in range(1, groups):
        for ch in range(lch):
            level_send(ch, i).wait_send()
        for j in range(pairs):
            pair_send(j, i).wait_send()
        for part in range(2):
            obs_send(part, i).wait_send()
    own_out.wait()
    own_mean.wait()
    for r in range(RQ):
        for i in range(1, groups):
            for copy in result_send(r, i):
                copy.wait_recv()
                copy.wait_send()


def order_kernel(K, RF, pair_in, mean_in, pair_out, mean_out, pv, mv, sem):
    nv = pv.shape[0]
    pairs = pair_in.shape[0]

    def put(value, ref, first, r):
        for v in range(nv):
            ref[v, pl.ds(first + r, K, stride=RF), :] = value[:, v * LANES : (v + 1) * LANES]

    copies = []

    def send(ref, first, out, row):
        for v in range(nv):
            copy = pltpu.make_async_copy(
                ref.at[v, pl.ds(first, K * RF)],
                out.at[pl.ds(first, K * RF), pl.ds(v * LANES, LANES)],
                sem.at[row, v],
            )
            copy.start()
            copies.append(copy)

    for m in range(pairs):
        for r in range(RF):
            put(pair_in[m, r], pv, m * K * RF, r)
        send(pv, m * K * RF, pair_out, m)
    for r in range(RF):
        put(mean_in[r], mv, 0, r)
    send(mv, 0, mean_out, pairs)
    for copy in copies:
        copy.wait()


def axis_stages(tiles):
    axes, stride = [], 1
    for size in (2, 4, 4):
        if stride < tiles:
            axes.append((stride, size))
            stride *= size
    return tuple(stage for stage in (tuple(axes[:2]), tuple(axes[2:])) if stage)


def per_device(
    fine_members,
    coarse_members,
    diffusion,
    hyper,
    drift,
    obs_value,
    obs_var,
    obs_row,
    obs_col,
    obs_layer,
    obs_count,
):
    tiles = lax.axis_size("rows")
    groups = lax.axis_size("mem")
    pairs, K, RF, NC = fine_members.shape
    levels, _, RC, NCC = coarse_members.shape
    stages = axis_stages(tiles)
    sizes = (tiles, groups, pairs, levels, K, RF, RC, NC, NCC, stages)
    slots = obs_value.shape[0]
    E = (pairs + levels) * groups
    nb = 4
    per = slots // nb
    RQ, RQC = RF // groups, RC // groups
    chunks = levels // 2 + 2 * pairs
    peers = sum(math.prod(size for _, size in stage) - 1 for stage in stages)
    nv, nvc = NC // LANES, NCC // LANES
    anyspace = pl.BlockSpec(memory_space=pl.ANY)
    hbm = pl.BlockSpec(memory_space=pltpu.HBM)
    vmem = pl.BlockSpec(memory_space=pltpu.VMEM)
    dma = pltpu.SemaphoreType.DMA

    def flat(obs):
        return obs.reshape(slots // LANES, LANES)

    def keep(array):
        return pltpu.with_memory_space_constraint(array, pltpu.HBM)

    pair_rows, mean_rows = pl.pallas_call(
        functools.partial(cycle_kernel, sizes),
        out_shape=(
            jax.ShapeDtypeStruct((pairs, RF, K, NC), F32),
            jax.ShapeDtypeStruct((RF, K, NC), F32),
        ),
        in_specs=[hbm] * 11,
        out_specs=(anyspace, anyspace),
        scratch_shapes=[
            pltpu.SMEM((K,), F32),
            pltpu.SMEM((K,), F32),
            pltpu.SMEM((K,), F32),
            pltpu.SMEM((1,), jnp.int32),
            pltpu.VMEM((slots // LANES, LANES), F32),
            pltpu.VMEM((slots // LANES, LANES), F32),
            pltpu.VMEM((slots // LANES, LANES), jnp.int32),
            pltpu.VMEM((slots // LANES, LANES), jnp.int32),
            pltpu.VMEM((slots // LANES, LANES), jnp.int32),
            pltpu.VMEM((nv, pairs * K * RF, LANES), F32),
            pltpu.VMEM((nvc, levels * K * RC, LANES), F32),
            pltpu.VMEM((pairs, RF + 2 * HALO, K, NC), F32),
            pltpu.VMEM((levels + pairs, RC + 2 * HALO, K, NCC), F32),
            pltpu.VMEM((RF + 8, K, NC), F32),
            pltpu.VMEM((RF + 4, K, NC), F32),
            pltpu.VMEM((2, RC + 8, K, NCC), F32),
            pltpu.VMEM((2, RC + 4, K, NCC), F32),
            pltpu.VMEM((levels + pairs, RC, K, NCC), F32),
            pltpu.VMEM((pairs, RF, K, NC), F32),
            pltpu.VMEM((groups, pairs, RQ, K, NC), F32),
            pltpu.VMEM((groups, levels, RQC, K, NCC), F32),
            pltpu.VMEM((nb, NC, per), BF16),
            pltpu.VMEM((nb, RF * K, per), F32),
            pltpu.VMEM((nb, NCC, per), BF16),
            pltpu.VMEM((nb, RC * K, per), F32),
            pltpu.VMEM((nb + nb // 2, levels, per), F32),
            pltpu.VMEM((groups, nb + nb // 2, levels, per), F32),
            pltpu.VMEM((len(stages), E // 2, LANES), F32),
            pltpu.VMEM((peers, E // 2, LANES), F32),
            pltpu.VMEM((2 * (pairs * groups + 2) * K, E * K), BF16),
            pltpu.VMEM((2 * (pairs * groups + 2) * K, NC), F32),
            pltpu.VMEM((RQ, pairs * groups * K, NC), F32),
            pltpu.VMEM((RQ, E * K, NC), BF16),
            pltpu.VMEM((RQ, E * K, NC), BF16),
            pltpu.VMEM((RQ, K, NC), F32),
            pltpu.VMEM((pairs * groups, RQ, K, NC), F32),
            pltpu.VMEM((RQ, K, NC), F32),
            dma((nv + nvc,)),
            dma((9,)),
            dma((chunks, 2)),
            dma((chunks, 2)),
            dma((2, groups - 1)),
            dma((2, groups - 1)),
            dma((peers,)),
            dma((peers,)),
            dma((levels // 2 + pairs, groups - 1)),
            dma((levels // 2 + pairs, groups - 1)),
            dma((2, RQ, groups - 1)),
            dma((2, RQ, groups - 1)),
            dma((4,)),
        ],
        compiler_params=pltpu.CompilerParams(
            collective_id=0, has_side_effects=True, vmem_limit_bytes=48 * 1024 * 1024
        ),
        name="cycle",
    )(
        keep(fine_members.reshape(pairs * K * RF, NC)),
        keep(coarse_members.reshape(levels * K * RC, NCC)),
        keep(diffusion),
        keep(hyper),
        keep(drift),
        keep(flat(obs_value)),
        keep(flat(obs_var)),
        keep(flat(obs_row)),
        keep(flat(obs_col)),
        keep(flat(obs_layer)),
        obs_count,
    )
    pair, mean = pl.pallas_call(
        functools.partial(order_kernel, K, RF),
        out_shape=(
            jax.ShapeDtypeStruct((pairs * K * RF, NC), F32),
            jax.ShapeDtypeStruct((K * RF, NC), F32),
        ),
        in_specs=[vmem, vmem],
        out_specs=(anyspace, anyspace),
        scratch_shapes=[
            pltpu.VMEM((nv, pairs * K * RF, LANES), F32),
            pltpu.VMEM((nv, K * RF, LANES), F32),
            dma((pairs + 1, nv)),
        ],
        compiler_params=pltpu.CompilerParams(vmem_limit_bytes=16 * 1024 * 1024),
        name="order",
    )(pair_rows, mean_rows)
    return mean.reshape(K, RF, NC), pair.reshape(pairs, K, RF, NC)


def solution(mesh):
    in_specs = (
        P("mem", None, "rows", None),
        P("mem", None, "rows", None),
        P(),
        P(),
        P(),
        P("rows"),
        P("rows"),
        P("rows"),
        P("rows"),
        P("rows"),
        P("rows"),
    )
    out_specs = (P(None, "rows", None), P("mem", None, "rows", None))
    return jax.shard_map(
        per_device, mesh=mesh, in_specs=in_specs, out_specs=out_specs, check_vma=False
    )
```

```python
import functools
import itertools
import math

import jax
import jax.numpy as jnp
from jax import lax
from jax.experimental import pallas as pl
from jax.experimental.pallas import tpu as pltpu
from jax.sharding import PartitionSpec as P

STEPS = 3
EARLY = 1
HALO = 2 * STEPS
LANES = 128
MESH = pl.DeviceIdType.MESH
HIGHEST = lax.Precision.HIGHEST
F32 = jnp.float32
BF16 = jnp.bfloat16


def iota(shape, axis):
    return lax.broadcasted_iota(jnp.int32, shape, axis)


def halves(value):
    high = value.astype(BF16)
    return high, (value - high.astype(F32)).astype(BF16)


def dot(left, right):
    return jnp.dot(left, right, preferred_element_type=F32)


def select_dot(left, right):
    rows = left.shape[0]
    high = left.astype(BF16)
    rest = left - high.astype(F32)
    mid = rest.astype(BF16)
    low = (rest - mid.astype(F32)).astype(BF16)
    out = dot(jnp.concatenate([high, mid, low], 0), right)
    return out[:rows] + (out[rows : 2 * rows] + out[2 * rows :])


def column_at(place, parts):
    return (place % LANES) * parts + place // LANES


def place_of(column, parts):
    shift = parts.bit_length() - 1
    return (column & (parts - 1)) * LANES + (column >> shift)


def shifted(row, packed):
    width = row.shape[-1]
    first, last = row[:, :LANES], row[:, width - LANES :]
    left = jnp.concatenate([pltpu.roll(last, packed, axis=1), row[:, : width - LANES]], 1)
    right = jnp.concatenate([row[:, LANES:], pltpu.roll(first, LANES - packed, axis=1)], 1)
    return left, right


def halved(row):
    tiles = [row[:, i * LANES : (i + 1) * LANES] for i in range(row.shape[1] // LANES)]
    return jnp.concatenate([a + b for a, b in zip(tiles[::2], tiles[1::2])], 1)


def doubled(row):
    tiles = [row[:, i * LANES : (i + 1) * LANES] for i in range(row.shape[1] // LANES)]
    return jnp.concatenate([tile for tile in tiles for _ in range(2)], 1)


def layer_vector(ref, scale, layers, width):
    at = iota((layers, width), 0)
    out = jnp.zeros((layers, width), F32)
    for k in range(layers):
        out = jnp.where(at == k, ref[k] * scale, out)
    return out


def advance(read, write, count, first_row, grid_rows, own, coef, packed=1):
    lap_c, hyp_c, drift_c, up_c, low_c = coef
    layers = up_c.shape[0]
    beside = (count + 4 - own) // 2

    def inside(j, value):
        if beside <= j < beside + own:
            return value
        at = first_row + j
        return value * jnp.where((at >= 0) & (at < grid_rows), 1.0, 0.0).astype(F32)

    q0, q1, q2, q3 = read(0), read(1), read(2), read(3)
    left, right = shifted(q1, packed)
    f1 = inside(1, q2 + q0 + left + right - 4.0 * q1)
    left, right = shifted(q2, packed)
    f2 = inside(2, q3 + q1 + left + right - 4.0 * q2)
    side = right - left
    for i in range(count):
        q2, q3, q4 = read(i + 2), read(i + 3), read(i + 4)
        left, right = shifted(q3, packed)
        f3 = inside(i + 3, q4 + q2 + left + right - 4.0 * q3)
        fl, fr = shifted(f2, packed)
        out = (
            0.8 * q2
            + up_c * pltpu.roll(q2, layers - 1, axis=0)
            + low_c * pltpu.roll(q2, 1, axis=0)
            + lap_c * f2
            - hyp_c * (f1 + f3 + fl + fr)
            - drift_c * side
        )
        write(i, inside(i + 2, out))
        f1, f2, side = f2, f3, right - left


def cycle_kernel(
    sizes,
    fine_in,
    coarse_in,
    diff_in,
    hyper_in,
    drift_in,
    val_in,
    var_in,
    row_in,
    col_in,
    layer_in,
    count_in,
    pair_out,
    mean_out,
    diff_ref,
    hyper_ref,
    drift_ref,
    count_ref,
    val_ref,
    var_ref,
    row_ref,
    col_ref,
    layer_ref,
    xv,
    zv,
    fq,
    cq,
    zq,
    ft1,
    ft2,
    ct1,
    ct2,
    cres,
    zres,
    g,
    gh,
    gl,
    zh,
    zl,
    ga,
    za,
    oc,
    rm,
    occ,
    rmc,
    sown,
    sx,
    ar0,
    ar1,
    kron_ref,
    inc,
    dg,
    dh,
    dl,
    mu,
    ob,
    mb,
    load_sem,
    small_sem,
    hs_sem,
    hr_sem,
    ss_sem,
    sr_sem,
    as_sem,
    ar_sem,
    ts_sem,
    tr_sem,
    os_sem,
    or_sem,
    own_sem,
):
    tiles, groups, pairs, levels, K, RF, RC, NC, NCC, stages = sizes
    tile = lax.axis_index("rows")
    me = lax.axis_index("mem")
    level_all, pair_all = levels * groups, pairs * groups
    E = level_all + pair_all
    nv, nvc = NC // LANES, NCC // LANES
    lch = levels // 2
    RQ, RQC = RF // groups, RC // groups
    s_f, s_c = math.sqrt(pair_all - 1), math.sqrt(level_all - 1)

    def at(row, mem):
        return (row, mem)

    def mem_peer(i):
        return lax.rem(me + i, groups)

    def stage_peers(stage):
        peers = []
        for offsets in itertools.product(*[range(size) for _, size in stage]):
            if any(offsets):
                peer = tile
                for offset, (stride, size) in zip(offsets, stage):
                    mine = lax.rem(tile // stride, size)
                    peer = peer + (lax.rem(mine + offset, size) - mine) * stride
                peers.append(peer)
        return peers

    up = lax.rem(tile + tiles - 1, tiles)
    down = lax.rem(tile + 1, tiles)

    loads = []
    for v in range(nvc):
        loads.append(pltpu.make_async_copy(coarse_in.at[:, pl.ds(v * LANES, LANES)], zv.at[v], load_sem.at[v]))
    for v in range(nv):
        loads.append(pltpu.make_async_copy(fine_in.at[:, pl.ds(v * LANES, LANES)], xv.at[v], load_sem.at[nvc + v]))
    for load in loads:
        load.start()
    smalls = [
        (diff_in, diff_ref),
        (hyper_in, hyper_ref),
        (drift_in, drift_ref),
        (count_in, count_ref),
        (val_in, val_ref),
        (var_in, var_ref),
        (row_in, row_ref),
        (col_in, col_ref),
        (layer_in, layer_ref),
    ]
    smalls = [pltpu.make_async_copy(a, b, small_sem.at[n]) for n, (a, b) in enumerate(smalls)]
    for small in smalls:
        small.start()

    targets = [(up, me), (down, me)]
    targets += [(tile, mem_peer(i)) for i in range(1, groups)]
    for stage in stages:
        targets += [(peer, me) for peer in stage_peers(stage)]
    barrier = pltpu.get_barrier_semaphore()
    for target in targets:
        pl.semaphore_signal(barrier, inc=1, device_id=at(*target), device_id_type=MESH)

    def columns_in(width):
        shape = (width, width)
        held = column_at(iota(shape, 1), width // LANES)
        return jnp.where(iota(shape, 0) == held, 1.0, 0.0).astype(BF16)

    def halo_copy(ref, lead, src, dst, rows, number, way):
        return pltpu.make_async_remote_copy(
            src_ref=ref.at[lead, pl.ds(src, rows)],
            dst_ref=ref.at[lead, pl.ds(dst, rows)],
            send_sem=hs_sem.at[number, way],
            recv_sem=hr_sem.at[number, way],
            device_id=at(up if way == 0 else down, me),
            device_id_type=MESH,
        )

    def level_halo(ch, way):
        src, dst = ((HALO, HALO + RC), (RC, 0))[way]
        return halo_copy(zq, ch, src, dst, HALO, ch, way)

    def fine_halo(j, way):
        src, dst = ((HALO, HALO + RF), (RF, 0))[way]
        return halo_copy(fq, j, src, dst, HALO, lch + j, way)

    near = HALO // 2

    def pair_halo(j, way):
        src, dst = ((HALO + near, HALO + RC + near), (RC, 0))[way]
        return halo_copy(cq, j, src, dst, HALO - near, lch + pairs + j, way)

    def level_column(p):
        return (p % LANES) // 2 * nv + p // LANES

    p = iota((2 * NCC, NC), 1)
    order_c = jnp.where(iota((2 * NCC, NC), 0) == p % 2 * NCC + level_column(p), 1.0, 0.0).astype(BF16)

    def place_level(ch, _):
        rows = []
        for r in range(RC):
            row = []
            for m in range(2):
                row += [zv[v, pl.ds((2 * ch + m) * K * RC + r, K, stride=RC), :] for v in range(nvc)]
            rows.append(jnp.concatenate(row, 1))
        zq[ch, HALO : HALO + RC] = select_dot(jnp.concatenate(rows, 0), order_c).reshape(RC, K, NC)
        return 0

    for load in loads[:nvc]:
        load.wait()
    lax.fori_loop(0, lch, place_level, 0)

    pl.semaphore_wait(barrier, len(targets))
    for ch in range(lch):
        for way in range(2):
            level_halo(ch, way).start()

    order_f = columns_in(NC)

    def place_fine(m):
        rows = []
        for r in range(RF):
            first = m * K * RF + r
            rows.append(jnp.concatenate([xv[v, pl.ds(first, K, stride=RF), :] for v in range(nv)], 1))
        fq[m, HALO : HALO + RF] = select_dot(jnp.concatenate(rows, 0), order_f).reshape(RF, K, NC)
        restrict(m, HALO, HALO, RC)

    def send_fine(m):
        for way in range(2):
            fine_halo(m, way).start()
            pair_halo(m, way).start()

    def restrict(m, fine_row, coarse_row, count):
        for r in range(count):
            both = fq[m, fine_row + 2 * r] + fq[m, fine_row + 2 * r + 1]
            cq[m, coarse_row + r] = 0.25 * halved(both)

    def place_and_send(m, _):
        place_fine(m)
        send_fine(m)
        return 0

    for load in loads[nvc:]:
        load.wait()
    lax.fori_loop(0, pairs, place_and_send, 0)

    for small in smalls:
        small.wait()
    nb = 4
    per = val_ref.shape[0] * LANES // nb
    sub = per // LANES

    def row_of(ref, first, number):
        return jnp.concatenate([ref[i : i + 1, :] for i in range(first, first + number)], 1)

    for b in range(nb):
        col = row_of(col_ref, b * sub, sub)
        lay = row_of(layer_ref, b * sub, sub)
        loc = row_of(row_ref, b * sub, sub) - tile * RF
        oc[b] = jnp.where(iota((NC, per), 0) == place_of(col, nv), 1.0, 0.0).astype(BF16)
        place = ((col >> 1) & (nv - 1)) * LANES + (col >> 1) // nv * 2
        for m in range(2):
            occ[b, m] = jnp.where(iota((NC, per), 0) == place + m, 1.0, 0.0).astype(BF16)
        rm[b] = jnp.where(iota((RF * K, per), 0) == loc * K + lay, 1.0, 0.0).astype(F32)
        rmc[b] = jnp.where(iota((RC * K, per), 0) == (loc >> 1) * K + lay, 1.0, 0.0).astype(F32)

    def coefs(scale_a, scale_h, scale_u, width):
        a = layer_vector(diff_ref, scale_a, K, width)
        h = layer_vector(hyper_ref, scale_h, K, width)
        u = layer_vector(drift_ref, scale_u, K, width)
        k = iota((K, width), 0)
        up_c = jnp.where(k < K - 1, 0.1, 0.0).astype(F32)
        low_c = jnp.where(k > 0, 0.1, 0.0).astype(F32)
        return a + 4.0 * h, h, 0.5 * u, up_c, low_c

    def zero_edges(clear_low, clear_high):
        @pl.when(tile == 0)
        def _():
            clear_low()

        @pl.when(tile == tiles - 1)
        def _():
            clear_high()

    coarse_coef = coefs(0.25, 0.0625, 0.5, NCC)
    level_coef = coefs(0.25, 0.0625, 0.5, NC)
    row_c = tile * RC - HALO
    grid_c = tiles * RC

    def reader(ref, lead):
        return lambda j: ref[lead + (j,)]

    def writer(ref, lead):
        def write(i, value):
            ref[lead + (i,)] = value
        return write

    def coarse_steps(j):
        advance(reader(cq, (j,)), writer(ct1, ()), RC + 8, row_c, grid_c, RC, coarse_coef)
        advance(reader(ct1, ()), writer(ct2, ()), RC + 4, row_c + 2, grid_c, RC, coarse_coef)
        advance(reader(ct2, ()), writer(cres, (j,)), RC, row_c + 4, grid_c, RC, coarse_coef)

    def level_steps(ch):
        advance(reader(zq, (ch,)), writer(ft1, ()), RC + 8, row_c, grid_c, RC, level_coef, 2)
        advance(reader(ft1, ()), writer(ft2, ()), RC + 4, row_c + 2, grid_c, RC, level_coef, 2)
        advance(reader(ft2, ()), writer(zres, (ch,)), RC, row_c + 4, grid_c, RC, level_coef, 2)
        zh[ch], zl[ch] = halves(zres[ch].reshape(RC * K, NC))

    def level_send(ch, i):
        peer = mem_peer(i)
        return pltpu.make_async_remote_copy(
            src_ref=zres.at[ch, pl.ds(peer * RQC, RQC)],
            dst_ref=za.at[me, ch],
            send_sem=ts_sem.at[ch, i - 1],
            recv_sem=tr_sem.at[ch, i - 1],
            device_id=at(tile, peer),
            device_id_type=MESH,
        )

    def pair_send(j, i):
        peer = mem_peer(i)
        return pltpu.make_async_remote_copy(
            src_ref=g.at[j, pl.ds(peer * RQ, RQ)],
            dst_ref=ga.at[me, j],
            send_sem=ts_sem.at[lch + j, i - 1],
            recv_sem=tr_sem.at[lch + j, i - 1],
            device_id=at(tile, peer),
            device_id_type=MESH,
        )

    def level_chunk(ch, _):
        level_halo(ch, 0).wait_recv()
        level_halo(ch, 1).wait_recv()

        def clear(first):
            zq[ch, first : first + HALO] = jnp.zeros((HALO, K, NC), F32)

        zero_edges(lambda: clear(0), lambda: clear(HALO + RC))
        level_steps(ch)
        for i in range(1, groups):
            level_send(ch, i).start()
        return 0

    def gather(high, low, columns, rows):
        number = high.shape[0]
        flat = (number * high.shape[1], high.shape[2])
        got = dot(high[...].reshape(flat), columns) + dot(low[...].reshape(flat), columns)
        return jnp.sum(got.reshape((number,) + rows.shape) * rows[None], axis=1)

    def level_gather(b, _):
        sown[b] = jnp.concatenate([gather(zh, zl, occ[b, m], rmc[b]) for m in range(2)], 0)
        return 0

    def pair_gather(half, _):
        sown[nb + half] = jnp.concatenate([gather(gh, gl, oc[2 * half + b], rm[2 * half + b]) for b in range(2)], 0)
        return 0

    def obs_send(part, i):
        span = (pl.ds(nb, nb // 2), pl.ds(0, nb))[part]
        return pltpu.make_async_remote_copy(
            src_ref=sown.at[span],
            dst_ref=sx.at[me, span],
            send_sem=ss_sem.at[part, i - 1],
            recv_sem=sr_sem.at[part, i - 1],
            device_id=at(tile, mem_peer(i)),
            device_id_type=MESH,
        )

    lax.fori_loop(0, lch, level_chunk, 0)
    lax.fori_loop(0, nb, level_gather, 0)
    for i in range(1, groups):
        obs_send(1, i).start()

    fine_coef = coefs(1.0, 1.0, 1.0, NC)
    row_f = tile * RF - HALO
    grid_f = tiles * RF

    def fine_member(j, _):
        for way in range(2):
            fine_halo(j, way).wait_recv()
            pair_halo(j, way).wait_recv()

        def clear(first, first_c):
            fq[j, first : first + HALO] = jnp.zeros((HALO, K, NC), F32)
            cq[j, first_c : first_c + HALO] = jnp.zeros((HALO, K, NCC), F32)

        restrict(j, 0, near, near)
        restrict(j, HALO + RF, HALO + RC, near)
        zero_edges(lambda: clear(0, 0), lambda: clear(HALO + RF, HALO + RC))
        coarse_steps(j)

        def put_g(i, value):
            g[j, i] = value - doubled(cres[j, i // 2])

        advance(reader(fq, (j,)), writer(ft1, ()), RF + 8, row_f, grid_f, RF, fine_coef)
        advance(reader(ft1, ()), writer(ft2, ()), RF + 4, row_f + 2, grid_f, RF, fine_coef)
        advance(reader(ft2, ()), put_g, RF, row_f + 4, grid_f, RF, fine_coef)
        gh[j], gl[j] = halves(g[j].reshape(RF * K, NC))

        @pl.when(j < EARLY)
        def _():
            for i in range(1, groups):
                pair_send(j, i).start()

        return 0

    lax.fori_loop(0, pairs, fine_member, 0)

    lax.fori_loop(0, nb // 2, pair_gather, 0)
    for i in range(1, groups):
        obs_send(0, i).start()
    sx[me] = sown[...]
    for j in range(EARLY, pairs):
        for i in range(1, groups):
            pair_send(j, i).start()
    for i in range(1, groups):
        obs_send(1, i).wait_recv()
    level_parts = []
    for b in range(nb):
        z = jnp.concatenate([sx[x, b, m * lch : (m + 1) * lch] for m in range(2) for x in range(groups)], 0)
        z_mean = jnp.mean(z, axis=0, keepdims=True)
        slot = iota((1, per), 1) + b * per
        weight = jnp.where(slot < count_ref[0], 1.0 / row_of(var_ref, b * sub, sub), 0.0)
        level_parts.append(((z - z_mean) * (1.0 / s_c), row_of(val_ref, b * sub, sub) - z_mean, weight))
    for i in range(1, groups):
        obs_send(0, i).wait_recv()
    own_level = pltpu.make_async_copy(zres.at[:, pl.ds(me * RQC, RQC)], za.at[me], own_sem.at[0])
    own_pair = pltpu.make_async_copy(g.at[:, pl.ds(me * RQ, RQ)], ga.at[me], own_sem.at[1])
    own_level.start()
    own_pair.start()

    gram = jnp.zeros((E, E + 8), F32)
    for b in range(nb):
        z, rest, weight = level_parts[b]
        first = (b % 2) * pairs
        f = jnp.concatenate([sx[x, nb + b // 2, first : first + pairs] for x in range(groups)], 0)
        f_mean = jnp.mean(f, axis=0, keepdims=True)
        s = jnp.concatenate([z, (f - f_mean) * (1.0 / s_f)], 0)
        innov = rest - f_mean
        extra = jnp.where(iota((8, per), 0) == 0, weight * innov, 0.0)
        right = jnp.concatenate([s * weight, extra], 0)
        gram = gram + lax.dot_general(
            s, right, (((1,), (1,)), ((), ())), precision=HIGHEST, preferred_element_type=F32
        )
    half_e, half_l = E // 2, LANES // 2
    gram = jnp.concatenate([gram, jnp.zeros((E, LANES - E - 8), F32)], 1)
    gram = gram[:half_e] + pltpu.roll(gram[half_e:], half_l, axis=1)

    zk = level_all * K

    def level_anomalies():
        own_level.wait()
        for ch in range(lch):
            for i in range(1, groups):
                level_send(ch, i).wait_recv()

        p = iota((NC, NC), 0)
        hit = level_column(p) == iota((NC, NC), 1) // 2
        widen = [jnp.where(hit & (p % 2 == m), 1.0, 0.0).astype(BF16) for m in range(2)]
        even = iota((K, LANES), 1) % 2 == 0

        def with_other(tile):
            other = jnp.where(even, pltpu.roll(tile, LANES - 1, axis=1), pltpu.roll(tile, 1, axis=1))
            return tile + other

        def one(rc, _):
            z = za[:, :, rc].reshape(level_all // 2, K, NC)
            total = jnp.sum(z, axis=0)
            total = jnp.concatenate([with_other(total[:, v * LANES : (v + 1) * LANES]) for v in range(nv)], 1)
            z_mean = total * (1.0 / level_all)
            high, low = halves(((z - z_mean[None]) * (1.0 / s_c)).reshape(zk // 2, NC))
            wide_mean = select_dot(z_mean, widen[0])
            for m in range(2):
                wide_high, wide_low = dot(high, widen[m]).astype(BF16), dot(low, widen[m]).astype(BF16)
                for half in range(2):
                    dh[2 * rc + half, m * zk // 2 : (m + 1) * zk // 2] = wide_high
                    dl[2 * rc + half, m * zk // 2 : (m + 1) * zk // 2] = wide_low
            for half in range(2):
                mu[2 * rc + half] = wide_mean
            return 0

        lax.fori_loop(0, RQC, one, 0)

    def columns_out(width, repeat):
        shape = (width, width * repeat)
        held = column_at(iota(shape, 0), width // LANES)
        return jnp.where(held == iota(shape, 1) // repeat, 1.0, 0.0).astype(BF16)

    def pair_anomalies():
        own_pair.wait()
        for j in range(pairs):
            for i in range(1, groups):
                pair_send(j, i).wait_recv()
        natural = columns_out(NC, 1)

        def one(r, _):
            f = ga[:, :, r].reshape(pair_all, K, NC)
            f_mean = jnp.mean(f, axis=0)
            mu[r] = mu[r] + select_dot(f_mean, natural)
            anom = ((f - f_mean[None]) * (1.0 / s_f)).reshape(pair_all * K, NC)
            high = anom.astype(BF16)
            rest = anom - high.astype(F32)
            mid = rest.astype(BF16)
            low = (rest - mid.astype(F32)).astype(BF16)
            high, mid, low = dot(high, natural), dot(mid, natural), dot(low, natural)
            dg[r] = high + (mid + low)
            dh[r, zk:] = high.astype(BF16)
            dl[r, zk:] = mid.astype(BF16)
            return 0

        lax.fori_loop(0, RQ, one, 0)

    slot0 = 0
    for s, stage in enumerate(stages):
        ar0[s] = gram
        sends = []
        for n, peer in enumerate(stage_peers(stage), slot0):
            send = pltpu.make_async_remote_copy(
                src_ref=ar0.at[s],
                dst_ref=ar1.at[n],
                send_sem=as_sem.at[n],
                recv_sem=ar_sem.at[n],
                device_id=at(peer, me),
                device_id_type=MESH,
            )
            send.start()
            sends.append((send, n))
        if s == 0:
            level_anomalies()
        if s == len(stages) - 1:
            pair_anomalies()
        for send, n in sends:
            send.wait_recv()
            gram = gram + ar1[n]
        for send, n in sends:
            send.wait_send()
        slot0 += len(sends)

    rows_t = E + pair_all + 8
    lane = iota((rows_t, LANES), 1)
    eye = jnp.where(iota((E, LANES), 0) == iota((E, LANES), 1), 1.0, 0.0).astype(F32)
    full = jnp.concatenate([gram, pltpu.roll(gram, half_l, axis=1)], 0)
    rhs = jnp.sum(full[:, E : E + 1] * eye, axis=0, keepdims=True)
    full = jnp.where(iota((E, LANES), 1) < E, full, 0.0)
    rhs = jnp.where(iota((8, LANES), 0) == 0, rhs, 0.0)
    table = jnp.concatenate([full + eye, full[level_all:E], rhs], 0)
    width = 4
    for k in range(0, E, width):
        block = range(width)
        columns = [jnp.broadcast_to(table[:, k + i : k + i + 1], (rows_t, LANES)) for i in block]
        heads = [table[k + i : k + i + 1, :] for i in block]
        inv = [[columns[j][k + i : k + i + 1, :] for j in block] for i in block]
        for p in block:
            pivot = 1.0 / inv[p][p]
            scaled = [pivot if j == p else inv[p][j] * pivot for j in block]
            inv = [
                scaled
                if i == p
                else [
                    -inv[i][p] * pivot if j == p else inv[i][j] - inv[i][p] * scaled[j] for j in block
                ]
                for i in block
            ]
        ends = []
        for i in block:
            end = columns[0] * inv[0][i]
            for j in range(1, width):
                end = end + columns[j] * inv[j][i]
            ends.append(end)
        change = ends[0] * heads[0]
        for i in range(1, width):
            change = change + ends[i] * heads[i]
        table = table - change
        for i in block:
            table = jnp.where(lane == k + i, ends[i], table)
    solved = jnp.concatenate([-0.5 * table[E : E + pair_all], table[E + pair_all :]], 0)

    spread = jnp.where(iota((LANES, E * K), 1) // K == iota((LANES, E * K), 0), 1.0, 0.0).astype(BF16)
    same = jnp.where(lax.rem(iota((K, E * K), 1), K) == iota((K, E * K), 0), 1.0, 0.0).astype(F32)
    coef_h, coef_l = halves(solved)

    def kron(part):
        wide = dot(part, spread)
        blocks = [wide[m : m + 1, :] * same for m in range(pair_all + 2)]
        return jnp.concatenate(blocks, 0).astype(BF16)

    kron_rows = kron_ref.shape[0] // 2
    kron_ref[0:kron_rows] = kron(coef_h)
    kron_ref[kron_rows:] = kron(coef_l)

    def result_send(r, i):
        peer = mem_peer(i)
        pair_copy = pltpu.make_async_remote_copy(
            src_ref=ob.at[pl.ds(peer * pairs, pairs), r],
            dst_ref=pair_out.at[:, me * RQ + r],
            send_sem=os_sem.at[0, r, i - 1],
            recv_sem=or_sem.at[0, r, i - 1],
            device_id=at(tile, peer),
            device_id_type=MESH,
        )
        mean_copy = pltpu.make_async_remote_copy(
            src_ref=mb.at[r],
            dst_ref=mean_out.at[me * RQ + r],
            send_sem=os_sem.at[1, r, i - 1],
            recv_sem=or_sem.at[1, r, i - 1],
            device_id=at(tile, peer),
            device_id_type=MESH,
        )
        return pair_copy, mean_copy

    np8 = pair_all * K

    def update(r, _):
        inc[...] = dot(kron_ref[...], dh[r])
        more = dot(kron_ref[0:kron_rows], dl[r])
        total = inc[0:kron_rows] + inc[kron_rows:] + more
        ob[:, r] = (s_f * (dg[r] + total[:np8])).reshape(pair_all, K, NC)
        mb[r] = mu[r] + total[np8 : np8 + K]
        for i in sorted(range(1, groups), key=lambda i: -min(i, groups - i)):
            for copy in result_send(r, i):
                copy.start()
        return 0

    lax.fori_loop(0, RQ, update, 0)
    own_out = pltpu.make_async_copy(ob.at[pl.ds(me * pairs, pairs)], pair_out.at[:, pl.ds(me * RQ, RQ)], own_sem.at[2])
    own_mean = pltpu.make_async_copy(mb, mean_out.at[pl.ds(me * RQ, RQ)], own_sem.at[3])
    own_out.start()
    own_mean.start()

    for way in range(2):
        for ch in range(lch):
            level_halo(ch, way).wait_send()
        for j in range(pairs):
            fine_halo(j, way).wait_send()
            pair_halo(j, way).wait_send()
    for i in range(1, groups):
        for ch in range(lch):
            level_send(ch, i).wait_send()
        for j in range(pairs):
            pair_send(j, i).wait_send()
        for part in range(2):
            obs_send(part, i).wait_send()
    own_out.wait()
    own_mean.wait()
    for r in range(RQ):
        for i in range(1, groups):
            for copy in result_send(r, i):
                copy.wait_recv()
                copy.wait_send()


def order_kernel(K, RF, pair_in, mean_in, pair_out, mean_out, pv, mv, sem):
    nv = pv.shape[0]
    pairs = pair_in.shape[0]

    def put(value, ref, first, r):
        for v in range(nv):
            ref[v, pl.ds(first + r, K, stride=RF), :] = value[:, v * LANES : (v + 1) * LANES]

    copies = []

    def send(ref, first, out, row):
        for v in range(nv):
            copy = pltpu.make_async_copy(
                ref.at[v, pl.ds(first, K * RF)],
                out.at[pl.ds(first, K * RF), pl.ds(v * LANES, LANES)],
                sem.at[row, v],
            )
            copy.start()
            copies.append(copy)

    for m in range(pairs):
        for r in range(RF):
            put(pair_in[m, r], pv, m * K * RF, r)
        send(pv, m * K * RF, pair_out, m)
    for r in range(RF):
        put(mean_in[r], mv, 0, r)
    send(mv, 0, mean_out, pairs)
    for copy in copies:
        copy.wait()


def axis_stages(tiles):
    axes, stride = [], 1
    for size in (2, 4, 4):
        if stride < tiles:
            axes.append((stride, size))
            stride *= size
    return tuple(stage for stage in (tuple(axes[:2]), tuple(axes[2:])) if stage)


def per_device(
    fine_members,
    coarse_members,
    diffusion,
    hyper,
    drift,
    obs_value,
    obs_var,
    obs_row,
    obs_col,
    obs_layer,
    obs_count,
):
    tiles = lax.axis_size("rows")
    groups = lax.axis_size("mem")
    pairs, K, RF, NC = fine_members.shape
    levels, _, RC, NCC = coarse_members.shape
    stages = axis_stages(tiles)
    sizes = (tiles, groups, pairs, levels, K, RF, RC, NC, NCC, stages)
    slots = obs_value.shape[0]
    E = (pairs + levels) * groups
    nb = 4
    per = slots // nb
    RQ, RQC = RF // groups, RC // groups
    chunks = levels // 2 + 2 * pairs
    peers = sum(math.prod(size for _, size in stage) - 1 for stage in stages)
    nv, nvc = NC // LANES, NCC // LANES
    anyspace = pl.BlockSpec(memory_space=pl.ANY)
    hbm = pl.BlockSpec(memory_space=pltpu.HBM)
    vmem = pl.BlockSpec(memory_space=pltpu.VMEM)
    dma = pltpu.SemaphoreType.DMA

    def flat(obs):
        return obs.reshape(slots // LANES, LANES)

    def keep(array):
        return pltpu.with_memory_space_constraint(array, pltpu.HBM)

    pair_rows, mean_rows = pl.pallas_call(
        functools.partial(cycle_kernel, sizes),
        out_shape=(
            jax.ShapeDtypeStruct((pairs, RF, K, NC), F32),
            jax.ShapeDtypeStruct((RF, K, NC), F32),
        ),
        in_specs=[hbm] * 11,
        out_specs=(anyspace, anyspace),
        scratch_shapes=[
            pltpu.SMEM((K,), F32),
            pltpu.SMEM((K,), F32),
            pltpu.SMEM((K,), F32),
            pltpu.SMEM((1,), jnp.int32),
            pltpu.VMEM((slots // LANES, LANES), F32),
            pltpu.VMEM((slots // LANES, LANES), F32),
            pltpu.VMEM((slots // LANES, LANES), jnp.int32),
            pltpu.VMEM((slots // LANES, LANES), jnp.int32),
            pltpu.VMEM((slots // LANES, LANES), jnp.int32),
            pltpu.VMEM((nv, pairs * K * RF, LANES), F32),
            pltpu.VMEM((nvc, levels * K * RC, LANES), F32),
            pltpu.VMEM((pairs, RF + 2 * HALO, K, NC), F32),
            pltpu.VMEM((pairs, RC + 2 * HALO, K, NCC), F32),
            pltpu.VMEM((levels // 2, RC + 2 * HALO, K, NC), F32),
            pltpu.VMEM((RF + 8, K, NC), F32),
            pltpu.VMEM((RF + 4, K, NC), F32),
            pltpu.VMEM((RC + 8, K, NCC), F32),
            pltpu.VMEM((RC + 4, K, NCC), F32),
            pltpu.VMEM((pairs, RC, K, NCC), F32),
            pltpu.VMEM((levels // 2, RC, K, NC), F32),
            pltpu.VMEM((pairs, RF, K, NC), F32),
            pltpu.VMEM((pairs, RF * K, NC), BF16),
            pltpu.VMEM((pairs, RF * K, NC), BF16),
            pltpu.VMEM((levels // 2, RC * K, NC), BF16),
            pltpu.VMEM((levels // 2, RC * K, NC), BF16),
            pltpu.VMEM((groups, pairs, RQ, K, NC), F32),
            pltpu.VMEM((groups, levels // 2, RQC, K, NC), F32),
            pltpu.VMEM((nb, NC, per), BF16),
            pltpu.VMEM((nb, RF * K, per), F32),
            pltpu.VMEM((nb, 2, NC, per), BF16),
            pltpu.VMEM((nb, RC * K, per), F32),
            pltpu.VMEM((nb + nb // 2, levels, per), F32),
            pltpu.VMEM((groups, nb + nb // 2, levels, per), F32),
            pltpu.VMEM((len(stages), E // 2, LANES), F32),
            pltpu.VMEM((peers, E // 2, LANES), F32),
            pltpu.VMEM((2 * (pairs * groups + 2) * K, E * K), BF16),
            pltpu.VMEM((2 * (pairs * groups + 2) * K, NC), F32),
            pltpu.VMEM((RQ, pairs * groups * K, NC), F32),
            pltpu.VMEM((RQ, E * K, NC), BF16),
            pltpu.VMEM((RQ, E * K, NC), BF16),
            pltpu.VMEM((RQ, K, NC), F32),
            pltpu.VMEM((pairs * groups, RQ, K, NC), F32),
            pltpu.VMEM((RQ, K, NC), F32),
            dma((nv + nvc,)),
            dma((9,)),
            dma((chunks, 2)),
            dma((chunks, 2)),
            dma((2, groups - 1)),
            dma((2, groups - 1)),
            dma((peers,)),
            dma((peers,)),
            dma((levels // 2 + pairs, groups - 1)),
            dma((levels // 2 + pairs, groups - 1)),
            dma((2, RQ, groups - 1)),
            dma((2, RQ, groups - 1)),
            dma((4,)),
        ],
        compiler_params=pltpu.CompilerParams(
            collective_id=0, has_side_effects=True, vmem_limit_bytes=48 * 1024 * 1024
        ),
        name="cycle",
    )(
        keep(fine_members.reshape(pairs * K * RF, NC)),
        keep(coarse_members.reshape(levels * K * RC, NCC)),
        keep(diffusion),
        keep(hyper),
        keep(drift),
        keep(flat(obs_value)),
        keep(flat(obs_var)),
        keep(flat(obs_row)),
        keep(flat(obs_col)),
        keep(flat(obs_layer)),
        obs_count,
    )
    pair, mean = pl.pallas_call(
        functools.partial(order_kernel, K, RF),
        out_shape=(
            jax.ShapeDtypeStruct((pairs * K * RF, NC), F32),
            jax.ShapeDtypeStruct((K * RF, NC), F32),
        ),
        in_specs=[vmem, vmem],
        out_specs=(anyspace, anyspace),
        scratch_shapes=[
            pltpu.VMEM((nv, pairs * K * RF, LANES), F32),
            pltpu.VMEM((nv, K * RF, LANES), F32),
            dma((pairs + 1, nv)),
        ],
        compiler_params=pltpu.CompilerParams(vmem_limit_bytes=16 * 1024 * 1024),
        name="order",
    )(pair_rows, mean_rows)
    return mean.reshape(K, RF, NC), pair.reshape(pairs, K, RF, NC)


def solution(mesh):
    in_specs = (
        P("mem", None, "rows", None),
        P("mem", None, "rows", None),
        P(),
        P(),
        P(),
        P("rows"),
        P("rows"),
        P("rows"),
        P("rows"),
        P("rows"),
        P("rows"),
    )
    out_specs = (P(None, "rows", None), P("mem", None, "rows", None))
    return jax.shard_map(
        per_device, mesh=mesh, in_specs=in_specs, out_specs=out_specs, check_vma=False
    )
```

```python
import functools
import itertools
import math

import jax
import jax.numpy as jnp
from jax import lax
from jax.experimental import pallas as pl
from jax.experimental.pallas import tpu as pltpu
from jax.sharding import PartitionSpec as P

STEPS = 3
EARLY = 1
HALO = 2 * STEPS
LANES = 128
MESH = pl.DeviceIdType.MESH
HIGHEST = lax.Precision.HIGHEST
F32 = jnp.float32
BF16 = jnp.bfloat16


def iota(shape, axis):
    return lax.broadcasted_iota(jnp.int32, shape, axis)


def halves(value):
    high = value.astype(BF16)
    return high, (value - high.astype(F32)).astype(BF16)


def dot(left, right):
    return jnp.dot(left, right, preferred_element_type=F32)


def select_dot(left, right):
    rows = left.shape[0]
    high = left.astype(BF16)
    rest = left - high.astype(F32)
    mid = rest.astype(BF16)
    low = (rest - mid.astype(F32)).astype(BF16)
    out = dot(jnp.concatenate([high, mid, low], 0), right)
    return out[:rows] + (out[rows : 2 * rows] + out[2 * rows :])


def column_at(place, parts):
    return (place % LANES) * parts + place // LANES


def place_of(column, parts):
    shift = parts.bit_length() - 1
    return (column & (parts - 1)) * LANES + (column >> shift)


def shifted(row, packed):
    width = row.shape[-1]
    first, last = row[:, :LANES], row[:, width - LANES :]
    left = jnp.concatenate([pltpu.roll(last, packed, axis=1), row[:, : width - LANES]], 1)
    right = jnp.concatenate([row[:, LANES:], pltpu.roll(first, LANES - packed, axis=1)], 1)
    return left, right


def halved(row):
    tiles = [row[:, i * LANES : (i + 1) * LANES] for i in range(row.shape[1] // LANES)]
    return jnp.concatenate([a + b for a, b in zip(tiles[::2], tiles[1::2])], 1)


def doubled(row):
    tiles = [row[:, i * LANES : (i + 1) * LANES] for i in range(row.shape[1] // LANES)]
    return jnp.concatenate([tile for tile in tiles for _ in range(2)], 1)


def layer_vector(ref, scale, layers, width):
    at = iota((layers, width), 0)
    out = jnp.zeros((layers, width), F32)
    for k in range(layers):
        out = jnp.where(at == k, ref[k] * scale, out)
    return out


def advance(read, write, count, first_row, grid_rows, own, coef, packed=1):
    lap_c, hyp_c, drift_c, up_c, low_c = coef
    layers = up_c.shape[0]
    beside = (count + 4 - own) // 2

    def inside(j, value):
        if beside <= j < beside + own:
            return value
        at = first_row + j
        return value * jnp.where((at >= 0) & (at < grid_rows), 1.0, 0.0).astype(F32)

    q0, q1, q2, q3 = read(0), read(1), read(2), read(3)
    left, right = shifted(q1, packed)
    f1 = inside(1, q2 + q0 + left + right - 4.0 * q1)
    left, right = shifted(q2, packed)
    f2 = inside(2, q3 + q1 + left + right - 4.0 * q2)
    side = right - left
    for i in range(count):
        q2, q3, q4 = read(i + 2), read(i + 3), read(i + 4)
        left, right = shifted(q3, packed)
        f3 = inside(i + 3, q4 + q2 + left + right - 4.0 * q3)
        fl, fr = shifted(f2, packed)
        out = (
            0.8 * q2
            + up_c * pltpu.roll(q2, layers - 1, axis=0)
            + low_c * pltpu.roll(q2, 1, axis=0)
            + lap_c * f2
            - hyp_c * (f1 + f3 + fl + fr)
            - drift_c * side
        )
        write(i, inside(i + 2, out))
        f1, f2, side = f2, f3, right - left


def cycle_kernel(
    sizes,
    fine_in,
    coarse_in,
    diff_in,
    hyper_in,
    drift_in,
    val_in,
    var_in,
    row_in,
    col_in,
    layer_in,
    count_in,
    pair_out,
    mean_out,
    diff_ref,
    hyper_ref,
    drift_ref,
    count_ref,
    val_ref,
    var_ref,
    row_ref,
    col_ref,
    layer_ref,
    xv,
    zv,
    fq,
    cq,
    zq,
    ft1,
    ft2,
    ct1,
    ct2,
    cres,
    zres,
    g,
    gh,
    gl,
    zh,
    zl,
    ga,
    za,
    oc,
    rm,
    occ,
    rmc,
    sown,
    sx,
    ar0,
    ar1,
    kron_ref,
    inc,
    dg,
    dh,
    dl,
    mu,
    ob,
    mb,
    load_sem,
    small_sem,
    hs_sem,
    hr_sem,
    ss_sem,
    sr_sem,
    as_sem,
    ar_sem,
    ts_sem,
    tr_sem,
    os_sem,
    or_sem,
    own_sem,
):
    tiles, groups, pairs, levels, K, RF, RC, NC, NCC, stages = sizes
    tile = lax.axis_index("rows")
    me = lax.axis_index("mem")
    level_all, pair_all = levels * groups, pairs * groups
    E = level_all + pair_all
    nv, nvc = NC // LANES, NCC // LANES
    lch = levels // 2
    RQ, RQC = RF // groups, RC // groups
    s_f, s_c = math.sqrt(pair_all - 1), math.sqrt(level_all - 1)

    def at(row, mem):
        return (row, mem)

    def mem_peer(i):
        return lax.rem(me + i, groups)

    def stage_peers(stage):
        peers = []
        for offsets in itertools.product(*[range(size) for _, size in stage]):
            if any(offsets):
                peer = tile
                for offset, (stride, size) in zip(offsets, stage):
                    mine = lax.rem(tile // stride, size)
                    peer = peer + (lax.rem(mine + offset, size) - mine) * stride
                peers.append(peer)
        return peers

    up = lax.rem(tile + tiles - 1, tiles)
    down = lax.rem(tile + 1, tiles)

    loads = []
    for v in range(nvc):
        loads.append(pltpu.make_async_copy(coarse_in.at[:, pl.ds(v * LANES, LANES)], zv.at[v], load_sem.at[v]))
    for v in range(nv):
        loads.append(pltpu.make_async_copy(fine_in.at[:, pl.ds(v * LANES, LANES)], xv.at[v], load_sem.at[nvc + v]))
    for load in loads:
        load.start()
    smalls = [
        (diff_in, diff_ref),
        (hyper_in, hyper_ref),
        (drift_in, drift_ref),
        (count_in, count_ref),
        (val_in, val_ref),
        (var_in, var_ref),
        (row_in, row_ref),
        (col_in, col_ref),
        (layer_in, layer_ref),
    ]
    smalls = [pltpu.make_async_copy(a, b, small_sem.at[n]) for n, (a, b) in enumerate(smalls)]
    for small in smalls:
        small.start()

    targets = [(up, me), (down, me)]
    targets += [(tile, mem_peer(i)) for i in range(1, groups)]
    for stage in stages:
        targets += [(peer, me) for peer in stage_peers(stage)]
    barrier = pltpu.get_barrier_semaphore()
    for target in targets:
        pl.semaphore_signal(barrier, inc=1, device_id=at(*target), device_id_type=MESH)

    def columns_in(width):
        shape = (width, width)
        held = column_at(iota(shape, 1), width // LANES)
        return jnp.where(iota(shape, 0) == held, 1.0, 0.0).astype(BF16)

    def halo_copy(ref, lead, src, dst, rows, number, way):
        return pltpu.make_async_remote_copy(
            src_ref=ref.at[lead, pl.ds(src, rows)],
            dst_ref=ref.at[lead, pl.ds(dst, rows)],
            send_sem=hs_sem.at[number, way],
            recv_sem=hr_sem.at[number, way],
            device_id=at(up if way == 0 else down, me),
            device_id_type=MESH,
        )

    def level_halo(ch, way):
        src, dst = ((HALO, HALO + RC), (RC, 0))[way]
        return halo_copy(zq, ch, src, dst, HALO, ch, way)

    def fine_halo(j, way):
        src, dst = ((HALO, HALO + RF), (RF, 0))[way]
        return halo_copy(fq, j, src, dst, HALO, lch + j, way)

    near = HALO // 2

    def pair_halo(j, way):
        src, dst = ((HALO + near, HALO + RC + near), (RC, 0))[way]
        return halo_copy(cq, j, src, dst, HALO - near, lch + pairs + j, way)

    def level_column(p):
        return (p % LANES) // 2 * nv + p // LANES

    p = iota((2 * NCC, NC), 1)
    order_c = jnp.where(iota((2 * NCC, NC), 0) == p % 2 * NCC + level_column(p), 1.0, 0.0).astype(BF16)

    def place_level(ch, _):
        rows = []
        for r in range(RC):
            row = []
            for m in range(2):
                row += [zv[v, pl.ds((2 * ch + m) * K * RC + r, K, stride=RC), :] for v in range(nvc)]
            rows.append(jnp.concatenate(row, 1))
        zq[ch, HALO : HALO + RC] = select_dot(jnp.concatenate(rows, 0), order_c).reshape(RC, K, NC)
        return 0

    for load in loads[:nvc]:
        load.wait()
    lax.fori_loop(0, lch, place_level, 0)

    pl.semaphore_wait(barrier, len(targets))
    for ch in range(lch):
        for way in range(2):
            level_halo(ch, way).start()

    order_f = columns_in(NC)

    def place_fine(m):
        rows = []
        for r in range(RF):
            first = m * K * RF + r
            rows.append(jnp.concatenate([xv[v, pl.ds(first, K, stride=RF), :] for v in range(nv)], 1))
        fq[m, HALO : HALO + RF] = select_dot(jnp.concatenate(rows, 0), order_f).reshape(RF, K, NC)
        restrict(m, HALO, HALO, RC)

    def send_fine(m):
        for way in range(2):
            fine_halo(m, way).start()
            pair_halo(m, way).start()

    def restrict(m, fine_row, coarse_row, count):
        for r in range(count):
            both = fq[m, fine_row + 2 * r] + fq[m, fine_row + 2 * r + 1]
            cq[m, coarse_row + r] = 0.25 * halved(both)

    def place_and_send(m, _):
        place_fine(m)
        send_fine(m)
        return 0

    for load in loads[nvc:]:
        load.wait()
    lax.fori_loop(0, pairs, place_and_send, 0)

    for small in smalls:
        small.wait()
    nb = 4
    per = val_ref.shape[0] * LANES // nb
    sub = per // LANES

    def row_of(ref, first, number):
        return jnp.concatenate([ref[i : i + 1, :] for i in range(first, first + number)], 1)

    for b in range(nb):
        col = row_of(col_ref, b * sub, sub)
        lay = row_of(layer_ref, b * sub, sub)
        loc = row_of(row_ref, b * sub, sub) - tile * RF
        oc[b] = jnp.where(iota((NC, per), 0) == place_of(col, nv), 1.0, 0.0).astype(BF16)
        place = ((col >> 1) & (nv - 1)) * LANES + (col >> 1) // nv * 2
        for m in range(2):
            occ[b, m] = jnp.where(iota((NC, per), 0) == place + m, 1.0, 0.0).astype(BF16)
        rm[b] = jnp.where(iota((RF * K, per), 0) == loc * K + lay, 1.0, 0.0).astype(F32)
        rmc[b] = jnp.where(iota((RC * K, per), 0) == (loc >> 1) * K + lay, 1.0, 0.0).astype(F32)

    def coefs(scale_a, scale_h, scale_u, width):
        a = layer_vector(diff_ref, scale_a, K, width)
        h = layer_vector(hyper_ref, scale_h, K, width)
        u = layer_vector(drift_ref, scale_u, K, width)
        k = iota((K, width), 0)
        up_c = jnp.where(k < K - 1, 0.1, 0.0).astype(F32)
        low_c = jnp.where(k > 0, 0.1, 0.0).astype(F32)
        return a + 4.0 * h, h, 0.5 * u, up_c, low_c

    def zero_edges(clear_low, clear_high):
        @pl.when(tile == 0)
        def _():
            clear_low()

        @pl.when(tile == tiles - 1)
        def _():
            clear_high()

    coarse_coef = coefs(0.25, 0.0625, 0.5, NCC)
    level_coef = coefs(0.25, 0.0625, 0.5, NC)
    row_c = tile * RC - HALO
    grid_c = tiles * RC

    def reader(ref, lead):
        return lambda j: ref[lead + (j,)]

    def writer(ref, lead):
        def write(i, value):
            ref[lead + (i,)] = value
        return write

    def coarse_steps(j):
        advance(reader(cq, (j,)), writer(ct1, ()), RC + 8, row_c, grid_c, RC, coarse_coef)
        advance(reader(ct1, ()), writer(ct2, ()), RC + 4, row_c + 2, grid_c, RC, coarse_coef)
        advance(reader(ct2, ()), writer(cres, (j,)), RC, row_c + 4, grid_c, RC, coarse_coef)

    def level_steps(ch):
        advance(reader(zq, (ch,)), writer(ft1, ()), RC + 8, row_c, grid_c, RC, level_coef, 2)
        advance(reader(ft1, ()), writer(ft2, ()), RC + 4, row_c + 2, grid_c, RC, level_coef, 2)
        advance(reader(ft2, ()), writer(zres, (ch,)), RC, row_c + 4, grid_c, RC, level_coef, 2)
        zh[ch], zl[ch] = halves(zres[ch].reshape(RC * K, NC))

    def level_send(ch, i):
        peer = mem_peer(i)
        return pltpu.make_async_remote_copy(
            src_ref=zres.at[ch, pl.ds(peer * RQC, RQC)],
            dst_ref=za.at[me, ch],
            send_sem=ts_sem.at[ch, i - 1],
            recv_sem=tr_sem.at[ch, i - 1],
            device_id=at(tile, peer),
            device_id_type=MESH,
        )

    def pair_send(j, i):
        peer = mem_peer(i)
        return pltpu.make_async_remote_copy(
            src_ref=g.at[j, pl.ds(peer * RQ, RQ)],
            dst_ref=ga.at[me, j],
            send_sem=ts_sem.at[lch + j, i - 1],
            recv_sem=tr_sem.at[lch + j, i - 1],
            device_id=at(tile, peer),
            device_id_type=MESH,
        )

    def level_chunk(ch, _):
        level_halo(ch, 0).wait_recv()
        level_halo(ch, 1).wait_recv()

        def clear(first):
            zq[ch, first : first + HALO] = jnp.zeros((HALO, K, NC), F32)

        zero_edges(lambda: clear(0), lambda: clear(HALO + RC))
        level_steps(ch)
        for i in range(1, groups):
            level_send(ch, i).start()
        return 0

    def gather(high, low, columns, rows):
        number = high.shape[0]
        flat = (number * high.shape[1], high.shape[2])
        got = dot(high[...].reshape(flat), columns) + dot(low[...].reshape(flat), columns)
        return jnp.sum(got.reshape((number,) + rows.shape) * rows[None], axis=1)

    def level_gather(b, _):
        sown[b] = jnp.concatenate([gather(zh, zl, occ[b, m], rmc[b]) for m in range(2)], 0)
        return 0

    def pair_gather(half, _):
        sown[nb + half] = jnp.concatenate([gather(gh, gl, oc[2 * half + b], rm[2 * half + b]) for b in range(2)], 0)
        return 0

    def obs_send(part, i):
        span = (pl.ds(nb, nb // 2), pl.ds(0, nb))[part]
        return pltpu.make_async_remote_copy(
            src_ref=sown.at[span],
            dst_ref=sx.at[me, span],
            send_sem=ss_sem.at[part, i - 1],
            recv_sem=sr_sem.at[part, i - 1],
            device_id=at(tile, mem_peer(i)),
            device_id_type=MESH,
        )

    lax.fori_loop(0, lch, level_chunk, 0)
    lax.fori_loop(0, nb, level_gather, 0)
    for i in range(1, groups):
        obs_send(1, i).start()

    fine_coef = coefs(1.0, 1.0, 1.0, NC)
    row_f = tile * RF - HALO
    grid_f = tiles * RF

    def fine_member(j, _):
        for way in range(2):
            fine_halo(j, way).wait_recv()
            pair_halo(j, way).wait_recv()

        def clear(first, first_c):
            fq[j, first : first + HALO] = jnp.zeros((HALO, K, NC), F32)
            cq[j, first_c : first_c + HALO] = jnp.zeros((HALO, K, NCC), F32)

        restrict(j, 0, near, near)
        restrict(j, HALO + RF, HALO + RC, near)
        zero_edges(lambda: clear(0, 0), lambda: clear(HALO + RF, HALO + RC))
        coarse_steps(j)

        def put_g(i, value):
            g[j, i] = value - doubled(cres[j, i // 2])

        advance(reader(fq, (j,)), writer(ft1, ()), RF + 8, row_f, grid_f, RF, fine_coef)
        advance(reader(ft1, ()), writer(ft2, ()), RF + 4, row_f + 2, grid_f, RF, fine_coef)
        advance(reader(ft2, ()), put_g, RF, row_f + 4, grid_f, RF, fine_coef)
        gh[j], gl[j] = halves(g[j].reshape(RF * K, NC))

        @pl.when(j < EARLY)
        def _():
            for i in range(1, groups):
                pair_send(j, i).start()

        return 0

    lax.fori_loop(0, pairs, fine_member, 0)

    lax.fori_loop(0, nb // 2, pair_gather, 0)
    for i in range(1, groups):
        obs_send(0, i).start()
    sx[me] = sown[...]
    for j in range(EARLY, pairs):
        for i in range(1, groups):
            pair_send(j, i).start()
    for i in range(1, groups):
        obs_send(1, i).wait_recv()
    level_parts = []
    for b in range(nb):
        z = jnp.concatenate([sx[x, b, m * lch : (m + 1) * lch] for m in range(2) for x in range(groups)], 0)
        z_mean = jnp.mean(z, axis=0, keepdims=True)
        slot = iota((1, per), 1) + b * per
        weight = jnp.where(slot < count_ref[0], 1.0 / row_of(var_ref, b * sub, sub), 0.0)
        level_parts.append(((z - z_mean) * (1.0 / s_c), row_of(val_ref, b * sub, sub) - z_mean, weight))
    for i in range(1, groups):
        obs_send(0, i).wait_recv()
    own_level = pltpu.make_async_copy(zres.at[:, pl.ds(me * RQC, RQC)], za.at[me], own_sem.at[0])
    own_pair = pltpu.make_async_copy(g.at[:, pl.ds(me * RQ, RQ)], ga.at[me], own_sem.at[1])
    own_level.start()
    own_pair.start()

    gram = jnp.zeros((E, E + 8), F32)
    for b in range(nb):
        z, rest, weight = level_parts[b]
        first = (b % 2) * pairs
        f = jnp.concatenate([sx[x, nb + b // 2, first : first + pairs] for x in range(groups)], 0)
        f_mean = jnp.mean(f, axis=0, keepdims=True)
        s = jnp.concatenate([z, (f - f_mean) * (1.0 / s_f)], 0)
        innov = rest - f_mean
        extra = jnp.where(iota((8, per), 0) == 0, weight * innov, 0.0)
        right = jnp.concatenate([s * weight, extra], 0)
        gram = gram + lax.dot_general(
            s, right, (((1,), (1,)), ((), ())), precision=HIGHEST, preferred_element_type=F32
        )
    half_e, half_l = E // 2, LANES // 2
    gram = jnp.concatenate([gram, jnp.zeros((E, LANES - E - 8), F32)], 1)
    gram = gram[:half_e] + pltpu.roll(gram[half_e:], half_l, axis=1)

    zk = level_all * K

    def level_anomalies():
        own_level.wait()
        for ch in range(lch):
            for i in range(1, groups):
                level_send(ch, i).wait_recv()

        p = iota((NC, NC), 0)
        hit = level_column(p) == iota((NC, NC), 1) // 2
        widen = [jnp.where(hit & (p % 2 == m), 1.0, 0.0).astype(BF16) for m in range(2)]
        even = iota((K, LANES), 1) % 2 == 0

        def with_other(tile):
            other = jnp.where(even, pltpu.roll(tile, LANES - 1, axis=1), pltpu.roll(tile, 1, axis=1))
            return tile + other

        def one(rc, _):
            z = za[:, :, rc].reshape(level_all // 2, K, NC)
            total = jnp.sum(z, axis=0)
            total = jnp.concatenate([with_other(total[:, v * LANES : (v + 1) * LANES]) for v in range(nv)], 1)
            z_mean = total * (1.0 / level_all)
            high, low = halves(((z - z_mean[None]) * (1.0 / s_c)).reshape(zk // 2, NC))
            wide_mean = select_dot(z_mean, widen[0])
            for m in range(2):
                wide_high, wide_low = dot(high, widen[m]).astype(BF16), dot(low, widen[m]).astype(BF16)
                for half in range(2):
                    dh[2 * rc + half, m * zk // 2 : (m + 1) * zk // 2] = wide_high
                    dl[2 * rc + half, m * zk // 2 : (m + 1) * zk // 2] = wide_low
            for half in range(2):
                mu[2 * rc + half] = wide_mean
            return 0

        lax.fori_loop(0, RQC, one, 0)

    def columns_out(width, repeat):
        shape = (width, width * repeat)
        held = column_at(iota(shape, 0), width // LANES)
        return jnp.where(held == iota(shape, 1) // repeat, 1.0, 0.0).astype(BF16)

    def pair_anomalies():
        own_pair.wait()
        for j in range(pairs):
            for i in range(1, groups):
                pair_send(j, i).wait_recv()
        natural = columns_out(NC, 1)

        def one(r, _):
            f = ga[:, :, r].reshape(pair_all, K, NC)
            f_mean = jnp.mean(f, axis=0)
            mu[r] = mu[r] + select_dot(f_mean, natural)
            anom = ((f - f_mean[None]) * (1.0 / s_f)).reshape(pair_all * K, NC)
            high = anom.astype(BF16)
            rest = anom - high.astype(F32)
            mid = rest.astype(BF16)
            low = (rest - mid.astype(F32)).astype(BF16)
            high, mid, low = dot(high, natural), dot(mid, natural), dot(low, natural)
            dg[r] = high + (mid + low)
            dh[r, zk:] = high.astype(BF16)
            dl[r, zk:] = mid.astype(BF16)
            return 0

        lax.fori_loop(0, RQ, one, 0)

    slot0 = 0
    row_sends = []
    for s, stage in enumerate(stages):
        ar0[s] = gram
        sends = []
        for n, peer in enumerate(stage_peers(stage), slot0):
            send = pltpu.make_async_remote_copy(
                src_ref=ar0.at[s],
                dst_ref=ar1.at[n],
                send_sem=as_sem.at[n],
                recv_sem=ar_sem.at[n],
                device_id=at(peer, me),
                device_id_type=MESH,
            )
            send.start()
            sends.append((send, n))
        if s == 0:
            level_anomalies()
        if s == len(stages) - 1:
            pair_anomalies()
        for send, n in sends:
            send.wait_recv()
            gram = gram + ar1[n]
        row_sends += [send for send, _ in sends]
        slot0 += len(sends)

    rows_t = E + pair_all + 8
    lane = iota((rows_t, LANES), 1)
    eye = jnp.where(iota((E, LANES), 0) == iota((E, LANES), 1), 1.0, 0.0).astype(F32)
    full = jnp.concatenate([gram, pltpu.roll(gram, half_l, axis=1)], 0)
    rhs = jnp.sum(full[:, E : E + 1] * eye, axis=0, keepdims=True)
    full = jnp.where(iota((E, LANES), 1) < E, full, 0.0)
    rhs = jnp.where(iota((8, LANES), 0) == 0, rhs, 0.0)
    table = jnp.concatenate([full + eye, full[level_all:E], rhs], 0)
    width = 4
    for k in range(0, E, width):
        block = range(width)
        columns = [jnp.broadcast_to(table[:, k + i : k + i + 1], (rows_t, LANES)) for i in block]
        heads = [table[k + i : k + i + 1, :] for i in block]
        inv = [[columns[j][k + i : k + i + 1, :] for j in block] for i in block]
        for p in block:
            pivot = 1.0 / inv[p][p]
            scaled = [pivot if j == p else inv[p][j] * pivot for j in block]
            inv = [
                scaled
                if i == p
                else [
                    -inv[i][p] * pivot if j == p else inv[i][j] - inv[i][p] * scaled[j] for j in block
                ]
                for i in block
            ]
        ends = []
        for i in block:
            end = columns[0] * inv[0][i]
            for j in range(1, width):
                end = end + columns[j] * inv[j][i]
            ends.append(end)
        change = ends[0] * heads[0]
        for i in range(1, width):
            change = change + ends[i] * heads[i]
        table = table - change
        for i in block:
            table = jnp.where(lane == k + i, ends[i], table)
    solved = jnp.concatenate([-0.5 * table[E : E + pair_all], table[E + pair_all :]], 0)

    spread = jnp.where(iota((LANES, E * K), 1) // K == iota((LANES, E * K), 0), 1.0, 0.0).astype(BF16)
    same = jnp.where(lax.rem(iota((K, E * K), 1), K) == iota((K, E * K), 0), 1.0, 0.0).astype(F32)
    coef_h, coef_l = halves(solved)

    def kron(part):
        wide = dot(part, spread)
        blocks = [wide[m : m + 1, :] * same for m in range(pair_all + 2)]
        return jnp.concatenate(blocks, 0).astype(BF16)

    kron_rows = kron_ref.shape[0] // 2
    kron_ref[0:kron_rows] = kron(coef_h)
    kron_ref[kron_rows:] = kron(coef_l)

    def result_send(r, i):
        peer = mem_peer(i)
        pair_copy = pltpu.make_async_remote_copy(
            src_ref=ob.at[pl.ds(peer * pairs, pairs), r],
            dst_ref=pair_out.at[:, me * RQ + r],
            send_sem=os_sem.at[0, r, i - 1],
            recv_sem=or_sem.at[0, r, i - 1],
            device_id=at(tile, peer),
            device_id_type=MESH,
        )
        mean_copy = pltpu.make_async_remote_copy(
            src_ref=mb.at[r],
            dst_ref=mean_out.at[me * RQ + r],
            send_sem=os_sem.at[1, r, i - 1],
            recv_sem=or_sem.at[1, r, i - 1],
            device_id=at(tile, peer),
            device_id_type=MESH,
        )
        return pair_copy, mean_copy

    np8 = pair_all * K

    def update(r, _):
        inc[...] = dot(kron_ref[...], dh[r])
        more = dot(kron_ref[0:kron_rows], dl[r])
        total = inc[0:kron_rows] + inc[kron_rows:] + more
        ob[:, r] = (s_f * (dg[r] + total[:np8])).reshape(pair_all, K, NC)
        mb[r] = mu[r] + total[np8 : np8 + K]
        for i in sorted(range(1, groups), key=lambda i: -min(i, groups - i)):
            for copy in result_send(r, i):
                copy.start()
        return 0

    lax.fori_loop(0, RQ, update, 0)
    own_out = pltpu.make_async_copy(ob.at[pl.ds(me * pairs, pairs)], pair_out.at[:, pl.ds(me * RQ, RQ)], own_sem.at[2])
    own_mean = pltpu.make_async_copy(mb, mean_out.at[pl.ds(me * RQ, RQ)], own_sem.at[3])
    own_out.start()
    own_mean.start()

    for send in row_sends:
        send.wait_send()
    for way in range(2):
        for ch in range(lch):
            level_halo(ch, way).wait_send()
        for j in range(pairs):
            fine_halo(j, way).wait_send()
            pair_halo(j, way).wait_send()
    for i in range(1, groups):
        for ch in range(lch):
            level_send(ch, i).wait_send()
        for j in range(pairs):
            pair_send(j, i).wait_send()
        for part in range(2):
            obs_send(part, i).wait_send()
    own_out.wait()
    own_mean.wait()
    for r in range(RQ):
        for i in range(1, groups):
            for copy in result_send(r, i):
                copy.wait_recv()
                copy.wait_send()


def order_kernel(K, RF, pair_in, mean_in, pair_out, mean_out, pv, mv, sem):
    nv = pv.shape[0]
    pairs = pair_in.shape[0]

    def put(value, ref, first, r):
        for v in range(nv):
            ref[v, pl.ds(first + r, K, stride=RF), :] = value[:, v * LANES : (v + 1) * LANES]

    copies = []

    def send(ref, first, out, row):
        for v in range(nv):
            copy = pltpu.make_async_copy(
                ref.at[v, pl.ds(first, K * RF)],
                out.at[pl.ds(first, K * RF), pl.ds(v * LANES, LANES)],
                sem.at[row, v],
            )
            copy.start()
            copies.append(copy)

    for m in range(pairs):
        for r in range(RF):
            put(pair_in[m, r], pv, m * K * RF, r)
        send(pv, m * K * RF, pair_out, m)
    for r in range(RF):
        put(mean_in[r], mv, 0, r)
    send(mv, 0, mean_out, pairs)
    for copy in copies:
        copy.wait()


def axis_stages(tiles):
    axes, stride = [], 1
    for size in (2, 4, 4):
        if stride < tiles:
            axes.append((stride, size))
            stride *= size
    return tuple(stage for stage in (tuple(axes[:2]), tuple(axes[2:])) if stage)


def per_device(
    fine_members,
    coarse_members,
    diffusion,
    hyper,
    drift,
    obs_value,
    obs_var,
    obs_row,
    obs_col,
    obs_layer,
    obs_count,
):
    tiles = lax.axis_size("rows")
    groups = lax.axis_size("mem")
    pairs, K, RF, NC = fine_members.shape
    levels, _, RC, NCC = coarse_members.shape
    stages = axis_stages(tiles)
    sizes = (tiles, groups, pairs, levels, K, RF, RC, NC, NCC, stages)
    slots = obs_value.shape[0]
    E = (pairs + levels) * groups
    nb = 4
    per = slots // nb
    RQ, RQC = RF // groups, RC // groups
    chunks = levels // 2 + 2 * pairs
    peers = sum(math.prod(size for _, size in stage) - 1 for stage in stages)
    nv, nvc = NC // LANES, NCC // LANES
    anyspace = pl.BlockSpec(memory_space=pl.ANY)
    hbm = pl.BlockSpec(memory_space=pltpu.HBM)
    vmem = pl.BlockSpec(memory_space=pltpu.VMEM)
    dma = pltpu.SemaphoreType.DMA

    def flat(obs):
        return obs.reshape(slots // LANES, LANES)

    def keep(array):
        return pltpu.with_memory_space_constraint(array, pltpu.HBM)

    pair_rows, mean_rows = pl.pallas_call(
        functools.partial(cycle_kernel, sizes),
        out_shape=(
            jax.ShapeDtypeStruct((pairs, RF, K, NC), F32),
            jax.ShapeDtypeStruct((RF, K, NC), F32),
        ),
        in_specs=[hbm] * 11,
        out_specs=(anyspace, anyspace),
        scratch_shapes=[
            pltpu.SMEM((K,), F32),
            pltpu.SMEM((K,), F32),
            pltpu.SMEM((K,), F32),
            pltpu.SMEM((1,), jnp.int32),
            pltpu.VMEM((slots // LANES, LANES), F32),
            pltpu.VMEM((slots // LANES, LANES), F32),
            pltpu.VMEM((slots // LANES, LANES), jnp.int32),
            pltpu.VMEM((slots // LANES, LANES), jnp.int32),
            pltpu.VMEM((slots // LANES, LANES), jnp.int32),
            pltpu.VMEM((nv, pairs * K * RF, LANES), F32),
            pltpu.VMEM((nvc, levels * K * RC, LANES), F32),
            pltpu.VMEM((pairs, RF + 2 * HALO, K, NC), F32),
            pltpu.VMEM((pairs, RC + 2 * HALO, K, NCC), F32),
            pltpu.VMEM((levels // 2, RC + 2 * HALO, K, NC), F32),
            pltpu.VMEM((RF + 8, K, NC), F32),
            pltpu.VMEM((RF + 4, K, NC), F32),
            pltpu.VMEM((RC + 8, K, NCC), F32),
            pltpu.VMEM((RC + 4, K, NCC), F32),
            pltpu.VMEM((pairs, RC, K, NCC), F32),
            pltpu.VMEM((levels // 2, RC, K, NC), F32),
            pltpu.VMEM((pairs, RF, K, NC), F32),
            pltpu.VMEM((pairs, RF * K, NC), BF16),
            pltpu.VMEM((pairs, RF * K, NC), BF16),
            pltpu.VMEM((levels // 2, RC * K, NC), BF16),
            pltpu.VMEM((levels // 2, RC * K, NC), BF16),
            pltpu.VMEM((groups, pairs, RQ, K, NC), F32),
            pltpu.VMEM((groups, levels // 2, RQC, K, NC), F32),
            pltpu.VMEM((nb, NC, per), BF16),
            pltpu.VMEM((nb, RF * K, per), F32),
            pltpu.VMEM((nb, 2, NC, per), BF16),
            pltpu.VMEM((nb, RC * K, per), F32),
            pltpu.VMEM((nb + nb // 2, levels, per), F32),
            pltpu.VMEM((groups, nb + nb // 2, levels, per), F32),
            pltpu.VMEM((len(stages), E // 2, LANES), F32),
            pltpu.VMEM((peers, E // 2, LANES), F32),
            pltpu.VMEM((2 * (pairs * groups + 2) * K, E * K), BF16),
            pltpu.VMEM((2 * (pairs * groups + 2) * K, NC), F32),
            pltpu.VMEM((RQ, pairs * groups * K, NC), F32),
            pltpu.VMEM((RQ, E * K, NC), BF16),
            pltpu.VMEM((RQ, E * K, NC), BF16),
            pltpu.VMEM((RQ, K, NC), F32),
            pltpu.VMEM((pairs * groups, RQ, K, NC), F32),
            pltpu.VMEM((RQ, K, NC), F32),
            dma((nv + nvc,)),
            dma((9,)),
            dma((chunks, 2)),
            dma((chunks, 2)),
            dma((2, groups - 1)),
            dma((2, groups - 1)),
            dma((peers,)),
            dma((peers,)),
            dma((levels // 2 + pairs, groups - 1)),
            dma((levels // 2 + pairs, groups - 1)),
            dma((2, RQ, groups - 1)),
            dma((2, RQ, groups - 1)),
            dma((4,)),
        ],
        compiler_params=pltpu.CompilerParams(
            collective_id=0, has_side_effects=True, vmem_limit_bytes=48 * 1024 * 1024
        ),
        name="cycle",
    )(
        keep(fine_members.reshape(pairs * K * RF, NC)),
        keep(coarse_members.reshape(levels * K * RC, NCC)),
        keep(diffusion),
        keep(hyper),
        keep(drift),
        keep(flat(obs_value)),
        keep(flat(obs_var)),
        keep(flat(obs_row)),
        keep(flat(obs_col)),
        keep(flat(obs_layer)),
        obs_count,
    )
    pair, mean = pl.pallas_call(
        functools.partial(order_kernel, K, RF),
        out_shape=(
            jax.ShapeDtypeStruct((pairs * K * RF, NC), F32),
            jax.ShapeDtypeStruct((K * RF, NC), F32),
        ),
        in_specs=[vmem, vmem],
        out_specs=(anyspace, anyspace),
        scratch_shapes=[
            pltpu.VMEM((nv, pairs * K * RF, LANES), F32),
            pltpu.VMEM((nv, K * RF, LANES), F32),
            dma((pairs + 1, nv)),
        ],
        compiler_params=pltpu.CompilerParams(vmem_limit_bytes=16 * 1024 * 1024),
        name="order",
    )(pair_rows, mean_rows)
    return mean.reshape(K, RF, NC), pair.reshape(pairs, K, RF, NC)


def solution(mesh):
    in_specs = (
        P("mem", None, "rows", None),
        P("mem", None, "rows", None),
        P(),
        P(),
        P(),
        P("rows"),
        P("rows"),
        P("rows"),
        P("rows"),
        P("rows"),
        P("rows"),
    )
    out_specs = (P(None, "rows", None), P("mem", None, "rows", None))
    return jax.shard_map(
        per_device, mesh=mesh, in_specs=in_specs, out_specs=out_specs, check_vma=False
    )
```
